256 devices in a mesh: dp: 16 (over z, core), mp: 16 (over x, y).
Axes of the slice: x: 4, y: 4, z: 8, core: 2. Of those that a mesh axis runs over, the one named last changes fastest.
Arguments:
- item_tokens: bfloat16 [32768, 2048], P('dp', 'mp'), may hold values from -60 to 60
- gate_weight: bfloat16 [2048, 5632], P(None, 'mp'), may hold values from -0.125 to 0.125
- up_weight: bfloat16 [2048, 5632], P(None, 'mp'), may hold values from -0.125 to 0.125
- down_weight: bfloat16 [5632, 2048], P('mp'), may hold values from -0.078125 to 0.078125
- user_gain: float32 [2048], P('mp'), may hold values from 0.1 to 1.9
- query_weight: bfloat16 [2048, 2048], P(None, 'mp'), may hold values from -0.125 to 0.125
- key_weight: bfloat16 [2048, 256], replicated, may hold values from -0.125 to 0.125
- value_weight: bfloat16 [2048, 256], replicated, may hold values from -0.125 to 0.125
- out_weight: bfloat16 [2048, 2048], P('mp'), may hold values from -0.125 to 0.125
- item_slot: int32 [1024], P('dp'), may hold values from -1 to 4095, as said below
- lengths: int32 [16], P('dp'), may hold values from 16 to 256, as said below
- targets: int32 [4096], P('dp'), may hold values from -1 to 1023, as said below
Outputs:
- item_embeddings: bfloat16 [1024, 2048], P('dp', 'mp')
- user_states: bfloat16 [4096, 2048], P('dp', 'mp')
- losses: float32 [4096], P('dp')
The draws below stay inside these ranges and needn't reach their ends.
Inputs may be any that keep to these rules, and one draw needn't show every extreme that they name: Slot item_slot[i] = h * 256 + p puts item i at position p of history h, or -1 if no history holds it. Slots are distinct and fill positions 0 to lengths[h] - 1 of every history. At most 64 items of one index of dp go to one history, and some history receives exactly 64 items from one index of dp. `lengths`: one history has exactly 256 items; the others have 16 to 32. targets[h * 256 + p] is the item at position p + 1 of history h, and -1 at the history's last position and past its end.
All inputs are finite; a program needn't handle non-finite values.
Results may differ from the reference program's by a relative error of at most 0.009.
Values may be sent and summed in bfloat16 or wider, within the bound.
A program may use at most 128 MiB of HBM per device.

```python
import jax
import jax.numpy as jnp
from jax import lax

D = 2048
FF = 5632
HEADS = 32
KV_HEADS = 4
HEAD_DIM = 64
ITEM_TOK = 32
ITEM_DEV = 64
POS_DEV = 256
MINLEN = 16
ITEMS = 1024
HISTORIES = 16
N_DP = 16


def layout(key):
    subkeys = jax.random.split(key, 4)
    long_owner = jax.random.randint(subkeys[0], (), 0, HISTORIES)
    start_source = jax.random.randint(subkeys[1], (), 0, N_DP)
    extra_len = jax.random.randint(subkeys[2], (HISTORIES,), 0, MINLEN + 1)
    devices = jnp.arange(HISTORIES, dtype=jnp.int32)
    is_long = devices == long_owner
    lengths = jnp.where(is_long, POS_DEV, MINLEN + extra_len).astype(jnp.int32)
    other_len = jnp.where(is_long, 0, lengths)
    offsets = jnp.cumsum(other_len) - other_len
    rest_count = ITEMS - POS_DEV
    shuffled = jax.random.permutation(subkeys[3], rest_count).astype(jnp.int32)
    slot_ids = jnp.arange(HISTORIES * POS_DEV, dtype=jnp.int32)
    slot_dev = slot_ids // POS_DEV
    slot_pos = slot_ids % POS_DEV
    run_start = start_source * ITEM_DEV
    long_item = (run_start + slot_pos) % ITEMS
    rest_index = jnp.clip(offsets[slot_dev] + slot_pos, 0, rest_count - 1)
    other_item = (run_start + POS_DEV + shuffled[rest_index]) % ITEMS
    in_history = slot_pos < lengths[slot_dev]
    slot_item = jnp.where(slot_dev == long_owner, long_item, jnp.where(in_history, other_item, -1)).astype(jnp.int32)
    return (lengths, slot_item)


def draw_item_slot(key, part):
    lengths, slot_item = layout(key)
    total_slots = HISTORIES * POS_DEV
    where_to = jnp.where(slot_item >= 0, slot_item, ITEMS)
    return jnp.full((ITEMS,), -1, jnp.int32).at[where_to].set(jnp.arange(total_slots, dtype=jnp.int32), mode='drop')


def draw_lengths(key, part):
    lengths, slot_item = layout(key)
    return lengths


def draw_targets(key, part):
    lengths, slot_item = layout(key)
    following = jnp.concatenate([slot_item[1:], jnp.full((1,), -1, jnp.int32)])
    slot_pos = jnp.arange(HISTORIES * POS_DEV, dtype=jnp.int32) % POS_DEV
    inside = (slot_pos + 1 < POS_DEV) & (following >= 0) & (slot_item >= 0)
    return jnp.where(inside, following, -1).astype(jnp.int32)


def draw_item_tokens(key, part):
    key = jax.random.fold_in(key, 7)
    subkeys = jax.random.split(key, 7)
    rough = jax.random.uniform(subkeys[0], (D,), jnp.float32, 0.7, 1.4)
    column = 0.25 * 10.0 ** (jnp.arange(D, dtype=jnp.float32) / D) * rough
    group_count = max(ITEMS // 8, 1)
    shuffled_ids = jax.random.permutation(subkeys[5], ITEMS).astype(jnp.int32)
    member_of = shuffled_ids % group_count
    centre = jax.random.normal(subkeys[6], (group_count, 1, D), jnp.float32)
    individual = jax.random.normal(subkeys[4], (ITEMS, 1, D), jnp.float32)
    shared = centre[member_of] + 0.3 * individual
    noise = jax.random.normal(subkeys[3], (ITEMS, ITEM_TOK, D), jnp.float32)
    values_out = (shared + 0.7 * noise) * column
    return jnp.clip(values_out, -60.0, 60.0).reshape(ITEMS * ITEM_TOK, D).astype(jnp.bfloat16)


def block_scale(stream_key, extent, cuts, smallest, high):
    def one(position, shards_of):
        steps = jax.random.uniform(jax.random.fold_in(jax.random.fold_in(stream_key, 6), position), (shards_of,), jnp.float32, smallest / len(cuts), high / len(cuts))
        return jnp.repeat(jnp.exp(steps), extent[position] // shards_of).reshape((-1,) + (1,) * (len(extent) - position - 1))

    gain = one(*cuts[0])
    for cut in cuts[1:]:
        gain = gain * one(*cut)
    return gain


def normal_values(stream_key, extent, deviation, limit, cuts=(), held_as=jnp.bfloat16):
    result = jax.random.normal(stream_key, extent, jnp.float32) * deviation
    if len(cuts) > 0:
        result = block_scale(stream_key, extent, cuts, -0.22, 0.18) * result
    return jnp.clip(result, min=-limit, max=limit).astype(held_as)


def setup_inputs(seed: int = 0) -> dict:
    arg_keys = jax.random.split(jax.random.key(seed), 13)
    item_tokens = draw_item_tokens(jax.random.fold_in(arg_keys[12], 71), 0)
    gate_weight = normal_values(arg_keys[1], (D, FF), D ** -0.5, 0.125, ((1, 16),))
    up_weight = normal_values(arg_keys[2], (D, FF), D ** -0.5, 0.125, ((1, 16),))
    down_weight = normal_values(arg_keys[3], (FF, D), FF ** -0.5, 0.078125, ((0, 16),))
    user_gain = jnp.clip(1.0 + 0.18 * jax.random.normal(arg_keys[4], (D,), jnp.float32), 0.1, 1.9)
    query_weight = normal_values(arg_keys[5], (D, HEADS * HEAD_DIM), D ** -0.5, 0.125, ((1, 16),))
    key_weight = normal_values(arg_keys[6], (D, KV_HEADS * HEAD_DIM), D ** -0.5, 0.125)
    value_weight = normal_values(arg_keys[7], (D, KV_HEADS * HEAD_DIM), D ** -0.5, 0.125)
    out_weight = normal_values(arg_keys[8], (HEADS * HEAD_DIM, D), (HEADS * HEAD_DIM) ** -0.5, 0.125, ((0, 16),))
    item_slot = draw_item_slot(jax.random.fold_in(arg_keys[12], 71), 0)
    lengths = draw_lengths(jax.random.fold_in(arg_keys[12], 71), 0)
    targets = draw_targets(jax.random.fold_in(arg_keys[12], 71), 0)
    return dict(item_tokens=item_tokens, gate_weight=gate_weight, up_weight=up_weight, down_weight=down_weight, user_gain=user_gain, query_weight=query_weight, key_weight=key_weight, value_weight=value_weight, out_weight=out_weight, item_slot=item_slot, lengths=lengths, targets=targets)


SCALE = 20.0

def rotate(values_in, positions):
    half_dim = values_in.shape[-1] // 2
    exponent = jnp.arange(half_dim, dtype=jnp.float32) * (2.0 / values_in.shape[-1])
    frequency = 10000.0 ** (-exponent)
    angles = positions.astype(jnp.float32)[:, None] * frequency[None, :]
    cosine = jnp.cos(angles)[:, None, :]
    sine_part = jnp.sin(angles)[:, None, :]
    first_half = values_in[..., :half_dim]
    second_half = values_in[..., half_dim:]
    return jnp.concatenate([first_half * cosine - second_half * sine_part, second_half * cosine + first_half * sine_part], axis=-1)

def pooled_items(item_block, gate_weight, up_weight, down_weight):
    gate_acc = jnp.dot(item_block, gate_weight, preferred_element_type=jnp.float32)
    up_part = jnp.dot(item_block, up_weight, preferred_element_type=jnp.float32)
    hidden = (jax.nn.silu(gate_acc) * up_part).astype(jnp.bfloat16)
    mixed_rows = jnp.dot(hidden, down_weight, preferred_element_type=jnp.float32)
    summed = item_block.astype(jnp.float32) + mixed_rows
    return lax.optimization_barrier(jnp.mean(summed.reshape(-1, ITEM_TOK, summed.shape[-1]), axis=1))

def history_layer(states, length, user_gain, query_weight, key_weight, value_weight, out_weight):
    positions = jnp.arange(POS_DEV, dtype=jnp.int32)
    states_wide = states.astype(jnp.float32)
    mean_square = lax.optimization_barrier(jnp.mean(states_wide * states_wide, axis=-1))
    normed = (states_wide * lax.rsqrt(mean_square + 1e-05)[:, None] * user_gain.astype(jnp.float32)).astype(jnp.bfloat16)
    query_all = jnp.dot(normed, query_weight, preferred_element_type=jnp.float32).reshape(POS_DEV, HEADS, HEAD_DIM)
    key_all = jnp.dot(normed, key_weight, preferred_element_type=jnp.float32).reshape(POS_DEV, KV_HEADS, HEAD_DIM)
    value_all = jnp.dot(normed, value_weight, preferred_element_type=jnp.float32).reshape(POS_DEV, KV_HEADS, HEAD_DIM)
    query_all = rotate(query_all, positions).astype(jnp.bfloat16)
    key_all = rotate(key_all, positions).astype(jnp.bfloat16)
    value_all = value_all.astype(jnp.bfloat16)
    group_size = HEADS // KV_HEADS
    key_heads = jnp.repeat(key_all, group_size, axis=1)
    value_heads = jnp.repeat(value_all, group_size, axis=1)
    scores = jnp.einsum('qhe,khe->hqk', query_all.astype(jnp.float32), key_heads.astype(jnp.float32)) * HEAD_DIM ** (-0.5)
    allowed = (positions[None, :] <= positions[:, None]) & (positions[None, :] < length)
    weights = jnp.where(allowed[None, :, :], jnp.exp(scores), 0.0)
    weights = (weights / lax.optimization_barrier(jnp.sum(weights, axis=-1, keepdims=True))).astype(jnp.bfloat16)
    attended = jnp.einsum('hqk,khe->qhe', weights.astype(jnp.float32), value_heads.astype(jnp.float32))
    attended = attended.astype(jnp.bfloat16).reshape(POS_DEV, HEADS * HEAD_DIM)
    attn_rows = jnp.dot(attended, out_weight, preferred_element_type=jnp.float32)
    valid_rows = (positions < length).astype(jnp.float32)
    return (states_wide + attn_rows) * valid_rows[:, None]

def reference(item_tokens, gate_weight, up_weight, down_weight, user_gain, query_weight, key_weight, value_weight, out_weight, item_slot, lengths, targets):
    blocks = item_tokens.reshape(N_DP, ITEM_DEV * ITEM_TOK, D)
    pooled = lax.map(lambda item_block: pooled_items(item_block, gate_weight, up_weight, down_weight), blocks)
    item_embeddings = pooled.reshape(ITEMS, D).astype(jnp.bfloat16)
    total_slots = HISTORIES * POS_DEV
    where_to = jnp.where(item_slot >= 0, item_slot, total_slots).astype(jnp.int32)
    placed = jnp.zeros((total_slots, D), jnp.bfloat16).at[where_to].set(item_embeddings, mode='drop')
    combined = lax.map(lambda user_pair: history_layer(user_pair[0], user_pair[1], user_gain, query_weight, key_weight, value_weight, out_weight), (placed.reshape(HISTORIES, POS_DEV, D), lengths))
    combined = combined.reshape(total_slots, D)
    user_states = combined.astype(jnp.bfloat16)
    item_wide = item_embeddings.astype(jnp.float32)
    item_unit = (item_wide * lax.rsqrt(lax.optimization_barrier(jnp.sum(item_wide * item_wide, axis=-1)) + 1e-06)[:, None]).astype(jnp.bfloat16)
    user_unit = (combined * lax.rsqrt(lax.optimization_barrier(jnp.sum(combined * combined, axis=-1)) + 1e-06)[:, None]).astype(jnp.bfloat16)
    logits = SCALE * jnp.dot(user_unit, item_unit.T, preferred_element_type=jnp.float32)
    totals = lax.optimization_barrier(jnp.sum(jnp.exp(logits), axis=-1))
    columns = jnp.arange(ITEMS, dtype=jnp.int32)
    picked = lax.optimization_barrier(jnp.sum(jnp.where(columns[None, :] == targets[:, None], logits, 0.0), axis=-1))
    losses = jnp.where(targets >= 0, jnp.log(totals) - picked, 0.0)
    return (item_embeddings, user_states, losses)
```

```python
import functools

import jax
import jax.numpy as jnp
import numpy as np
from jax import lax
from jax.experimental import pallas as pl
from jax.experimental.pallas import tpu as pltpu
from jax.sharding import PartitionSpec as P

HEAD_DIM = 64
ITEM_TOK = 32
SCALE = 20.0
SHORT = 32
LANES = 128
RING = 4
CHUNKS = 8
MESH = pl.DeviceIdType.MESH
BF16 = jnp.bfloat16
F32 = jnp.float32
NT = (((1,), (1,)), ((), ()))


def rope_tables(positions):
    half = HEAD_DIM // 2
    exponent = np.arange(half, dtype=np.float32) * np.float32(2.0 / HEAD_DIM)
    frequency = (10000.0 ** (-exponent.astype(np.float64))).astype(np.float32)
    angles = np.arange(positions, dtype=np.float32)[:, None] * frequency[None, :]
    angles = angles.astype(np.float64)
    cosine, sine = np.cos(angles), np.sin(angles)
    cos_table = np.concatenate([cosine, cosine, cosine, cosine], axis=1)
    sin_table = np.concatenate([-sine, sine, -sine, sine], axis=1)
    return cos_table.astype(np.float32), sin_table.astype(np.float32)


def kernel(
    sizes,
    tok, wg, wu, wd, wq, wk, wv, wo, gain, slot, cos_t, sin_t,
    emb_out, us_out, loss_out,
    g_buf, wg_v, wu_v, wd_v, wq_v, wk_v, wv_v, wo_v,
    pooled, tok_mean, s1, r1, items, x_buf, it_buf, iu, kv_long, s5, r5, us_long, u_buf,
    gains, slots, tp, ll,
    w_sem, g_send, g_recv, mp_send, mp_recv, r1_recv, it_sem, dp_send, dp_recv, item_recv, gs_sem,
):
    n_dp, n_mp, rows, ff, item_dev, short, positions = sizes
    n_items = n_dp * item_dev
    long_rows = positions // n_dp
    mine = short + long_rows
    chunk_items = n_items // n_mp
    chunk_rows = rows // CHUNKS
    pool_items = chunk_rows // ITEM_TOK
    halves = 2
    half_items = item_dev // halves
    half_chunks = CHUNKS // halves
    d = lax.axis_index("dp")
    m = lax.axis_index("mp")
    sibling = d + 1 - 2 * lax.rem(d, 2)

    def to_mp(src, dst, send_sem, recv_sem, j):
        return pltpu.make_async_remote_copy(
            src_ref=src, dst_ref=dst, send_sem=send_sem, recv_sem=recv_sem,
            device_id={"mp": j}, device_id_type=MESH,
        )

    def to_dp(src, dst, send_sem, recv_sem, j):
        return pltpu.make_async_remote_copy(
            src_ref=src, dst_ref=dst, send_sem=send_sem, recv_sem=recv_sem,
            device_id={"dp": j}, device_id_type=MESH,
        )

    def wait_for(ref, sem):
        pltpu.make_async_copy(ref, ref, sem).wait()

    barrier = pltpu.get_barrier_semaphore()
    for k in range(1, n_mp):
        pl.semaphore_signal(
            barrier, inc=1, device_id={"mp": lax.rem(m + k, n_mp)}, device_id_type=MESH
        )
    for k in range(1, n_dp):
        pl.semaphore_signal(
            barrier, inc=1, device_id={"dp": lax.rem(d + k, n_dp)}, device_id_type=MESH
        )

    kv_block = pl.ds(pl.multiple_of((m // 8) * LANES, LANES), LANES)
    loads = [
        (tok, g_buf.at[m]), (wg, wg_v), (wu, wu_v), (wd, wd_v), (wq, wq_v),
        (wk.at[:, kv_block], wk_v), (wv.at[:, kv_block], wv_v), (wo, wo_v),
    ]
    copies = [pltpu.make_async_copy(a, b, w_sem.at[i]) for i, (a, b) in enumerate(loads)]
    for copy in copies:
        copy.start()
    gains[m] = gain[...]
    slots[d] = jnp.concatenate(
        [slot[...], jnp.full((1, LANES - item_dev), -1, jnp.int32)], axis=1
    )
    pl.semaphore_wait(barrier, n_mp + n_dp - 2)

    x_at, y_at = m // RING, lax.rem(m, RING)

    def place(c, o1, o2):
        p = lax.rem(c, 2)
        c1 = x_at * (1 - p) + y_at * p
        c2 = y_at * (1 - p) + x_at * p
        return lax.rem(c1 + o1, RING) * (RING - 3 * p) + lax.rem(c2 + o2, RING) * (1 + 3 * p)

    def chunk(c):
        return pl.ds(pl.multiple_of(c * chunk_rows, chunk_rows), chunk_rows)

    def forward(c, block, target, group):
        to_mp(
            g_buf.at[block, chunk(c)], g_buf.at[block, chunk(c)],
            g_send.at[c], g_recv.at[c, group], target,
        ).start()

    def own(c, target, group):
        to_mp(
            tok.at[chunk(c)], g_buf.at[m, chunk(c)], g_send.at[c], g_recv.at[c, group], target
        ).start()

    def arrived(c, group, count):
        wait_for(g_buf.at[pl.ds(0, count), chunk(c)], g_recv.at[c, group])

    def stage_own(c):
        for o in (1, 3):
            own(c, place(c, o, 0), 0)
        for o in (1, 3):
            own(c, place(c, 0, o), 2)

    def stage_first(c):
        arrived(c, 0, 2)
        way = lax.rem(c // 2, 2)
        forward(c, place(c, 3 - 2 * way, 0), place(c, 1 + 2 * way, 0), 1)
        for o1 in (1, 3):
            for o2 in (1, 3):
                forward(c, place(c, o1, 0), place(c, 0, o2), 2)

    def stage_opposite(c):
        arrived(c, 1, 1)
        for o2 in (1, 3):
            forward(c, place(c, 2, 0), place(c, 0, o2), 2)

    def stage_second(c):
        arrived(c, 2, 8)
        for o1 in (0, 2):
            forward(c, place(c, o1, 3), place(c, 0, 1), 3)
        for o1 in (1, 3):
            forward(c, place(c, o1, 1), place(c, 0, 3), 3)

    pool_of = lax.broadcasted_iota(jnp.int32, (pool_items, chunk_rows), 1) // ITEM_TOK
    pool_row = lax.broadcasted_iota(jnp.int32, (pool_items, chunk_rows), 0)
    pool = (pool_of == pool_row).astype(F32).astype(BF16)

    def stage_compute(c):
        arrived(c, 3, 4)
        here = chunk(c)
        wide = jnp.concatenate([g_buf[k, here, :] for k in range(n_mp)], axis=1)
        gate = jnp.dot(wide, wg_v[...], preferred_element_type=F32)
        up = jnp.dot(wide, wu_v[...], preferred_element_type=F32)
        hidden = (gate / (1.0 + jnp.exp(-gate)) * up).astype(BF16)
        out_rows = pl.ds(pl.multiple_of(c * pool_items, pool_items), pool_items)
        pooled[out_rows, :] = jnp.dot(pool, hidden, preferred_element_type=F32)
        tok_mean[out_rows, :] = jnp.dot(pool, g_buf[m, here, :], preferred_element_type=F32)

    def stage_down(h):
        here = pl.ds(pl.multiple_of(h * half_items, half_items), half_items)
        mean = (pooled[here, :] * (1.0 / ITEM_TOK)).astype(BF16)
        part = jnp.dot(mean, wd_v[...], preferred_element_type=F32).astype(BF16)
        for j in range(n_mp):
            s1[j, here, :] = part[:, j * LANES : (j + 1) * LANES]
        r1[m, here, :] = s1[m, here, :]
        for k in range(1, n_mp):
            j = lax.rem(m + k, n_mp)
            to_mp(s1.at[j, here], r1.at[m, here], mp_send.at[0], r1_recv.at[h], j).start()

    def step(i, carry):
        @pl.when(i < CHUNKS)
        def _():
            stage_own(i)

        @pl.when((i >= 1) & (i < CHUNKS + 1))
        def _():
            stage_first(i - 1)

        @pl.when((i >= 2) & (i < CHUNKS + 2))
        def _():
            stage_opposite(i - 2)

        @pl.when((i >= 3) & (i < CHUNKS + 3))
        def _():
            stage_second(i - 3)

        @pl.when(i == 4)
        def _():
            for copy in copies:
                copy.wait()

        @pl.when(i >= 4)
        def _():
            c = i - 4
            stage_compute(c)

            @pl.when(lax.rem(c, half_chunks) == half_chunks - 1)
            def _():
                stage_down(c // half_chunks)

        return carry

    for k in range(1, n_mp):
        j = lax.rem(m + k, n_mp)
        to_mp(gains.at[m], gains.at[m], gs_sem.at[0], gs_sem.at[1], j).start()
    for k in range(1, n_dp):
        j = lax.rem(d + k, n_dp)
        to_dp(slots.at[d], slots.at[d], gs_sem.at[2], gs_sem.at[3], j).start()

    lax.fori_loop(0, CHUNKS + 4, step, 0)

    for i, (ref, count) in enumerate(((gains, n_mp), (gains, n_mp), (slots, n_dp), (slots, n_dp))):
        wait_for(ref.at[pl.ds(0, count - 1)], gs_sem.at[i])

    slot_row = jnp.concatenate([slots[k][:, :item_dev] for k in range(n_dp)], axis=1)
    last = (slot_row >= 0) & (jnp.bitwise_and(slot_row, positions - 1) == positions - 1)
    long_base = jnp.max(
        jnp.where(last, slot_row, positions - 1), axis=1, keepdims=True
    ) - (positions - 1)
    is_long = long_base == d * positions
    row = lax.broadcasted_iota(jnp.int32, (LANES, 1), 0)
    position = jnp.where(row < short, row, row - short + d * long_rows)
    row_slot = jnp.where(row < short, d * positions, long_base) + position
    row_slot = jnp.where(row < mine, row_slot, -2)
    holds = jnp.where(slot_row == row_slot[:mine], 1.0, 0.0).astype(BF16)
    next_slot = jnp.where((position + 1 < positions) & (row < mine), row_slot + 1, -2)
    follows = jnp.where(slot_row == next_slot, 1.0, 0.0).astype(BF16)
    valid = jnp.sum(holds.astype(F32), axis=1, keepdims=True)
    has_target = lax.dot_general(
        jnp.ones((8, n_items), BF16), follows, NT, preferred_element_type=F32
    )
    item_id = lax.broadcasted_iota(jnp.int32, (n_items, chunk_items), 0)
    chunk_id = lax.broadcasted_iota(jnp.int32, (n_items, chunk_items), 1) + m * chunk_items
    to_chunk = jnp.where(item_id == chunk_id, 1.0, 0.0).astype(BF16)
    picks = jnp.dot(follows[:mine], to_chunk, preferred_element_type=F32)

    for h in range(halves):
        wait_for(r1.at[pl.ds(0, n_mp - 1), pl.ds(h * half_items, half_items)], r1_recv.at[h])
    total = tok_mean[...] * (1.0 / ITEM_TOK)
    for j in range(n_mp):
        total = total + r1[j].astype(F32)
    embedding = total.astype(BF16)
    emb_out[...] = embedding

    def dp_block(k):
        return pl.ds(pl.multiple_of(k * item_dev, item_dev), item_dev)

    items[dp_block(d), :] = embedding
    for k in range(n_dp // 2):
        j = lax.rem(d + 2 * k, n_dp) if k else sibling
        to_dp(
            items.at[dp_block(d)], items.at[dp_block(d)], dp_send.at[0], item_recv.at[d], j
        ).start()
    for k in range(1, n_dp // 2):
        j = lax.rem(d + n_dp - 2 * k, n_dp)
        wait_for(items.at[dp_block(j)], item_recv.at[j])
        to_dp(
            items.at[dp_block(j)], items.at[dp_block(j)], dp_send.at[0], item_recv.at[j], sibling
        ).start()
    for k in range(n_dp // 2):
        j = lax.rem(sibling + n_dp - 2 * k, n_dp)
        wait_for(items.at[dp_block(j)], item_recv.at[j])

    placed = jnp.dot(holds, items[...], preferred_element_type=F32)
    x_buf[m] = placed.astype(BF16)
    for k in range(1, n_mp):
        j = lax.rem(m + k, n_mp)
        to_mp(x_buf.at[m], x_buf.at[m], mp_send.at[1], mp_recv.at[1], j).start()

    def item_block(k):
        return pl.ds(pl.multiple_of(k * chunk_items, chunk_items), chunk_items)

    it_buf[m] = items[item_block(m), :]
    for k in range(1, n_mp):
        j = lax.rem(m + k, n_mp)
        to_mp(items.at[item_block(j)], it_buf.at[m], it_sem.at[0], it_sem.at[1], j).start()
    wait_for(x_buf.at[pl.ds(0, n_mp - 1)], mp_recv.at[1])

    states = [x_buf[j].astype(F32) for j in range(n_mp)]
    squares = states[0] * states[0]
    for block in states[1:]:
        squares = squares + block * block
    features = n_mp * LANES
    inverse = lax.rsqrt(jnp.sum(squares, axis=1, keepdims=True) / features + 1e-05)
    normed = jnp.concatenate(
        [(states[j] * inverse * gains[j]).astype(BF16) for j in range(n_mp)], axis=1
    )
    query = jnp.dot(normed, wq_v[...], preferred_element_type=F32)
    key = jnp.dot(normed, wk_v[...], preferred_element_type=F32)
    value = jnp.dot(normed, wv_v[...], preferred_element_type=F32)

    long_here = pl.ds(pl.multiple_of(d * long_rows, long_rows), long_rows)
    cosine = jnp.concatenate([cos_t[0:short, :], cos_t[long_here, :]], axis=0)
    sine = jnp.concatenate([sin_t[0:short, :], sin_t[long_here, :]], axis=0)
    lane = lax.broadcasted_iota(jnp.int32, (mine, LANES), 1)
    low = lax.rem(lane, HEAD_DIM) < HEAD_DIM // 2
    left = lane < HEAD_DIM

    def rotate(v):
        swapped = jnp.where(
            low,
            pltpu.roll(v, LANES - HEAD_DIM // 2, axis=1),
            pltpu.roll(v, HEAD_DIM // 2, axis=1),
        )
        return v * cosine + swapped * sine

    query = rotate(query) * HEAD_DIM ** (-0.5)
    key = rotate(key)
    first_kv = (lane * 0 + lax.rem(m // 4, 2)) == 0
    key_part = jnp.where(first_kv, key, pltpu.roll(key, HEAD_DIM, axis=1))
    value_part = jnp.where(first_kv, pltpu.roll(value, HEAD_DIM, axis=1), value)
    pair = jnp.where(left, key_part, value_part).astype(BF16)
    kv_long[long_here, :] = pair[short:]
    for k in range(1, n_dp):
        j = lax.rem(d + k, n_dp)
        to_dp(
            kv_long.at[long_here], kv_long.at[long_here], dp_send.at[1], dp_recv.at[1], j
        ).start()

    head0 = jnp.where(left, query, 0.0).astype(BF16)
    head1 = jnp.where(left, pltpu.roll(query, HEAD_DIM, axis=1), 0.0).astype(BF16)

    def attend(q_rows, keys, first_position):
        count, n_keys = q_rows.shape[0], keys.shape[0]
        scores = lax.dot_general(q_rows, keys, NT, preferred_element_type=F32)
        at = lax.rem(lax.broadcasted_iota(jnp.int32, (count, n_keys), 0), count // 2)
        of = lax.broadcasted_iota(jnp.int32, (count, n_keys), 1)
        weights = jnp.where(of <= at + first_position, jnp.exp(scores), 0.0)
        weights = (weights / jnp.sum(weights, axis=1, keepdims=True)).astype(BF16)
        mixed = jnp.dot(weights, keys, preferred_element_type=F32)
        top, bottom = mixed[: count // 2], mixed[count // 2 :]
        at_left = lax.broadcasted_iota(jnp.int32, top.shape, 1) < HEAD_DIM
        return jnp.where(at_left, pltpu.roll(top, HEAD_DIM, axis=1), bottom).astype(BF16)

    short_rows = attend(
        jnp.concatenate([head0[:short], head1[:short]], axis=0), pair[:short], 0
    )
    wait_for(
        kv_long.at[pl.ds(0, (n_dp - 1) * long_rows)], dp_recv.at[1]
    )
    rest = attend(
        jnp.concatenate([head0[short:], head1[short:]], axis=0), kv_long[...], d * long_rows
    )
    attended = jnp.concatenate([short_rows, rest], axis=0)
    attn = jnp.dot(attended, wo_v[...], preferred_element_type=F32).astype(BF16)
    for j in range(n_mp):
        s5[j] = attn[:, j * LANES : (j + 1) * LANES]
    r5[m] = s5[m]
    for k in range(1, n_mp):
        j = lax.rem(m + k, n_mp)
        to_mp(s5.at[j], r5.at[m], mp_send.at[2], mp_recv.at[2], j).start()

    wait_for(it_buf.at[pl.ds(0, n_mp - 1)], it_sem.at[1])
    wide_items = [it_buf[j].astype(F32) for j in range(n_mp)]
    item_squares = wide_items[0] * wide_items[0]
    for block in wide_items[1:]:
        item_squares = item_squares + block * block
    item_scale = lax.rsqrt(jnp.sum(item_squares, axis=1, keepdims=True) + 1e-06)
    for j in range(n_mp):
        iu[:, j * LANES : (j + 1) * LANES] = (wide_items[j] * item_scale).astype(BF16)

    wait_for(r5.at[pl.ds(0, n_mp - 1)], mp_recv.at[2])
    combined = placed
    for j in range(n_mp):
        combined = combined + r5[j].astype(F32)
    combined = jnp.where(valid > 0.5, combined, 0.0).astype(BF16)
    u_buf[m] = combined
    for k in range(1, n_mp):
        j = lax.rem(m + k, n_mp)
        to_mp(u_buf.at[m], u_buf.at[m], mp_send.at[3], mp_recv.at[3], j).start()
    us_long[long_here, :] = combined[short:]
    for k in range(1, n_dp):
        j = lax.rem(d + k, n_dp)
        to_dp(
            us_long.at[long_here], us_long.at[long_here], dp_send.at[2], dp_recv.at[2], j
        ).start()

    wait_for(u_buf.at[pl.ds(0, n_mp - 1)], mp_recv.at[3])
    users = [u_buf[j] for j in range(n_mp)]
    user_squares = users[0].astype(F32) * users[0].astype(F32)
    for block in users[1:]:
        user_squares = user_squares + block.astype(F32) * block.astype(F32)
    user_scale = lax.rsqrt(jnp.sum(user_squares, axis=1, keepdims=True) + 1e-06)
    logits = lax.dot_general(
        jnp.concatenate(users, axis=1), iu[...], NT, preferred_element_type=F32
    ) * (SCALE * user_scale)
    stack = jnp.concatenate(
        [jnp.exp(logits), logits * picks, jnp.zeros((LANES - 2 * mine, chunk_items), F32)], axis=0
    )
    sums = lax.dot_general(
        jnp.ones((8, chunk_items), F32), stack, NT,
        precision=lax.Precision.HIGHEST, preferred_element_type=F32,
    )
    tp[m] = sums[0:1]
    for k in range(1, n_mp):
        j = lax.rem(m + k, n_mp)
        to_mp(tp.at[m], tp.at[m], mp_send.at[4], mp_recv.at[4], j).start()

    wait_for(us_long.at[pl.ds(0, (n_dp - 1) * long_rows)], dp_recv.at[2])
    short_states = jnp.concatenate(
        [combined[:short].astype(F32), jnp.zeros((positions - short, LANES), F32)], axis=0
    )
    us_out[...] = jnp.where(is_long, us_long[...].astype(F32), short_states).astype(BF16)

    wait_for(tp.at[pl.ds(0, n_mp - 1)], mp_recv.at[4])
    sums = tp[0]
    for j in range(1, n_mp):
        sums = sums + tp[j]
    sums = jnp.broadcast_to(sums, (8, LANES))
    counted = has_target > 0.5
    picked = pltpu.roll(sums, LANES - mine, axis=1)
    loss = jnp.where(counted, jnp.log(jnp.where(counted, sums, 1.0)) - picked, 0.0)
    at_lane = lax.broadcasted_iota(jnp.int32, (LANES, positions), 0)
    at_position = lax.broadcasted_iota(jnp.int32, (LANES, positions), 1)
    chosen = (at_lane >= short) & (at_lane < mine)
    chosen = chosen & (at_position == at_lane - short + d * long_rows)
    spread = jnp.dot(
        loss, jnp.where(chosen, 1.0, 0.0),
        precision=lax.Precision.HIGHEST, preferred_element_type=F32,
    )
    ll[d] = spread[0:1]
    for k in range(1, n_dp):
        j = lax.rem(d + k, n_dp)
        to_dp(ll.at[d], ll.at[d], dp_send.at[3], dp_recv.at[3], j).start()
    same = (at_lane < short) & (at_position == at_lane)
    short_loss = jnp.dot(
        loss, jnp.where(same, 1.0, 0.0),
        precision=lax.Precision.HIGHEST, preferred_element_type=F32,
    )[0:1]
    wait_for(ll.at[pl.ds(0, n_dp - 1)], dp_recv.at[3])
    long_loss = ll[0]
    for j in range(1, n_dp):
        long_loss = long_loss + ll[j]
    loss_out[...] = jnp.where(is_long, long_loss, short_loss)

    for c in range(CHUNKS):
        wait_for(g_buf.at[pl.ds(0, n_mp - 1), pl.ds(c * chunk_rows, chunk_rows)], g_send.at[c])
    wait_for(s1.at[pl.ds(0, n_mp - 1)], mp_send.at[0])
    wait_for(x_buf.at[pl.ds(0, n_mp - 1)], mp_send.at[1])
    wait_for(s5.at[pl.ds(0, n_mp - 1)], mp_send.at[2])
    wait_for(u_buf.at[pl.ds(0, n_mp - 1)], mp_send.at[3])
    wait_for(tp.at[pl.ds(0, n_mp - 1)], mp_send.at[4])
    wait_for(it_buf.at[pl.ds(0, n_mp - 1)], it_sem.at[0])
    wait_for(items.at[pl.ds(0, (n_dp - 1) * item_dev)], dp_send.at[0])
    wait_for(kv_long.at[pl.ds(0, (n_dp - 1) * long_rows)], dp_send.at[1])
    wait_for(us_long.at[pl.ds(0, (n_dp - 1) * long_rows)], dp_send.at[2])
    wait_for(ll.at[pl.ds(0, n_dp - 1)], dp_send.at[3])


def solution(mesh, short=SHORT):
    n_dp, n_mp = mesh.shape["dp"], mesh.shape["mp"]

    def local(tok, wg, wu, wd, gain, wq, wk, wv, wo, item_slot, lengths, targets):
        rows, features = tok.shape[0], wg.shape[0]
        ff, item_dev, positions = wg.shape[1], item_slot.shape[0], targets.shape[0]
        n_items = n_dp * item_dev
        mine = short + positions // n_dp
        cos_table, sin_table = rope_tables(positions)
        any_spec = pl.BlockSpec(memory_space=pl.ANY)
        vmem = pl.BlockSpec(memory_space=pltpu.VMEM)
        dma = pltpu.SemaphoreType.DMA
        sizes = (n_dp, n_mp, rows, ff, item_dev, short, positions)
        embeddings, states, losses = pl.pallas_call(
            functools.partial(kernel, sizes),
            out_shape=(
                jax.ShapeDtypeStruct((item_dev, LANES), BF16),
                jax.ShapeDtypeStruct((positions, LANES), BF16),
                jax.ShapeDtypeStruct((1, positions), F32),
            ),
            in_specs=[any_spec] * 8 + [vmem] * 4,
            out_specs=(vmem, vmem, vmem),
            scratch_shapes=[
                pltpu.VMEM((n_mp, rows, LANES), BF16),
                pltpu.VMEM((features, ff), BF16),
                pltpu.VMEM((features, ff), BF16),
                pltpu.VMEM((ff, features), BF16),
                pltpu.VMEM((features, LANES), BF16),
                pltpu.VMEM((features, LANES), BF16),
                pltpu.VMEM((features, LANES), BF16),
                pltpu.VMEM((LANES, features), BF16),
                pltpu.VMEM((item_dev, ff), F32),
                pltpu.VMEM((item_dev, LANES), F32),
                pltpu.VMEM((n_mp, item_dev, LANES), BF16),
                pltpu.VMEM((n_mp, item_dev, LANES), BF16),
                pltpu.VMEM((n_items, LANES), BF16),
                pltpu.VMEM((n_mp, mine, LANES), BF16),
                pltpu.VMEM((n_mp, n_items // n_mp, LANES), BF16),
                pltpu.VMEM((n_items // n_mp, features), BF16),
                pltpu.VMEM((positions, LANES), BF16),
                pltpu.VMEM((n_mp, mine, LANES), BF16),
                pltpu.VMEM((n_mp, mine, LANES), BF16),
                pltpu.VMEM((positions, LANES), BF16),
                pltpu.VMEM((n_mp, mine, LANES), BF16),
                pltpu.VMEM((n_mp, 1, LANES), F32),
                pltpu.VMEM((n_dp, 1, LANES), jnp.int32),
                pltpu.VMEM((n_mp, 1, LANES), F32),
                pltpu.VMEM((n_dp, 1, positions), F32),
                dma((8,)),
                dma((CHUNKS,)),
                dma((CHUNKS, 4)),
                dma((5,)),
                dma((5,)),
                dma((2,)),
                dma((2,)),
                dma((4,)),
                dma((4,)),
                dma((n_dp,)),
                dma((4,)),
            ],
            compiler_params=pltpu.CompilerParams(
                collective_id=0, has_side_effects=True, vmem_limit_bytes=48 * 1024 * 1024
            ),
        )(
            tok, wg, wu, wd, wq, wk, wv, wo,
            gain.reshape(1, LANES), item_slot.reshape(1, item_dev),
            jnp.asarray(cos_table), jnp.asarray(sin_table),
        )
        return embeddings, states, losses.reshape(positions)

    return jax.shard_map(
        local,
        mesh=mesh,
        in_specs=(
            P("dp", "mp"), P(None, "mp"), P(None, "mp"), P("mp", None), P("mp"),
            P(None, "mp"), P(), P(), P("mp", None), P("dp"), P("dp"), P("dp"),
        ),
        out_specs=(P("dp", "mp"), P("dp", "mp"), P("dp")),
        check_vma=False,
    )
```

```python
import functools

import jax
import jax.numpy as jnp
import numpy as np
from jax import lax
from jax.experimental import pallas as pl
from jax.experimental.pallas import tpu as pltpu
from jax.sharding import PartitionSpec as P

HEAD_DIM = 64
ITEM_TOK = 32
SCALE = 20.0
SHORT = 32
LANES = 128
RING = 4
SPOT = (0, 2, 3, 1)
CHUNKS = 8
MESH = pl.DeviceIdType.MESH
BF16 = jnp.bfloat16
F32 = jnp.float32
NT = (((1,), (1,)), ((), ()))


def rope_tables(positions):
    half = HEAD_DIM // 2
    exponent = np.arange(half, dtype=np.float32) * np.float32(2.0 / HEAD_DIM)
    frequency = (10000.0 ** (-exponent.astype(np.float64))).astype(np.float32)
    angles = np.arange(positions, dtype=np.float32)[:, None] * frequency[None, :]
    angles = angles.astype(np.float64)
    cosine, sine = np.cos(angles), np.sin(angles)
    cos_table = np.concatenate([cosine, cosine, cosine, cosine], axis=1)
    sin_table = np.concatenate([-sine, sine, -sine, sine], axis=1)
    return cos_table.astype(np.float32), sin_table.astype(np.float32)


def kernel(
    sizes,
    tok, wg, wu, wd, wq, wk, wv, wo, gain, slot, cos_t, sin_t,
    emb_out, us_out, loss_out,
    g_buf, tok_v, w2, wg_v, wu_v, wd_v, wq_v, wk_v, wv_v, wo_v,
    pooled, pooled2, pooled_out, pooled_in, tok_mean, s1, r1, items, x_buf, it_buf, iu, kv_long, s5, r5, us_long, u_buf,
    gains, slots, tp, ll,
    w_sem, e_send, e_recv, gx_send, gy_send, g_recv, w2_send, w2_first, w2_up, w2_down, w2_side, p_sem,
    mp_send, mp_recv, r1_recv, it_sem, dp_send, dp_recv, item_recv, gs_sem,
):
    n_dp, n_mp, rows, ff, item_dev, short, positions = sizes
    n_items = n_dp * item_dev
    long_rows = positions // n_dp
    mine = short + long_rows
    chunk_items = n_items // n_mp
    half_rows = rows // 2
    chunk_rows = half_rows // CHUNKS
    x_rows = chunk_rows // 2
    span = 2 * chunk_rows
    pool_items = span // ITEM_TOK
    half_items = item_dev // 2
    d = lax.axis_index("dp")
    m = lax.axis_index("mp")
    sibling = d + 1 - 2 * lax.rem(d, 2)

    def to_mp(src, dst, send_sem, recv_sem, j):
        return pltpu.make_async_remote_copy(
            src_ref=src, dst_ref=dst, send_sem=send_sem, recv_sem=recv_sem,
            device_id={"mp": j}, device_id_type=MESH,
        )

    def to_dp(src, dst, send_sem, recv_sem, j):
        return pltpu.make_async_remote_copy(
            src_ref=src, dst_ref=dst, send_sem=send_sem, recv_sem=recv_sem,
            device_id={"dp": j}, device_id_type=MESH,
        )

    def wait_for(ref, sem):
        pltpu.make_async_copy(ref, ref, sem).wait()

    barrier = pltpu.get_barrier_semaphore()
    for k in range(1, n_mp):
        pl.semaphore_signal(
            barrier, inc=1, device_id={"mp": lax.rem(m + k, n_mp)}, device_id_type=MESH
        )
    for k in range(1, n_dp):
        pl.semaphore_signal(
            barrier, inc=1, device_id={"dp": lax.rem(d + k, n_dp)}, device_id_type=MESH
        )

    kv_block = pl.ds(pl.multiple_of((m // 8) * LANES, LANES), LANES)
    at_half = pl.ds(pl.multiple_of((lax.rem(m, RING) // 2) * half_rows, half_rows), half_rows)
    at_spot = m // RING * RING + lax.rem((lax.rem(m, RING) + 1) // 2, 2) * 2 + lax.rem(m, RING) // 2
    loads = [
        (tok.at[at_half], g_buf.at[at_spot]), (tok, tok_v), (wg, wg_v), (wu, wu_v), (wd, wd_v),
        (wq, wq_v), (wk.at[:, kv_block], wk_v), (wv.at[:, kv_block], wv_v), (wo, wo_v),
    ]
    copies = [pltpu.make_async_copy(a, b, w_sem.at[i]) for i, (a, b) in enumerate(loads)]
    for copy in copies:
        copy.start()
    token_of = lax.broadcasted_iota(jnp.int32, (item_dev, rows), 1) // ITEM_TOK
    token_row = lax.broadcasted_iota(jnp.int32, (item_dev, rows), 0)
    token_pool = (token_of == token_row).astype(F32).astype(BF16)
    gains[m] = gain[...]
    slots[d] = jnp.concatenate(
        [slot[...], jnp.full((1, LANES - item_dev), -1, jnp.int32)], axis=1
    )
    pl.semaphore_wait(barrier, n_mp + n_dp - 2)

    x_at, y_at = m // RING, lax.rem(m, RING)
    half = y_at // 2
    pair_at = lax.rem((y_at + 1) // 2, 2)
    base = x_at * RING + pair_at * 2
    partner = x_at * RING + 3 - y_at
    beside = x_at * RING + y_at + 1 - 2 * lax.rem(y_at, 2)
    x_next = lax.rem(x_at + 1, RING)
    x_back = lax.rem(x_at + RING - 1, RING)
    x_far = lax.rem(x_at + 2, RING)
    ahead, behind = x_next * RING + y_at, x_back * RING + y_at
    X1, X2, X3, Y1, Y2, Y3 = range(6)

    def chunk(c):
        return pl.ds(pl.multiple_of(c * chunk_rows, chunk_rows), chunk_rows)

    def rows_x(c):
        return pl.ds(pl.multiple_of(c * chunk_rows, 16), x_rows)

    def rows_y(c):
        return pl.ds(pl.multiple_of(c * chunk_rows + x_rows, 16), chunk_rows - x_rows)

    def forward(start, count, there, sem, stage, c, target):
        blocks = g_buf.at[pl.ds(start, count), there]
        to_mp(blocks, blocks, sem.at[c], g_recv.at[c, stage], target).start()

    def arrived(count, there, stage, c):
        wait_for(g_buf.at[pl.ds(0, count), there], g_recv.at[c, stage])

    def stage_exchange(c):
        theirs = (1 - half) * half_rows + c * chunk_rows
        to_mp(
            tok.at[pl.ds(pl.multiple_of(theirs, chunk_rows), chunk_rows)],
            g_buf.at[base + half, chunk(c)], e_send.at[c], e_recv.at[c], partner,
        ).start()

    def stage_own(c):
        wait_for(g_buf.at[0, chunk(c)], e_recv.at[c])
        forward(base, 2, rows_x(c), gx_send, X1, c, ahead)
        forward(base, 2, rows_x(c), gx_send, X1, c, behind)
        forward(base, 2, rows_y(c), gy_send, Y1, c, beside)

    def stage_first(c):
        arrived(2, rows_y(c), Y1, c)
        forward(x_at * RING, 4, rows_y(c), gy_send, Y2, c, ahead)
        forward(x_at * RING, 4, rows_y(c), gy_send, Y2, c, behind)
        arrived(4, rows_x(c), X1, c)
        forward(x_back * RING + pair_at * 2, 1, rows_x(c), gx_send, X2, c, ahead)
        forward(x_next * RING + pair_at * 2 + 1, 1, rows_x(c), gx_send, X2, c, behind)

    def stage_second(c):
        arrived(2, rows_x(c), X2, c)
        for k in range(RING):
            forward(k * RING + pair_at * 2, 2, rows_x(c), gx_send, X3, c, beside)
        arrived(8, rows_y(c), Y2, c)
        forward(x_back * RING, 2, rows_y(c), gy_send, Y3, c, ahead)
        forward(x_next * RING + 2, 2, rows_y(c), gy_send, Y3, c, behind)

    def stage_last(c):
        arrived(8, rows_x(c), X3, c)
        arrived(4, rows_y(c), Y3, c)

    core = lax.rem(d, 2)

    def piece(steps):
        return lax.rem(d + n_dp + 2 * steps, n_dp)

    def pass_on(steps, part, target, sem):
        k = piece(steps)
        ref = w2.at[k] if part is None else w2.at[k, part]
        to_dp(ref, ref, w2_send, sem, target).start()

    def weights_start():
        lanes = pl.ds(pl.multiple_of(d * LANES, LANES), LANES)
        for part, ref in enumerate((wg, wu)):
            to_mp(ref.at[:, lanes], w2.at[d, part], w2_send, w2_first, partner).start()

    def weights_step(k):
        up, down = piece(1), piece(-1)
        if k == 0:
            wait_for(w2.at[0], w2_first)
            pass_on(0, None, up, w2_up.at[0])
            pass_on(0, None, down, w2_down.at[0])
            pass_on(0, None, sibling, w2_side)
            return
        wait_for(w2.at[0], w2_up.at[k - 1])
        wait_for(w2.at[0], w2_down.at[k - 1])
        last = k == n_dp // 4 - 1
        pass_on(-k, 0 if last else None, up, w2_up.at[k])
        pass_on(k, 1 if last else None, down, w2_down.at[k])
        pass_on(-k, None, sibling, w2_side)
        pass_on(k, None, sibling, w2_side)

    def weights_end():
        k = n_dp // 4 - 1
        wait_for(w2.at[0, 0], w2_up.at[k])
        wait_for(w2.at[0, 1], w2_down.at[k])
        pass_on(n_dp // 4, None, sibling, w2_side)

    pool_of = lax.broadcasted_iota(jnp.int32, (pool_items, span), 1) // ITEM_TOK
    pool_row = lax.broadcasted_iota(jnp.int32, (pool_items, span), 0)
    pool = (pool_of == pool_row).astype(F32).astype(BF16)

    def ffn(k, gate_w, up_w, result):
        here = pl.ds(pl.multiple_of(k * span, span), span)
        wide = jnp.concatenate(
            [g_buf[j // RING * RING + SPOT[j % RING], here, :] for j in range(n_mp)], axis=1
        )
        gate = lax.dot_general(gate_w, wide, NT, preferred_element_type=F32)
        up = lax.dot_general(up_w, wide, NT, preferred_element_type=F32)
        hidden = (gate / (1.0 + jnp.exp(-gate)) * up).astype(BF16)
        there = pl.ds(pl.multiple_of(k * pool_items, pool_items), pool_items)
        result[there, :] = lax.dot_general(pool, hidden, NT, preferred_element_type=F32)

    def ffn_own(k):
        ffn(k, wg_v[...], wu_v[...], pooled)

    def ffn_partner(k):
        gate_w = jnp.concatenate([w2[j, 0] for j in range(n_mp)], axis=1)
        up_w = jnp.concatenate([w2[j, 1] for j in range(n_mp)], axis=1)
        ffn(k, gate_w, up_w, pooled2)

    def stage_down(h, source, order):
        here = pl.ds(pl.multiple_of(h * half_items, half_items), half_items)
        part = jnp.dot(source, wd_v[...], preferred_element_type=F32).astype(BF16)
        for j in range(n_mp):
            s1[j, here, :] = part[:, j * LANES : (j + 1) * LANES]
        r1[m, here, :] = s1[m, here, :]
        for k in range(1, n_mp):
            j = lax.rem(m + k, n_mp)
            to_mp(s1.at[j, here], r1.at[m, here], mp_send.at[0], r1_recv.at[order], j).start()

    def step(i, carry):
        @pl.when(i < CHUNKS - 2)
        def _():
            stage_exchange(i + 2)

        @pl.when(i < CHUNKS)
        def _():
            stage_own(i)

        @pl.when((i >= 1) & (i < CHUNKS + 1))
        def _():
            stage_first(i - 1)

        @pl.when((i >= 2) & (i < CHUNKS + 2))
        def _():
            stage_second(i - 2)

        for k in range(n_dp // 4):
            @pl.when(i == k + 1)
            def _(k=k):
                weights_step(k)

        @pl.when(i == n_dp // 4 + 1)
        def _():
            weights_end()

        @pl.when((i >= 3) & (i < CHUNKS + 3))
        def _():
            stage_last(i - 3)

        @pl.when(i == 3)
        def _():
            for copy in copies[1:]:
                copy.wait()
            token_sum = jnp.dot(token_pool, tok_v[...], preferred_element_type=F32)
            tok_mean[...] = token_sum * (1.0 / ITEM_TOK)

        @pl.when(i == CHUNKS - 1)
        def _():
            wait_for(w2.at[pl.ds(0, n_dp // 2)], w2_side)

        @pl.when(i >= CHUNKS - 1)
        def _():
            ffn_partner(i - CHUNKS + 1)

        @pl.when(i == CHUNKS + 2)
        def _():
            pooled_out[...] = (pooled2[...] * (1.0 / ITEM_TOK)).astype(BF16)
            to_mp(pooled_out, pooled_in, p_sem.at[0], p_sem.at[1], partner).start()

        @pl.when((i >= 4) & (lax.rem(i, 2) == 0))
        def _():
            ffn_own((i - 4) // 2)

        return carry

    for k in range(1, n_mp):
        j = lax.rem(m + k, n_mp)
        to_mp(gains.at[m], gains.at[m], gs_sem.at[0], gs_sem.at[1], j).start()
    for k in range(1, n_dp):
        j = lax.rem(d + k, n_dp)
        to_dp(slots.at[d], slots.at[d], gs_sem.at[2], gs_sem.at[3], j).start()

    copies[0].wait()
    stage_exchange(0)
    stage_exchange(1)
    weights_start()
    lax.fori_loop(0, CHUNKS + 3, step, 0)
    stage_down(half, (pooled[...] * (1.0 / ITEM_TOK)).astype(BF16), 0)
    wait_for(pooled_in, p_sem.at[1])
    stage_down(1 - half, pooled_in[...], 1)

    for i, (ref, count) in enumerate(((gains, n_mp), (gains, n_mp), (slots, n_dp), (slots, n_dp))):
        wait_for(ref.at[pl.ds(0, count - 1)], gs_sem.at[i])

    slot_row = jnp.concatenate([slots[k][:, :item_dev] for k in range(n_dp)], axis=1)
    last = (slot_row >= 0) & (jnp.bitwise_and(slot_row, positions - 1) == positions - 1)
    long_base = jnp.max(
        jnp.where(last, slot_row, positions - 1), axis=1, keepdims=True
    ) - (positions - 1)
    is_long = long_base == d * positions
    row = lax.broadcasted_iota(jnp.int32, (LANES, 1), 0)
    position = jnp.where(row < short, row, row - short + d * long_rows)
    row_slot = jnp.where(row < short, d * positions, long_base) + position
    row_slot = jnp.where(row < mine, row_slot, -2)
    holds = jnp.where(slot_row == row_slot[:mine], 1.0, 0.0).astype(BF16)
    next_slot = jnp.where((position + 1 < positions) & (row < mine), row_slot + 1, -2)
    follows = jnp.where(slot_row == next_slot, 1.0, 0.0).astype(BF16)
    valid = jnp.sum(holds.astype(F32), axis=1, keepdims=True)
    has_target = lax.dot_general(
        jnp.ones((8, n_items), BF16), follows, NT, preferred_element_type=F32
    )
    item_id = lax.broadcasted_iota(jnp.int32, (n_items, chunk_items), 0)
    chunk_id = lax.broadcasted_iota(jnp.int32, (n_items, chunk_items), 1) + m * chunk_items
    to_chunk = jnp.where(item_id == chunk_id, 1.0, 0.0).astype(BF16)
    picks = jnp.dot(follows[:mine], to_chunk, preferred_element_type=F32)

    for h in range(2):
        wait_for(r1.at[pl.ds(0, n_mp - 1), pl.ds(0, half_items)], r1_recv.at[h])
    total = tok_mean[...]
    for j in range(n_mp):
        total = total + r1[j].astype(F32)
    embedding = total.astype(BF16)
    emb_out[...] = embedding

    def dp_block(k):
        return pl.ds(pl.multiple_of(k * item_dev, item_dev), item_dev)

    items[dp_block(d), :] = embedding
    for k in range(n_dp // 2):
        j = lax.rem(d + 2 * k, n_dp) if k else sibling
        to_dp(
            items.at[dp_block(d)], items.at[dp_block(d)], dp_send.at[0], item_recv.at[d], j
        ).start()
    for k in range(1, n_dp // 2):
        j = lax.rem(d + n_dp - 2 * k, n_dp)
        wait_for(items.at[dp_block(j)], item_recv.at[j])
        to_dp(
            items.at[dp_block(j)], items.at[dp_block(j)], dp_send.at[0], item_recv.at[j], sibling
        ).start()
    for k in range(n_dp // 2):
        j = lax.rem(sibling + n_dp - 2 * k, n_dp)
        wait_for(items.at[dp_block(j)], item_recv.at[j])

    placed = jnp.dot(holds, items[...], preferred_element_type=F32)
    x_buf[m] = placed.astype(BF16)
    for k in range(1, n_mp):
        j = lax.rem(m + k, n_mp)
        to_mp(x_buf.at[m], x_buf.at[m], mp_send.at[1], mp_recv.at[1], j).start()

    def item_block(k):
        return pl.ds(pl.multiple_of(k * chunk_items, chunk_items), chunk_items)

    it_buf[m] = items[item_block(m), :]
    for k in range(1, n_mp):
        j = lax.rem(m + k, n_mp)
        to_mp(items.at[item_block(j)], it_buf.at[m], it_sem.at[0], it_sem.at[1], j).start()
    wait_for(x_buf.at[pl.ds(0, n_mp - 1)], mp_recv.at[1])

    states = [x_buf[j].astype(F32) for j in range(n_mp)]
    squares = states[0] * states[0]
    for block in states[1:]:
        squares = squares + block * block
    features = n_mp * LANES
    inverse = lax.rsqrt(jnp.sum(squares, axis=1, keepdims=True) / features + 1e-05)
    normed = jnp.concatenate(
        [(states[j] * inverse * gains[j]).astype(BF16) for j in range(n_mp)], axis=1
    )
    query = jnp.dot(normed, wq_v[...], preferred_element_type=F32)
    key = jnp.dot(normed, wk_v[...], preferred_element_type=F32)
    value = jnp.dot(normed, wv_v[...], preferred_element_type=F32)

    long_here = pl.ds(pl.multiple_of(d * long_rows, long_rows), long_rows)
    cosine = jnp.concatenate([cos_t[0:short, :], cos_t[long_here, :]], axis=0)
    sine = jnp.concatenate([sin_t[0:short, :], sin_t[long_here, :]], axis=0)
    lane = lax.broadcasted_iota(jnp.int32, (mine, LANES), 1)
    low = lax.rem(lane, HEAD_DIM) < HEAD_DIM // 2
    left = lane < HEAD_DIM

    def rotate(v):
        swapped = jnp.where(
            low,
            pltpu.roll(v, LANES - HEAD_DIM // 2, axis=1),
            pltpu.roll(v, HEAD_DIM // 2, axis=1),
        )
        return v * cosine + swapped * sine

    query = rotate(query) * HEAD_DIM ** (-0.5)
    key = rotate(key)
    first_kv = (lane * 0 + lax.rem(m // 4, 2)) == 0
    key_part = jnp.where(first_kv, key, pltpu.roll(key, HEAD_DIM, axis=1))
    value_part = jnp.where(first_kv, pltpu.roll(value, HEAD_DIM, axis=1), value)
    pair = jnp.where(left, key_part, value_part).astype(BF16)
    kv_long[long_here, :] = pair[short:]
    for k in range(1, n_dp):
        j = lax.rem(d + k, n_dp)
        to_dp(
            kv_long.at[long_here], kv_long.at[long_here], dp_send.at[1], dp_recv.at[1], j
        ).start()

    head0 = jnp.where(left, query, 0.0).astype(BF16)
    head1 = jnp.where(left, pltpu.roll(query, HEAD_DIM, axis=1), 0.0).astype(BF16)

    def attend(q_rows, keys, first_position):
        count, n_keys = q_rows.shape[0], keys.shape[0]
        scores = lax.dot_general(q_rows, keys, NT, preferred_element_type=F32)
        at = lax.rem(lax.broadcasted_iota(jnp.int32, (count, n_keys), 0), count // 2)
        of = lax.broadcasted_iota(jnp.int32, (count, n_keys), 1)
        weights = jnp.where(of <= at + first_position, jnp.exp(scores), 0.0)
        weights = (weights / jnp.sum(weights, axis=1, keepdims=True)).astype(BF16)
        mixed = jnp.dot(weights, keys, preferred_element_type=F32)
        top, bottom = mixed[: count // 2], mixed[count // 2 :]
        at_left = lax.broadcasted_iota(jnp.int32, top.shape, 1) < HEAD_DIM
        return jnp.where(at_left, pltpu.roll(top, HEAD_DIM, axis=1), bottom).astype(BF16)

    short_rows = attend(
        jnp.concatenate([head0[:short], head1[:short]], axis=0), pair[:short], 0
    )
    wait_for(
        kv_long.at[pl.ds(0, (n_dp - 1) * long_rows)], dp_recv.at[1]
    )
    rest = attend(
        jnp.concatenate([head0[short:], head1[short:]], axis=0), kv_long[...], d * long_rows
    )
    attended = jnp.concatenate([short_rows, rest], axis=0)
    attn = jnp.dot(attended, wo_v[...], preferred_element_type=F32).astype(BF16)
    for j in range(n_mp):
        s5[j] = attn[:, j * LANES : (j + 1) * LANES]
    r5[m] = s5[m]
    for k in range(1, n_mp):
        j = lax.rem(m + k, n_mp)
        to_mp(s5.at[j], r5.at[m], mp_send.at[2], mp_recv.at[2], j).start()

    wait_for(it_buf.at[pl.ds(0, n_mp - 1)], it_sem.at[1])
    wide_items = [it_buf[j].astype(F32) for j in range(n_mp)]
    item_squares = wide_items[0] * wide_items[0]
    for block in wide_items[1:]:
        item_squares = item_squares + block * block
    item_scale = lax.rsqrt(jnp.sum(item_squares, axis=1, keepdims=True) + 1e-06)
    for j in range(n_mp):
        iu[:, j * LANES : (j + 1) * LANES] = (wide_items[j] * item_scale).astype(BF16)

    wait_for(r5.at[pl.ds(0, n_mp - 1)], mp_recv.at[2])
    combined = placed
    for j in range(n_mp):
        combined = combined + r5[j].astype(F32)
    combined = jnp.where(valid > 0.5, combined, 0.0).astype(BF16)
    u_buf[m] = combined
    for k in range(1, n_mp):
        j = lax.rem(m + k, n_mp)
        to_mp(u_buf.at[m], u_buf.at[m], mp_send.at[3], mp_recv.at[3], j).start()
    us_long[long_here, :] = combined[short:]
    for k in range(1, n_dp):
        j = lax.rem(d + k, n_dp)
        to_dp(
            us_long.at[long_here], us_long.at[long_here], dp_send.at[2], dp_recv.at[2], j
        ).start()

    wait_for(u_buf.at[pl.ds(0, n_mp - 1)], mp_recv.at[3])
    users = [u_buf[j] for j in range(n_mp)]
    user_squares = users[0].astype(F32) * users[0].astype(F32)
    for block in users[1:]:
        user_squares = user_squares + block.astype(F32) * block.astype(F32)
    user_scale = lax.rsqrt(jnp.sum(user_squares, axis=1, keepdims=True) + 1e-06)
    logits = lax.dot_general(
        jnp.concatenate(users, axis=1), iu[...], NT, preferred_element_type=F32
    ) * (SCALE * user_scale)
    stack = jnp.concatenate(
        [jnp.exp(logits), logits * picks, jnp.zeros((LANES - 2 * mine, chunk_items), F32)], axis=0
    )
    sums = lax.dot_general(
        jnp.ones((8, chunk_items), F32), stack, NT,
        precision=lax.Precision.HIGHEST, preferred_element_type=F32,
    )
    tp[m] = sums[0:1]
    for k in range(1, n_mp):
        j = lax.rem(m + k, n_mp)
        to_mp(tp.at[m], tp.at[m], mp_send.at[4], mp_recv.at[4], j).start()

    wait_for(us_long.at[pl.ds(0, (n_dp - 1) * long_rows)], dp_recv.at[2])
    short_states = jnp.concatenate(
        [combined[:short].astype(F32), jnp.zeros((positions - short, LANES), F32)], axis=0
    )
    us_out[...] = jnp.where(is_long, us_long[...].astype(F32), short_states).astype(BF16)

    wait_for(tp.at[pl.ds(0, n_mp - 1)], mp_recv.at[4])
    sums = tp[0]
    for j in range(1, n_mp):
        sums = sums + tp[j]
    sums = jnp.broadcast_to(sums, (8, LANES))
    counted = has_target > 0.5
    picked = pltpu.roll(sums, LANES - mine, axis=1)
    loss = jnp.where(counted, jnp.log(jnp.where(counted, sums, 1.0)) - picked, 0.0)
    at_lane = lax.broadcasted_iota(jnp.int32, (LANES, positions), 0)
    at_position = lax.broadcasted_iota(jnp.int32, (LANES, positions), 1)
    chosen = (at_lane >= short) & (at_lane < mine)
    chosen = chosen & (at_position == at_lane - short + d * long_rows)
    spread = jnp.dot(
        loss, jnp.where(chosen, 1.0, 0.0),
        precision=lax.Precision.HIGHEST, preferred_element_type=F32,
    )
    ll[d] = spread[0:1]
    for k in range(1, n_dp):
        j = lax.rem(d + k, n_dp)
        to_dp(ll.at[d], ll.at[d], dp_send.at[3], dp_recv.at[3], j).start()
    same = (at_lane < short) & (at_position == at_lane)
    short_loss = jnp.dot(
        loss, jnp.where(same, 1.0, 0.0),
        precision=lax.Precision.HIGHEST, preferred_element_type=F32,
    )[0:1]
    wait_for(ll.at[pl.ds(0, n_dp - 1)], dp_recv.at[3])
    long_loss = ll[0]
    for j in range(1, n_dp):
        long_loss = long_loss + ll[j]
    loss_out[...] = jnp.where(is_long, long_loss, short_loss)

    for c in range(CHUNKS):
        wait_for(g_buf.at[0, pl.ds(0, chunk_rows)], e_send.at[c])
        wait_for(g_buf.at[pl.ds(0, n_mp - 2), pl.ds(0, x_rows)], gx_send.at[c])
        wait_for(g_buf.at[pl.ds(0, n_mp - 2), pl.ds(0, chunk_rows - x_rows)], gy_send.at[c])
    wait_for(w2, w2_send)
    wait_for(pooled_out, p_sem.at[0])
    wait_for(s1.at[pl.ds(0, n_mp - 1)], mp_send.at[0])
    wait_for(x_buf.at[pl.ds(0, n_mp - 1)], mp_send.at[1])
    wait_for(s5.at[pl.ds(0, n_mp - 1)], mp_send.at[2])
    wait_for(u_buf.at[pl.ds(0, n_mp - 1)], mp_send.at[3])
    wait_for(tp.at[pl.ds(0, n_mp - 1)], mp_send.at[4])
    wait_for(it_buf.at[pl.ds(0, n_mp - 1)], it_sem.at[0])
    wait_for(items.at[pl.ds(0, (n_dp - 1) * item_dev)], dp_send.at[0])
    wait_for(kv_long.at[pl.ds(0, (n_dp - 1) * long_rows)], dp_send.at[1])
    wait_for(us_long.at[pl.ds(0, (n_dp - 1) * long_rows)], dp_send.at[2])
    wait_for(ll.at[pl.ds(0, n_dp - 1)], dp_send.at[3])


def solution(mesh, short=SHORT):
    n_dp, n_mp = mesh.shape["dp"], mesh.shape["mp"]

    def local(tok, wg, wu, wd, gain, wq, wk, wv, wo, item_slot, lengths, targets):
        rows, features = tok.shape[0], wg.shape[0]
        ff, item_dev, positions = wg.shape[1], item_slot.shape[0], targets.shape[0]
        n_items = n_dp * item_dev
        mine = short + positions // n_dp
        cos_table, sin_table = rope_tables(positions)
        any_spec = pl.BlockSpec(memory_space=pl.ANY)
        vmem = pl.BlockSpec(memory_space=pltpu.VMEM)
        dma = pltpu.SemaphoreType.DMA
        sizes = (n_dp, n_mp, rows, ff, item_dev, short, positions)
        embeddings, states, losses = pl.pallas_call(
            functools.partial(kernel, sizes),
            out_shape=(
                jax.ShapeDtypeStruct((item_dev, LANES), BF16),
                jax.ShapeDtypeStruct((positions, LANES), BF16),
                jax.ShapeDtypeStruct((1, positions), F32),
            ),
            in_specs=[any_spec] * 8 + [vmem] * 4,
            out_specs=(vmem, vmem, vmem),
            scratch_shapes=[
                pltpu.VMEM((n_mp, rows // 2, LANES), BF16),
                pltpu.VMEM((rows, LANES), BF16),
                pltpu.VMEM((n_dp, 2, ff, LANES), BF16),
                pltpu.VMEM((ff, features), BF16),
                pltpu.VMEM((ff, features), BF16),
                pltpu.VMEM((ff, features), BF16),
                pltpu.VMEM((features, LANES), BF16),
                pltpu.VMEM((features, LANES), BF16),
                pltpu.VMEM((features, LANES), BF16),
                pltpu.VMEM((LANES, features), BF16),
                pltpu.VMEM((item_dev // 2, ff), F32),
                pltpu.VMEM((item_dev // 2, ff), F32),
                pltpu.VMEM((item_dev // 2, ff), BF16),
                pltpu.VMEM((item_dev // 2, ff), BF16),
                pltpu.VMEM((item_dev, LANES), F32),
                pltpu.VMEM((n_mp, item_dev, LANES), BF16),
                pltpu.VMEM((n_mp, item_dev, LANES), BF16),
                pltpu.VMEM((n_items, LANES), BF16),
                pltpu.VMEM((n_mp, mine, LANES), BF16),
                pltpu.VMEM((n_mp, n_items // n_mp, LANES), BF16),
                pltpu.VMEM((n_items // n_mp, features), BF16),
                pltpu.VMEM((positions, LANES), BF16),
                pltpu.VMEM((n_mp, mine, LANES), BF16),
                pltpu.VMEM((n_mp, mine, LANES), BF16),
                pltpu.VMEM((positions, LANES), BF16),
                pltpu.VMEM((n_mp, mine, LANES), BF16),
                pltpu.VMEM((n_mp, 1, LANES), F32),
                pltpu.VMEM((n_dp, 1, LANES), jnp.int32),
                pltpu.VMEM((n_mp, 1, LANES), F32),
                pltpu.VMEM((n_dp, 1, positions), F32),
                dma((9,)),
                dma((CHUNKS,)),
                dma((CHUNKS,)),
                dma((CHUNKS,)),
                dma((CHUNKS,)),
                dma((CHUNKS, 6)),
                dma,
                dma,
                dma((n_dp // 4,)),
                dma((n_dp // 4,)),
                dma,
                dma((2,)),
                dma((5,)),
                dma((5,)),
                dma((2,)),
                dma((2,)),
                dma((4,)),
                dma((4,)),
                dma((n_dp,)),
                dma((4,)),
            ],
            compiler_params=pltpu.CompilerParams(
                collective_id=0, has_side_effects=True, vmem_limit_bytes=64 * 1024 * 1024 - 65536
            ),
        )(
            tok, wg.T, wu.T, wd, wq, wk, wv, wo,
            gain.reshape(1, LANES), item_slot.reshape(1, item_dev),
            jnp.asarray(cos_table), jnp.asarray(sin_table),
        )
        return embeddings, states, losses.reshape(positions)

    return jax.shard_map(
        local,
        mesh=mesh,
        in_specs=(
            P("dp", "mp"), P(None, "mp"), P(None, "mp"), P("mp", None), P("mp"),
            P(None, "mp"), P(), P(), P("mp", None), P("dp"), P("dp"), P("dp"),
        ),
        out_specs=(P("dp", "mp"), P("dp", "mp"), P("dp")),
        check_vma=False,
    )
```

```python
import functools

import jax
import jax.numpy as jnp
import numpy as np
from jax import lax
from jax.experimental import pallas as pl
from jax.experimental.pallas import tpu as pltpu
from jax.sharding import PartitionSpec as P

HEAD_DIM = 64
ITEM_TOK = 32
SCALE = 20.0
SHORT = 32
LANES = 128
RING = 4
SPOT = (0, 2, 3, 1)
CHUNKS = 8
LAG = 2
AHEAD = 3
SPANS = 4
RING_STEPS = (1, 1, 2, 3, 4, 4, 5, 6, 7, 7)
MESH = pl.DeviceIdType.MESH
BF16 = jnp.bfloat16
F32 = jnp.float32
NT = (((1,), (1,)), ((), ()))


def rope_tables(positions):
    half = HEAD_DIM // 2
    exponent = np.arange(half, dtype=np.float32) * np.float32(2.0 / HEAD_DIM)
    frequency = (10000.0 ** (-exponent.astype(np.float64))).astype(np.float32)
    angles = np.arange(positions, dtype=np.float32)[:, None] * frequency[None, :]
    angles = angles.astype(np.float64)
    cosine, sine = np.cos(angles), np.sin(angles)
    cos_table = np.concatenate([cosine, cosine, cosine, cosine], axis=1)
    sin_table = np.concatenate([-sine, sine, -sine, sine], axis=1)
    return cos_table.astype(np.float32), sin_table.astype(np.float32)


def kernel(
    sizes,
    tok, wg, wu, wd, wq, wk, wv, wo, gain, slot, cos_t, sin_t,
    emb_out, us_out, loss_out,
    g_buf, tok_v, w2, wg_v, wu_v, wd_v, wq_v, wk_v, wv_v, wo_v,
    pooled, pooled2, pooled_out, pooled_in, tok_mean, s1, r1, items, x_buf, it_buf, iu, qkv, holds_long, s5, r5, us_long, u_buf,
    gains, slots, tp, ll,
    w_sem, e_recv, g_send, g_recv, w2_send, w2_first, w2_up, w2_down, w2_side, p_sem,
    mp_send, mp_recv, r1_recv, it_sem, dp_send, dp_recv, item_recv, qkv_recv, gs_sem,
):
    n_dp, n_mp, rows, ff, item_dev, short, positions = sizes
    n_items = n_dp * item_dev
    long_rows = positions // n_dp
    mine = short + long_rows
    chunk_items = n_items // n_mp
    half_rows = rows // 2
    chunk_rows = half_rows // CHUNKS
    x_rows = (chunk_rows // 2, chunk_rows // 2 - 16)
    span = half_rows // SPANS
    pool_items = span // ITEM_TOK
    half_items = item_dev // 2
    d = lax.axis_index("dp")
    m = lax.axis_index("mp")
    sibling = d + 1 - 2 * lax.rem(d, 2)

    def to_mp(src, dst, send_sem, recv_sem, j):
        return pltpu.make_async_remote_copy(
            src_ref=src, dst_ref=dst, send_sem=send_sem, recv_sem=recv_sem,
            device_id={"mp": j}, device_id_type=MESH,
        )

    def to_dp(src, dst, send_sem, recv_sem, j):
        return pltpu.make_async_remote_copy(
            src_ref=src, dst_ref=dst, send_sem=send_sem, recv_sem=recv_sem,
            device_id={"dp": j}, device_id_type=MESH,
        )

    def wait_for(ref, sem):
        pltpu.make_async_copy(ref, ref, sem).wait()

    barrier = pltpu.get_barrier_semaphore()
    for k in range(1, n_mp):
        pl.semaphore_signal(
            barrier, inc=1, device_id={"mp": lax.rem(m + k, n_mp)}, device_id_type=MESH
        )
    for k in range(1, n_dp):
        pl.semaphore_signal(
            barrier, inc=1, device_id={"dp": lax.rem(d + k, n_dp)}, device_id_type=MESH
        )

    kv_block = pl.ds(pl.multiple_of((m // 8) * LANES, LANES), LANES)
    at_half = pl.ds(pl.multiple_of((lax.rem(m, RING) // 2) * half_rows, half_rows), half_rows)
    at_spot = m // RING * RING + lax.rem((lax.rem(m, RING) + 1) // 2, 2) * 2 + lax.rem(m, RING) // 2
    loads = [
        (tok.at[at_half], g_buf.at[at_spot]), (tok, tok_v), (wg, wg_v), (wu, wu_v), (wd, wd_v),
        (wq, wq_v), (wk.at[:, kv_block], wk_v), (wv.at[:, kv_block], wv_v), (wo, wo_v),
    ]
    copies = [pltpu.make_async_copy(a, b, w_sem.at[i]) for i, (a, b) in enumerate(loads)]
    for copy in copies:
        copy.start()
    token_of = lax.broadcasted_iota(jnp.int32, (item_dev, rows), 1) // ITEM_TOK
    token_row = lax.broadcasted_iota(jnp.int32, (item_dev, rows), 0)
    token_pool = (token_of == token_row).astype(F32).astype(BF16)
    gains[m] = gain[...]
    slots[d] = jnp.concatenate(
        [slot[...], jnp.full((1, LANES - item_dev), -1, jnp.int32)], axis=1
    )
    pl.semaphore_wait(barrier, n_mp + n_dp - 2)

    x_at, y_at = m // RING, lax.rem(m, RING)
    half = y_at // 2
    pair_at = lax.rem((y_at + 1) // 2, 2)
    base = x_at * RING + pair_at * 2
    partner = x_at * RING + 3 - y_at
    beside = x_at * RING + y_at + 1 - 2 * lax.rem(y_at, 2)
    x_next = lax.rem(x_at + 1, RING)
    x_back = lax.rem(x_at + RING - 1, RING)
    x_far = lax.rem(x_at + 2, RING)
    ahead, behind = x_next * RING + y_at, x_back * RING + y_at
    NEAR, FAR, X_BESIDE, Y_BESIDE, Y_FAR = range(5)

    def chunk(c):
        return pl.ds(pl.multiple_of(c * chunk_rows, chunk_rows), chunk_rows)

    def rows_x(c, odd):
        return pl.ds(pl.multiple_of(c * chunk_rows, 16), x_rows[odd])

    def rows_y(c, odd):
        return pl.ds(pl.multiple_of(c * chunk_rows + x_rows[odd], 16), chunk_rows - x_rows[odd])

    def by_kind(stage, c):
        for odd in range(2):
            @pl.when(lax.rem(c, 2) == odd)
            def _(odd=odd):
                stage(c, odd)

    def send(start, count, here, stage, c, target):
        blocks = g_buf.at[pl.ds(start, count), here]
        to_mp(blocks, blocks, g_send.at[c], g_recv.at[c, stage], target).start()

    def arrived(count, here, stage, c):
        wait_for(g_buf.at[pl.ds(0, count), here], g_recv.at[c, stage])

    def to_neighbours(block, c):
        for target in (beside, ahead, behind):
            send(block, 1, chunk(c), NEAR, c, target)

    def stage_exchange(c, carry):
        theirs = (1 - half) * half_rows + c * chunk_rows
        to_mp(
            tok.at[pl.ds(pl.multiple_of(theirs, chunk_rows), chunk_rows)],
            g_buf.at[base + half, chunk(c)], g_send.at[c], e_recv.at[c], partner,
        ).start()
        to_neighbours(base + half, c)
        return carry

    def stage_partner(c):
        wait_for(g_buf.at[0, chunk(c)], e_recv.at[c])
        to_neighbours(base + 1 - half, c)

    def stage_near(c, odd):
        arrived(6, chunk(c), NEAR, c)
        send(x_back * RING + pair_at * 2, 1, chunk(c), FAR, c, ahead)
        send(x_next * RING + pair_at * 2 + 1, 1, chunk(c), FAR, c, behind)
        beside_pair = x_at * RING + 2 - pair_at * 2
        send(beside_pair, 2, rows_y(c, odd), Y_BESIDE, c, ahead)
        send(beside_pair, 2, rows_y(c, odd), Y_BESIDE, c, behind)
        send(x_back * RING + pair_at * 2, 2, rows_x(c, odd), X_BESIDE, c, beside)
        send(x_next * RING + pair_at * 2, 2, rows_x(c, odd), X_BESIDE, c, beside)

    def stage_far(c, odd):
        arrived(2, chunk(c), FAR, c)
        send(x_far * RING + pair_at * 2, 2, rows_x(c, odd), X_BESIDE, c, beside)
        arrived(4, rows_y(c, odd), Y_BESIDE, c)
        send(x_back * RING + 2 - pair_at * 2, 1, rows_y(c, odd), Y_FAR, c, ahead)
        send(x_next * RING + 3 - pair_at * 2, 1, rows_y(c, odd), Y_FAR, c, behind)

    def stage_last(c, odd):
        arrived(6, rows_x(c, odd), X_BESIDE, c)
        arrived(2, rows_y(c, odd), Y_FAR, c)

    core = lax.rem(d, 2)

    def piece(steps):
        return lax.rem(d + n_dp + 2 * steps, n_dp)

    quarter = n_dp // 4

    def pass_on(steps, part, target, sem):
        ref = w2.at[piece(steps), part]
        to_dp(ref, ref, w2_send, sem, target).start()

    def weights_start():
        lanes = pl.ds(pl.multiple_of(d * LANES, LANES), LANES)
        for part, ref in enumerate((wg, wu)):
            to_mp(ref.at[:, lanes], w2.at[d, part], w2_send, w2_first.at[part], partner).start()

    def weights_step(k, part):
        up, down = piece(1), piece(-1)
        if k == 0:
            wait_for(w2.at[0, 0], w2_first.at[part])
            pass_on(0, part, up, w2_up.at[0, part])
            pass_on(0, part, down, w2_down.at[0, part])
            pass_on(0, part, sibling, w2_side)
            return
        wait_for(w2.at[0, 0], w2_up.at[k - 1, part])
        wait_for(w2.at[0, 0], w2_down.at[k - 1, part])
        if k < quarter - 1 or part == 0:
            pass_on(-k, part, up, w2_up.at[k, part])
        if k < quarter - 1 or part == 1:
            pass_on(k, part, down, w2_down.at[k, part])
        pass_on(-k, part, sibling, w2_side)
        pass_on(k, part, sibling, w2_side)

    def weights_end(part):
        wait_for(w2.at[0, 0], (w2_up, w2_down)[part].at[quarter - 1, part])
        pass_on(quarter, part, sibling, w2_side)

    pool_of = lax.broadcasted_iota(jnp.int32, (pool_items, span), 1) // ITEM_TOK
    pool_row = lax.broadcasted_iota(jnp.int32, (pool_items, span), 0)
    pool = (pool_of == pool_row).astype(F32).astype(BF16)

    def ffn(k, gate_w, up_w, result):
        here = pl.ds(pl.multiple_of(k * span, span), span)
        wide = jnp.concatenate(
            [g_buf[j // RING * RING + SPOT[j % RING], here, :] for j in range(n_mp)], axis=1
        )
        gate = lax.dot_general(gate_w, wide, NT, preferred_element_type=F32)
        up = lax.dot_general(up_w, wide, NT, preferred_element_type=F32)
        hidden = (gate / (1.0 + jnp.exp(-gate)) * up).astype(BF16)
        there = pl.ds(pl.multiple_of(k * pool_items, pool_items), pool_items)
        result[there, :] = lax.dot_general(pool, hidden, NT, preferred_element_type=F32)

    def ffn_own(k):
        ffn(k, wg_v[...], wu_v[...], pooled)

    def ffn_partner(k):
        gate_w = jnp.concatenate([w2[j, 0] for j in range(n_mp)], axis=1)
        up_w = jnp.concatenate([w2[j, 1] for j in range(n_mp)], axis=1)
        ffn(k, gate_w, up_w, pooled2)

    def stage_down(h, source, order):
        here = pl.ds(pl.multiple_of(h * half_items, half_items), half_items)
        part = jnp.dot(source, wd_v[...], preferred_element_type=F32).astype(BF16)
        for j in range(n_mp):
            s1[j, here, :] = part[:, j * LANES : (j + 1) * LANES]
        r1[m, here, :] = s1[m, here, :]
        for k in range(1, n_mp):
            j = lax.rem(m + k, n_mp)
            to_mp(s1.at[j, here], r1.at[m, here], mp_send.at[0], r1_recv.at[order], j).start()

    def step(i, carry):
        @pl.when(i < CHUNKS - AHEAD)
        def _():
            stage_partner(i + AHEAD)

        @pl.when(i < CHUNKS)
        def _():
            by_kind(stage_near, i)

        @pl.when((i >= LAG) & (i < CHUNKS + LAG))
        def _():
            by_kind(stage_far, i - LAG)

        for k in range(quarter + 1):
            for part in range(2):
                @pl.when(i == RING_STEPS[2 * k + part])
                def _(k=k, part=part):
                    weights_step(k, part) if k < quarter else weights_end(part)

        @pl.when(i >= 2 * LAG)
        def _():
            by_kind(stage_last, i - 2 * LAG)

        @pl.when(i == 2)
        def _():
            for copy in copies[1:]:
                copy.wait()
            token_sum = jnp.dot(token_pool, tok_v[...], preferred_element_type=F32)
            tok_mean[...] = token_sum * (1.0 / ITEM_TOK)

        behind_by = CHUNKS + 2 * LAG - 1 - i

        @pl.when(behind_by == SPANS - 1)
        def _():
            wait_for(w2.at[pl.ds(0, n_dp // 2)], w2_side)

        @pl.when(behind_by < SPANS)
        def _():
            ffn_partner(SPANS - 1 - behind_by)

        @pl.when(behind_by == 0)
        def _():
            pooled_out[...] = (pooled2[...] * (1.0 / ITEM_TOK)).astype(BF16)
            to_mp(pooled_out, pooled_in, p_sem.at[0], p_sem.at[1], partner).start()

        @pl.when((i >= 2 * LAG) & (lax.rem(behind_by, CHUNKS // SPANS) == 0))
        def _():
            ffn_own(SPANS - 1 - behind_by // (CHUNKS // SPANS))

        return carry

    for k in range(1, n_mp):
        j = lax.rem(m + k, n_mp)
        to_mp(gains.at[m], gains.at[m], gs_sem.at[0], gs_sem.at[1], j).start()
    for k in range(1, n_dp):
        j = lax.rem(d + k, n_dp)
        to_dp(slots.at[d], slots.at[d], gs_sem.at[2], gs_sem.at[3], j).start()

    copies[0].wait()
    lax.fori_loop(0, CHUNKS // 4, stage_exchange, 0)
    weights_start()
    lax.fori_loop(CHUNKS // 4, CHUNKS, stage_exchange, 0)
    for c in range(AHEAD):
        stage_partner(c)
    lax.fori_loop(0, CHUNKS + 2 * LAG, step, 0)
    stage_down(half, (pooled[...] * (1.0 / ITEM_TOK)).astype(BF16), 0)
    wait_for(pooled_in, p_sem.at[1])
    stage_down(1 - half, pooled_in[...], 1)

    for i, (ref, count) in enumerate(((gains, n_mp), (gains, n_mp), (slots, n_dp), (slots, n_dp))):
        wait_for(ref.at[pl.ds(0, count - 1)], gs_sem.at[i])

    slot_row = jnp.concatenate([slots[k][:, :item_dev] for k in range(n_dp)], axis=1)
    last = (slot_row >= 0) & (jnp.bitwise_and(slot_row, positions - 1) == positions - 1)
    long_base = jnp.max(
        jnp.where(last, slot_row, positions - 1), axis=1, keepdims=True
    ) - (positions - 1)
    is_long = long_base == d * positions
    row = lax.broadcasted_iota(jnp.int32, (LANES, 1), 0)
    position = jnp.where(row < short, row, row - short + d * long_rows)
    row_slot = jnp.where(row < short, d * positions, long_base) + position
    row_slot = jnp.where(row < mine, row_slot, -2)
    holds = jnp.where(slot_row == row_slot[:mine], 1.0, 0.0).astype(BF16)
    long_row = lax.broadcasted_iota(jnp.int32, (positions, 1), 0)
    holds_long[...] = jnp.where(slot_row == long_base + long_row, 1.0, 0.0).astype(BF16)
    next_slot = jnp.where((position + 1 < positions) & (row < mine), row_slot + 1, -2)
    follows = jnp.where(slot_row == next_slot, 1.0, 0.0).astype(BF16)
    valid = jnp.sum(holds.astype(F32), axis=1, keepdims=True)
    has_target = lax.dot_general(
        jnp.ones((8, n_items), BF16), follows, NT, preferred_element_type=F32
    )
    item_id = lax.broadcasted_iota(jnp.int32, (n_items, chunk_items), 0)
    chunk_id = lax.broadcasted_iota(jnp.int32, (n_items, chunk_items), 1) + m * chunk_items
    to_chunk = jnp.where(item_id == chunk_id, 1.0, 0.0).astype(BF16)
    picks = jnp.dot(follows[:mine], to_chunk, preferred_element_type=F32)

    for h in range(2):
        wait_for(r1.at[pl.ds(0, n_mp - 1), pl.ds(0, half_items)], r1_recv.at[h])
    total = tok_mean[...]
    for j in range(n_mp):
        total = total + r1[j].astype(F32)
    embedding = total.astype(BF16)
    emb_out[...] = embedding

    def dp_block(k):
        return pl.ds(pl.multiple_of(k * item_dev, item_dev), item_dev)

    def share(ref, sem, arrivals):
        here = dp_block(d)
        for k in range(n_dp // 2):
            j = lax.rem(d + 2 * k, n_dp) if k else sibling
            to_dp(ref.at[here], ref.at[here], sem, arrivals.at[d], j).start()

    def pass_across(ref, sem, arrivals):
        for k in sorted(range(1, n_dp // 2), key=lambda k: min(k, n_dp // 2 - k)):
            j = lax.rem(d + n_dp - 2 * k, n_dp)
            wait_for(ref.at[dp_block(j)], arrivals.at[j])
            to_dp(ref.at[dp_block(j)], ref.at[dp_block(j)], sem, arrivals.at[j], sibling).start()
        for k in range(n_dp // 2):
            j = lax.rem(sibling + n_dp - 2 * k, n_dp)
            wait_for(ref.at[dp_block(j)], arrivals.at[j])

    x_buf[m] = embedding
    for k in range(1, n_mp):
        j = lax.rem(m + k, n_mp)
        to_mp(x_buf.at[m], x_buf.at[m], mp_send.at[1], mp_recv.at[1], j).start()
    items[dp_block(d), :] = embedding
    share(items, dp_send.at[0], item_recv)
    wait_for(x_buf.at[pl.ds(0, n_mp - 1)], mp_recv.at[1])

    states = [x_buf[j].astype(F32) for j in range(n_mp)]
    squares = states[0] * states[0]
    for block in states[1:]:
        squares = squares + block * block
    features = n_mp * LANES
    inverse = lax.rsqrt(jnp.sum(squares, axis=1, keepdims=True) / features + 1e-05)
    normed = jnp.concatenate(
        [(states[j] * inverse * gains[j]).astype(BF16) for j in range(n_mp)], axis=1
    )
    query = jnp.dot(normed, wq_v[...], preferred_element_type=F32) * HEAD_DIM ** (-0.5)
    key = jnp.dot(normed, wk_v[...], preferred_element_type=F32)
    value = jnp.dot(normed, wv_v[...], preferred_element_type=F32)
    item_lane = lax.broadcasted_iota(jnp.int32, (item_dev, LANES), 1)
    first_kv = (item_lane * 0 + lax.rem(m // 4, 2)) == 0
    key_part = jnp.where(first_kv, key, pltpu.roll(key, HEAD_DIM, axis=1))
    value_part = jnp.where(first_kv, pltpu.roll(value, HEAD_DIM, axis=1), value)
    pair = jnp.where(item_lane < HEAD_DIM, key_part, value_part)
    qkv[dp_block(d), :] = jnp.concatenate([query, pair], axis=1).astype(BF16)
    share(qkv, dp_send.at[1], qkv_recv)
    pass_across(items, dp_send.at[0], item_recv)

    placed = jnp.dot(holds, items[...], preferred_element_type=F32)

    def item_block(k):
        return pl.ds(pl.multiple_of(k * chunk_items, chunk_items), chunk_items)

    it_buf[m] = items[item_block(m), :]
    for k in range(1, n_mp):
        j = lax.rem(m + k, n_mp)
        to_mp(items.at[item_block(j)], it_buf.at[m], it_sem.at[0], it_sem.at[1], j).start()
    pass_across(qkv, dp_send.at[1], qkv_recv)

    own_rows = jnp.dot(holds, qkv[...], preferred_element_type=F32)
    long_pairs = jnp.dot(holds_long[...], qkv[:, LANES:], preferred_element_type=F32)
    long_here = pl.ds(pl.multiple_of(d * long_rows, long_rows), long_rows)
    cosine = jnp.concatenate([cos_t[0:short, :], cos_t[long_here, :]], axis=0)
    sine = jnp.concatenate([sin_t[0:short, :], sin_t[long_here, :]], axis=0)
    lane = lax.broadcasted_iota(jnp.int32, (mine, LANES), 1)
    left = lane < HEAD_DIM

    def rotate(v, cosine, sine):
        at = lax.rem(lax.broadcasted_iota(jnp.int32, v.shape, 1), HEAD_DIM)
        swapped = jnp.where(
            at < HEAD_DIM // 2,
            pltpu.roll(v, LANES - HEAD_DIM // 2, axis=1),
            pltpu.roll(v, HEAD_DIM // 2, axis=1),
        )
        return v * cosine + swapped * sine

    def rotate_key(v, rows):
        is_key = lax.broadcasted_iota(jnp.int32, v.shape, 1) < HEAD_DIM
        cosine = jnp.where(is_key, cos_t[:rows, :], 1.0)
        sine = jnp.where(is_key, sin_t[:rows, :], 0.0)
        return rotate(v, cosine, sine).astype(BF16)

    query = rotate(own_rows[:, :LANES], cosine, sine)
    short_pairs = rotate_key(own_rows[:short, LANES:], short)
    long_pairs = rotate_key(long_pairs, positions)

    head0 = jnp.where(left, query, 0.0).astype(BF16)
    head1 = jnp.where(left, pltpu.roll(query, HEAD_DIM, axis=1), 0.0).astype(BF16)

    def attend(q_rows, keys, first_position):
        count, n_keys = q_rows.shape[0], keys.shape[0]
        scores = lax.dot_general(q_rows, keys, NT, preferred_element_type=F32)
        at = lax.rem(lax.broadcasted_iota(jnp.int32, (count, n_keys), 0), count // 2)
        of = lax.broadcasted_iota(jnp.int32, (count, n_keys), 1)
        weights = jnp.where(of <= at + first_position, jnp.exp(scores), 0.0)
        weights = (weights / jnp.sum(weights, axis=1, keepdims=True)).astype(BF16)
        mixed = jnp.dot(weights, keys, preferred_element_type=F32)
        top, bottom = mixed[: count // 2], mixed[count // 2 :]
        at_left = lax.broadcasted_iota(jnp.int32, top.shape, 1) < HEAD_DIM
        return jnp.where(at_left, pltpu.roll(top, HEAD_DIM, axis=1), bottom).astype(BF16)

    short_rows = attend(
        jnp.concatenate([head0[:short], head1[:short]], axis=0), short_pairs, 0
    )
    rest = attend(
        jnp.concatenate([head0[short:], head1[short:]], axis=0), long_pairs, d * long_rows
    )
    attended = jnp.concatenate([short_rows, rest], axis=0)
    attn = jnp.dot(attended, wo_v[...], preferred_element_type=F32).astype(BF16)
    for j in range(n_mp):
        s5[j] = attn[:, j * LANES : (j + 1) * LANES]
    r5[m] = s5[m]
    for k in range(1, n_mp):
        j = lax.rem(m + k, n_mp)
        to_mp(s5.at[j], r5.at[m], mp_send.at[2], mp_recv.at[2], j).start()

    wait_for(it_buf.at[pl.ds(0, n_mp - 1)], it_sem.at[1])
    wide_items = [it_buf[j].astype(F32) for j in range(n_mp)]
    item_squares = wide_items[0] * wide_items[0]
    for block in wide_items[1:]:
        item_squares = item_squares + block * block
    item_scale = lax.rsqrt(jnp.sum(item_squares, axis=1, keepdims=True) + 1e-06)
    for j in range(n_mp):
        iu[:, j * LANES : (j + 1) * LANES] = (wide_items[j] * item_scale).astype(BF16)

    wait_for(r5.at[pl.ds(0, n_mp - 1)], mp_recv.at[2])
    combined = placed
    for j in range(n_mp):
        combined = combined + r5[j].astype(F32)
    combined = jnp.where(valid > 0.5, combined, 0.0).astype(BF16)
    u_buf[m] = combined
    for k in range(1, n_mp):
        j = lax.rem(m + k, n_mp)
        to_mp(u_buf.at[m], u_buf.at[m], mp_send.at[3], mp_recv.at[3], j).start()
    us_long[long_here, :] = combined[short:]
    for k in range(1, n_dp):
        j = lax.rem(d + k, n_dp)
        to_dp(
            us_long.at[long_here], us_long.at[long_here], dp_send.at[2], dp_recv.at[2], j
        ).start()

    wait_for(u_buf.at[pl.ds(0, n_mp - 1)], mp_recv.at[3])
    users = [u_buf[j] for j in range(n_mp)]
    user_squares = users[0].astype(F32) * users[0].astype(F32)
    for block in users[1:]:
        user_squares = user_squares + block.astype(F32) * block.astype(F32)
    user_scale = lax.rsqrt(jnp.sum(user_squares, axis=1, keepdims=True) + 1e-06)
    logits = lax.dot_general(
        jnp.concatenate(users, axis=1), iu[...], NT, preferred_element_type=F32
    ) * (SCALE * user_scale)
    stack = jnp.concatenate(
        [jnp.exp(logits), logits * picks, jnp.zeros((LANES - 2 * mine, chunk_items), F32)], axis=0
    )
    sums = lax.dot_general(
        jnp.ones((8, chunk_items), F32), stack, NT,
        precision=lax.Precision.HIGHEST, preferred_element_type=F32,
    )
    tp[m] = sums[0:1]
    for k in range(1, n_mp):
        j = lax.rem(m + k, n_mp)
        to_mp(tp.at[m], tp.at[m], mp_send.at[4], mp_recv.at[4], j).start()

    wait_for(us_long.at[pl.ds(0, (n_dp - 1) * long_rows)], dp_recv.at[2])
    short_states = jnp.concatenate(
        [combined[:short].astype(F32), jnp.zeros((positions - short, LANES), F32)], axis=0
    )
    us_out[...] = jnp.where(is_long, us_long[...].astype(F32), short_states).astype(BF16)

    wait_for(tp.at[pl.ds(0, n_mp - 1)], mp_recv.at[4])
    sums = tp[0]
    for j in range(1, n_mp):
        sums = sums + tp[j]
    sums = jnp.broadcast_to(sums, (8, LANES))
    counted = has_target > 0.5
    picked = pltpu.roll(sums, LANES - mine, axis=1)
    loss = jnp.where(counted, jnp.log(jnp.where(counted, sums, 1.0)) - picked, 0.0)
    at_lane = lax.broadcasted_iota(jnp.int32, (LANES, positions), 0)
    at_position = lax.broadcasted_iota(jnp.int32, (LANES, positions), 1)
    chosen = (at_lane >= short) & (at_lane < mine)
    chosen = chosen & (at_position == at_lane - short + d * long_rows)
    spread = jnp.dot(
        loss, jnp.where(chosen, 1.0, 0.0),
        precision=lax.Precision.HIGHEST, preferred_element_type=F32,
    )
    ll[d] = spread[0:1]
    for k in range(1, n_dp):
        j = lax.rem(d + k, n_dp)
        to_dp(ll.at[d], ll.at[d], dp_send.at[3], dp_recv.at[3], j).start()
    same = (at_lane < short) & (at_position == at_lane)
    short_loss = jnp.dot(
        loss, jnp.where(same, 1.0, 0.0),
        precision=lax.Precision.HIGHEST, preferred_element_type=F32,
    )[0:1]
    wait_for(ll.at[pl.ds(0, n_dp - 1)], dp_recv.at[3])
    long_loss = ll[0]
    for j in range(1, n_dp):
        long_loss = long_loss + ll[j]
    loss_out[...] = jnp.where(is_long, long_loss, short_loss)

    for c in range(CHUNKS):
        wait_for(g_buf.at[pl.ds(0, n_mp - 1), pl.ds(0, chunk_rows)], g_send.at[c])
    wait_for(w2, w2_send)
    wait_for(pooled_out, p_sem.at[0])
    wait_for(s1.at[pl.ds(0, n_mp - 1)], mp_send.at[0])
    wait_for(x_buf.at[pl.ds(0, n_mp - 1)], mp_send.at[1])
    wait_for(s5.at[pl.ds(0, n_mp - 1)], mp_send.at[2])
    wait_for(u_buf.at[pl.ds(0, n_mp - 1)], mp_send.at[3])
    wait_for(tp.at[pl.ds(0, n_mp - 1)], mp_send.at[4])
    wait_for(it_buf.at[pl.ds(0, n_mp - 1)], it_sem.at[0])
    wait_for(items.at[pl.ds(0, (n_dp - 1) * item_dev)], dp_send.at[0])
    wait_for(qkv.at[pl.ds(0, (n_dp - 1) * item_dev)], dp_send.at[1])
    wait_for(us_long.at[pl.ds(0, (n_dp - 1) * long_rows)], dp_send.at[2])
    wait_for(ll.at[pl.ds(0, n_dp - 1)], dp_send.at[3])


def solution(mesh, short=SHORT):
    n_dp, n_mp = mesh.shape["dp"], mesh.shape["mp"]

    def local(tok, wg, wu, wd, gain, wq, wk, wv, wo, item_slot, lengths, targets):
        rows, features = tok.shape[0], wg.shape[0]
        ff, item_dev, positions = wg.shape[1], item_slot.shape[0], targets.shape[0]
        n_items = n_dp * item_dev
        mine = short + positions // n_dp
        cos_table, sin_table = rope_tables(positions)
        any_spec = pl.BlockSpec(memory_space=pl.ANY)
        vmem = pl.BlockSpec(memory_space=pltpu.VMEM)
        dma = pltpu.SemaphoreType.DMA
        sizes = (n_dp, n_mp, rows, ff, item_dev, short, positions)
        embeddings, states, losses = pl.pallas_call(
            functools.partial(kernel, sizes),
            out_shape=(
                jax.ShapeDtypeStruct((item_dev, LANES), BF16),
                jax.ShapeDtypeStruct((positions, LANES), BF16),
                jax.ShapeDtypeStruct((1, positions), F32),
            ),
            in_specs=[any_spec] * 8 + [vmem] * 4,
            out_specs=(vmem, vmem, vmem),
            scratch_shapes=[
                pltpu.VMEM((n_mp, rows // 2, LANES), BF16),
                pltpu.VMEM((rows, LANES), BF16),
                pltpu.VMEM((n_dp, 2, ff, LANES), BF16),
                pltpu.VMEM((ff, features), BF16),
                pltpu.VMEM((ff, features), BF16),
                pltpu.VMEM((ff, features), BF16),
                pltpu.VMEM((features, LANES), BF16),
                pltpu.VMEM((features, LANES), BF16),
                pltpu.VMEM((features, LANES), BF16),
                pltpu.VMEM((LANES, features), BF16),
                pltpu.VMEM((item_dev // 2, ff), F32),
                pltpu.VMEM((item_dev // 2, ff), F32),
                pltpu.VMEM((item_dev // 2, ff), BF16),
                pltpu.VMEM((item_dev // 2, ff), BF16),
                pltpu.VMEM((item_dev, LANES), F32),
                pltpu.VMEM((n_mp, item_dev, LANES), BF16),
                pltpu.VMEM((n_mp, item_dev, LANES), BF16),
                pltpu.VMEM((n_items, LANES), BF16),
                pltpu.VMEM((n_mp, item_dev, LANES), BF16),
                pltpu.VMEM((n_mp, n_items // n_mp, LANES), BF16),
                pltpu.VMEM((n_items // n_mp, features), BF16),
                pltpu.VMEM((n_items, 2 * LANES), BF16),
                pltpu.VMEM((positions, n_items), BF16),
                pltpu.VMEM((n_mp, mine, LANES), BF16),
                pltpu.VMEM((n_mp, mine, LANES), BF16),
                pltpu.VMEM((positions, LANES), BF16),
                pltpu.VMEM((n_mp, mine, LANES), BF16),
                pltpu.VMEM((n_mp, 1, LANES), F32),
                pltpu.VMEM((n_dp, 1, LANES), jnp.int32),
                pltpu.VMEM((n_mp, 1, LANES), F32),
                pltpu.VMEM((n_dp, 1, positions), F32),
                dma((9,)),
                dma((CHUNKS,)),
                dma((CHUNKS,)),
                dma((CHUNKS, 5)),
                dma,
                dma((2,)),
                dma((n_dp // 4, 2)),
                dma((n_dp // 4, 2)),
                dma,
                dma((2,)),
                dma((5,)),
                dma((5,)),
                dma((2,)),
                dma((2,)),
                dma((4,)),
                dma((4,)),
                dma((n_dp,)),
                dma((n_dp,)),
                dma((4,)),
            ],
            compiler_params=pltpu.CompilerParams(
                collective_id=0, has_side_effects=True, vmem_limit_bytes=64 * 1024 * 1024 - 65536
            ),
        )(
            tok, wg.T, wu.T, wd, wq, wk, wv, wo,
            gain.reshape(1, LANES), item_slot.reshape(1, item_dev),
            jnp.asarray(cos_table), jnp.asarray(sin_table),
        )
        return embeddings, states, losses.reshape(positions)

    return jax.shard_map(
        local,
        mesh=mesh,
        in_specs=(
            P("dp", "mp"), P(None, "mp"), P(None, "mp"), P("mp", None), P("mp"),
            P(None, "mp"), P(), P(), P("mp", None), P("dp"), P("dp"), P("dp"),
        ),
        out_specs=(P("dp", "mp"), P("dp", "mp"), P("dp")),
        check_vma=False,
    )
```

```python
import functools

import jax
import jax.numpy as jnp
import numpy as np
from jax import lax
from jax.experimental import pallas as pl
from jax.experimental.pallas import tpu as pltpu
from jax.sharding import PartitionSpec as P

HEAD_DIM = 64
ITEM_TOK = 32
SCALE = 20.0
SHORT = 32
LANES = 128
RING = 4
SPOT = (0, 2, 3, 1)
CHUNKS = 8
LAG = 2
AHEAD = 2
SPANS = 4
RING_STEPS = (1, 1, 2, 3, 4, 4, 5, 6, 7, 7)
MESH = pl.DeviceIdType.MESH
BF16 = jnp.bfloat16
F32 = jnp.float32
NT = (((1,), (1,)), ((), ()))


def rope_tables(positions):
    half = HEAD_DIM // 2
    exponent = np.arange(half, dtype=np.float32) * np.float32(2.0 / HEAD_DIM)
    frequency = (10000.0 ** (-exponent.astype(np.float64))).astype(np.float32)
    angles = np.arange(positions, dtype=np.float32)[:, None] * frequency[None, :]
    angles = angles.astype(np.float64)
    cosine, sine = np.cos(angles), np.sin(angles)
    cos_table = np.concatenate([cosine, cosine, cosine, cosine], axis=1)
    sin_table = np.concatenate([-sine, sine, -sine, sine], axis=1)
    return cos_table.astype(np.float32), sin_table.astype(np.float32)


def kernel(
    sizes,
    tok, wg, wu, wd, wq, wk, wv, wo, gain, slot, cos_hbm, sin_hbm,
    emb_out, us_out, loss_out,
    g_buf, tok_v, w2, wg_v, wu_v, wd_v, wq_v, wk_v, wv_v, wo_v,
    pooled, pooled2, pooled_out, pooled_in, tok_mean, s1, r1, items, x_buf, it_buf, iu, qkv, holds_long, s5, r5, us_long, u_buf,
    gains, slots, tp, ll, gain_v, slot_v, cos_t, sin_t,
    w_sem, e_recv, g_send, g_recv, w2_send, w2_first, w2_up, w2_down, w2_side, p_sem,
    mp_send, mp_recv, r1_recv, it_sem, dp_send, dp_recv, item_recv, qkv_recv, gs_sem,
):
    n_dp, n_mp, rows, ff, item_dev, short, positions = sizes
    n_items = n_dp * item_dev
    long_rows = positions // n_dp
    mine = short + long_rows
    chunk_items = n_items // n_mp
    half_rows = rows // 2
    chunk_rows = half_rows // CHUNKS
    x_rows = (chunk_rows // 2, chunk_rows // 2 - 16)
    span = half_rows // SPANS
    pool_items = span // ITEM_TOK
    half_items = item_dev // 2
    d = lax.axis_index("dp")
    m = lax.axis_index("mp")
    sibling = d + 1 - 2 * lax.rem(d, 2)

    def to_mp(src, dst, send_sem, recv_sem, j):
        return pltpu.make_async_remote_copy(
            src_ref=src, dst_ref=dst, send_sem=send_sem, recv_sem=recv_sem,
            device_id={"mp": j}, device_id_type=MESH,
        )

    def to_dp(src, dst, send_sem, recv_sem, j):
        return pltpu.make_async_remote_copy(
            src_ref=src, dst_ref=dst, send_sem=send_sem, recv_sem=recv_sem,
            device_id={"dp": j}, device_id_type=MESH,
        )

    def hops(a, size):
        return min(a, size - a)

    apart = [(a, b) for a in range(RING) for b in range(RING) if a or b]
    apart.sort(key=lambda ab: -hops(ab[0], RING) - hops(ab[1], RING))
    mp_peers = [
        lax.rem(m // RING + a, RING) * RING + lax.rem(lax.rem(m, RING) + b, RING) for a, b in apart
    ]
    levels = n_dp // 2
    z_apart = sorted(range(1, levels), key=lambda k: -hops(k, levels))
    z_peers = [lax.rem(d + 2 * k, n_dp) for k in z_apart]
    dp_peers = z_peers + [j + 1 - 2 * lax.rem(j, 2) for j in z_peers] + [sibling]

    def wait_for(ref, sem):
        pltpu.make_async_copy(ref, ref, sem).wait()

    barrier = pltpu.get_barrier_semaphore()
    for j in mp_peers:
        pl.semaphore_signal(barrier, inc=1, device_id={"mp": j}, device_id_type=MESH)
    for j in dp_peers:
        pl.semaphore_signal(barrier, inc=1, device_id={"dp": j}, device_id_type=MESH)

    kv_block = pl.ds(pl.multiple_of((m // 8) * LANES, LANES), LANES)
    at_half = pl.ds(pl.multiple_of((lax.rem(m, RING) // 2) * half_rows, half_rows), half_rows)
    at_spot = m // RING * RING + lax.rem((lax.rem(m, RING) + 1) // 2, 2) * 2 + lax.rem(m, RING) // 2
    loads = [
        (tok.at[at_half], g_buf.at[at_spot]), (tok, tok_v), (wg, wg_v), (wu, wu_v), (wd, wd_v),
        (wq, wq_v), (wk.at[:, kv_block], wk_v), (wv.at[:, kv_block], wv_v), (wo, wo_v),
        (cos_hbm, cos_t), (sin_hbm, sin_t), (gain, gain_v), (slot, slot_v),
    ]
    copies = [pltpu.make_async_copy(a, b, w_sem.at[i]) for i, (a, b) in enumerate(loads)]
    for copy in copies:
        copy.start()
    token_of = lax.broadcasted_iota(jnp.int32, (item_dev, rows), 1) // ITEM_TOK
    token_row = lax.broadcasted_iota(jnp.int32, (item_dev, rows), 0)
    token_pool = (token_of == token_row).astype(F32).astype(BF16)
    pl.semaphore_wait(barrier, n_mp + n_dp - 2)
    copies[-2].wait()
    copies[-1].wait()
    gains[m] = gain_v[...]
    slots[d] = jnp.concatenate(
        [slot_v[...], jnp.full((1, LANES - item_dev), -1, jnp.int32)], axis=1
    )

    x_at, y_at = m // RING, lax.rem(m, RING)
    half = y_at // 2
    pair_at = lax.rem((y_at + 1) // 2, 2)
    base = x_at * RING + pair_at * 2
    partner = x_at * RING + 3 - y_at
    beside = x_at * RING + y_at + 1 - 2 * lax.rem(y_at, 2)
    x_next = lax.rem(x_at + 1, RING)
    x_back = lax.rem(x_at + RING - 1, RING)
    x_far = lax.rem(x_at + 2, RING)
    ahead, behind = x_next * RING + y_at, x_back * RING + y_at
    NEAR, FAR, X_BESIDE, Y_BESIDE, Y_FAR = range(5)

    def chunk(c):
        return pl.ds(pl.multiple_of(c * chunk_rows, chunk_rows), chunk_rows)

    def rows_x(c, odd):
        return pl.ds(pl.multiple_of(c * chunk_rows, 16), x_rows[odd])

    def rows_y(c, odd):
        return pl.ds(pl.multiple_of(c * chunk_rows + x_rows[odd], 16), chunk_rows - x_rows[odd])

    def by_kind(stage, c):
        for odd in range(2):
            @pl.when(lax.rem(c, 2) == odd)
            def _(odd=odd):
                stage(c, odd)

    def send(start, count, here, stage, c, target):
        blocks = g_buf.at[pl.ds(start, count), here]
        to_mp(blocks, blocks, g_send.at[c], g_recv.at[c, stage], target).start()

    def arrived(count, here, stage, c):
        wait_for(g_buf.at[pl.ds(0, count), here], g_recv.at[c, stage])

    def to_neighbours(block, c):
        for target in (beside, ahead, behind):
            send(block, 1, chunk(c), NEAR, c, target)

    def stage_exchange(c, carry):
        theirs = (1 - half) * half_rows + c * chunk_rows
        to_mp(
            tok.at[pl.ds(pl.multiple_of(theirs, chunk_rows), chunk_rows)],
            g_buf.at[base + half, chunk(c)], g_send.at[c], e_recv.at[c], partner,
        ).start()
        to_neighbours(base + half, c)
        return carry

    def stage_partner(c):
        wait_for(g_buf.at[0, chunk(c)], e_recv.at[c])
        to_neighbours(base + 1 - half, c)

    def stage_near(c, odd):
        arrived(6, chunk(c), NEAR, c)
        send(x_back * RING + pair_at * 2, 1, chunk(c), FAR, c, ahead)
        send(x_next * RING + pair_at * 2 + 1, 1, chunk(c), FAR, c, behind)
        beside_pair = x_at * RING + 2 - pair_at * 2
        send(beside_pair, 2, rows_y(c, odd), Y_BESIDE, c, ahead)
        send(beside_pair, 2, rows_y(c, odd), Y_BESIDE, c, behind)
        send(x_back * RING + pair_at * 2, 2, rows_x(c, odd), X_BESIDE, c, beside)
        send(x_next * RING + pair_at * 2, 2, rows_x(c, odd), X_BESIDE, c, beside)

    def stage_far(c, odd):
        arrived(2, chunk(c), FAR, c)
        send(x_far * RING + pair_at * 2, 2, rows_x(c, odd), X_BESIDE, c, beside)
        arrived(4, rows_y(c, odd), Y_BESIDE, c)
        send(x_back * RING + 2 - pair_at * 2, 1, rows_y(c, odd), Y_FAR, c, ahead)
        send(x_next * RING + 3 - pair_at * 2, 1, rows_y(c, odd), Y_FAR, c, behind)

    def stage_last(c, odd):
        arrived(6, rows_x(c, odd), X_BESIDE, c)
        arrived(2, rows_y(c, odd), Y_FAR, c)

    core = lax.rem(d, 2)

    def piece(steps):
        return lax.rem(d + n_dp + 2 * steps, n_dp)

    quarter = n_dp // 4

    def pass_on(steps, part, target, sem):
        ref = w2.at[piece(steps), part]
        to_dp(ref, ref, w2_send, sem, target).start()

    def weights_start():
        lanes = pl.ds(pl.multiple_of(d * LANES, LANES), LANES)
        for part, ref in enumerate((wg, wu)):
            to_mp(ref.at[:, lanes], w2.at[d, part], w2_send, w2_first.at[part], partner).start()

    def weights_step(k, part):
        up, down = piece(1), piece(-1)
        if k == 0:
            wait_for(w2.at[0, 0], w2_first.at[part])
            pass_on(0, part, up, w2_up.at[0, part])
            pass_on(0, part, down, w2_down.at[0, part])
            pass_on(0, part, sibling, w2_side)
            return
        wait_for(w2.at[0, 0], w2_up.at[k - 1, part])
        wait_for(w2.at[0, 0], w2_down.at[k - 1, part])
        if k < quarter - 1 or part == 0:
            pass_on(-k, part, up, w2_up.at[k, part])
        if k < quarter - 1 or part == 1:
            pass_on(k, part, down, w2_down.at[k, part])
        pass_on(-k, part, sibling, w2_side)
        pass_on(k, part, sibling, w2_side)

    def weights_end(part):
        wait_for(w2.at[0, 0], (w2_up, w2_down)[part].at[quarter - 1, part])
        pass_on(quarter, part, sibling, w2_side)

    pool_of = lax.broadcasted_iota(jnp.int32, (pool_items, span), 1) // ITEM_TOK
    pool_row = lax.broadcasted_iota(jnp.int32, (pool_items, span), 0)
    pool = (pool_of == pool_row).astype(F32).astype(BF16)

    def ffn(k, gate_w, up_w, result):
        here = pl.ds(pl.multiple_of(k * span, span), span)
        wide = jnp.concatenate(
            [g_buf[j // RING * RING + SPOT[j % RING], here, :] for j in range(n_mp)], axis=1
        )
        gate = lax.dot_general(gate_w, wide, NT, preferred_element_type=F32)
        up = lax.dot_general(up_w, wide, NT, preferred_element_type=F32)
        hidden = (gate / (1.0 + jnp.exp(-gate)) * up).astype(BF16)
        there = pl.ds(pl.multiple_of(k * pool_items, pool_items), pool_items)
        result[there, :] = lax.dot_general(pool, hidden, NT, preferred_element_type=F32)

    def ffn_own(k):
        ffn(k, wg_v[...], wu_v[...], pooled)

    def ffn_partner(k):
        gate_w = jnp.concatenate([w2[j, 0] for j in range(n_mp)], axis=1)
        up_w = jnp.concatenate([w2[j, 1] for j in range(n_mp)], axis=1)
        ffn(k, gate_w, up_w, pooled2)

    def stage_down(h, source, order):
        here = pl.ds(pl.multiple_of(h * half_items, half_items), half_items)
        part = jnp.dot(source, wd_v[...], preferred_element_type=F32).astype(BF16)
        for j in range(n_mp):
            s1[j, here, :] = part[:, j * LANES : (j + 1) * LANES]
        r1[m, here, :] = s1[m, here, :]
        for j in mp_peers:
            to_mp(s1.at[j, here], r1.at[m, here], mp_send.at[0], r1_recv.at[order], j).start()

    def step(i, carry):
        @pl.when(i < CHUNKS - AHEAD)
        def _():
            stage_partner(i + AHEAD)

        @pl.when(i < CHUNKS)
        def _():
            by_kind(stage_near, i)

        @pl.when((i >= LAG) & (i < CHUNKS + LAG))
        def _():
            by_kind(stage_far, i - LAG)

        for k in range(quarter + 1):
            for part in range(2):
                @pl.when(i == RING_STEPS[2 * k + part])
                def _(k=k, part=part):
                    weights_step(k, part) if k < quarter else weights_end(part)

        @pl.when(i >= 2 * LAG)
        def _():
            by_kind(stage_last, i - 2 * LAG)

        @pl.when(i == 2)
        def _():
            for copy in copies[1:-2]:
                copy.wait()
            token_sum = jnp.dot(token_pool, tok_v[...], preferred_element_type=F32)
            tok_mean[...] = token_sum * (1.0 / ITEM_TOK)

        behind_by = CHUNKS + 2 * LAG - 1 - i

        @pl.when(behind_by == SPANS - 1)
        def _():
            wait_for(w2.at[pl.ds(0, n_dp // 2)], w2_side)

        @pl.when(behind_by < SPANS)
        def _():
            ffn_partner(SPANS - 1 - behind_by)

        @pl.when(behind_by == 0)
        def _():
            pooled_out[...] = (pooled2[...] * (1.0 / ITEM_TOK)).astype(BF16)
            to_mp(pooled_out, pooled_in, p_sem.at[0], p_sem.at[1], partner).start()

        @pl.when((i >= 2 * LAG) & (lax.rem(behind_by, CHUNKS // SPANS) == 0))
        def _():
            ffn_own(SPANS - 1 - behind_by // (CHUNKS // SPANS))

        return carry

    for j in mp_peers:
        to_mp(gains.at[m], gains.at[m], gs_sem.at[0], gs_sem.at[1], j).start()
    for j in dp_peers:
        to_dp(slots.at[d], slots.at[d], gs_sem.at[2], gs_sem.at[3], j).start()

    copies[0].wait()
    lax.fori_loop(0, CHUNKS // 2, stage_exchange, 0)
    weights_start()
    lax.fori_loop(CHUNKS // 2, CHUNKS, stage_exchange, 0)
    for c in range(AHEAD):
        stage_partner(c)
    lax.fori_loop(0, CHUNKS + 2 * LAG, step, 0)
    stage_down(half, (pooled[...] * (1.0 / ITEM_TOK)).astype(BF16), 0)
    wait_for(pooled_in, p_sem.at[1])
    stage_down(1 - half, pooled_in[...], 1)

    for i, (ref, count) in enumerate(((gains, n_mp), (gains, n_mp), (slots, n_dp), (slots, n_dp))):
        wait_for(ref.at[pl.ds(0, count - 1)], gs_sem.at[i])

    slot_row = jnp.concatenate([slots[k][:, :item_dev] for k in range(n_dp)], axis=1)
    last = (slot_row >= 0) & (jnp.bitwise_and(slot_row, positions - 1) == positions - 1)
    long_base = jnp.max(
        jnp.where(last, slot_row, positions - 1), axis=1, keepdims=True
    ) - (positions - 1)
    is_long = long_base == d * positions
    row = lax.broadcasted_iota(jnp.int32, (LANES, 1), 0)
    position = jnp.where(row < short, row, row - short + d * long_rows)
    row_slot = jnp.where(row < short, d * positions, long_base) + position
    row_slot = jnp.where(row < mine, row_slot, -2)
    holds = jnp.where(slot_row == row_slot[:mine], 1.0, 0.0).astype(BF16)
    long_row = lax.broadcasted_iota(jnp.int32, (positions, 1), 0)
    holds_long[...] = jnp.where(slot_row == long_base + long_row, 1.0, 0.0).astype(BF16)
    next_slot = jnp.where((position + 1 < positions) & (row < mine), row_slot + 1, -2)
    follows = jnp.where(slot_row == next_slot, 1.0, 0.0).astype(BF16)
    valid = jnp.sum(holds.astype(F32), axis=1, keepdims=True)
    has_target = lax.dot_general(
        jnp.ones((8, n_items), BF16), follows, NT, preferred_element_type=F32
    )
    item_id = lax.broadcasted_iota(jnp.int32, (n_items, chunk_items), 0)
    chunk_id = lax.broadcasted_iota(jnp.int32, (n_items, chunk_items), 1) + m * chunk_items
    to_chunk = jnp.where(item_id == chunk_id, 1.0, 0.0).astype(BF16)
    picks = jnp.dot(follows[:mine], to_chunk, preferred_element_type=F32)

    for h in range(2):
        wait_for(r1.at[pl.ds(0, n_mp - 1), pl.ds(0, half_items)], r1_recv.at[h])
    total = tok_mean[...]
    for j in range(n_mp):
        total = total + r1[j].astype(F32)
    embedding = total.astype(BF16)
    emb_out[...] = embedding

    def dp_block(k):
        return pl.ds(pl.multiple_of(k * item_dev, item_dev), item_dev)

    def share(ref, sem, arrivals):
        here = dp_block(d)
        for j in z_peers + [sibling]:
            to_dp(ref.at[here], ref.at[here], sem, arrivals.at[d], j).start()

    def pass_across(ref, sem, arrivals):
        for k in sorted(range(1, n_dp // 2), key=lambda k: min(k, n_dp // 2 - k)):
            j = lax.rem(d + n_dp - 2 * k, n_dp)
            wait_for(ref.at[dp_block(j)], arrivals.at[j])
            to_dp(ref.at[dp_block(j)], ref.at[dp_block(j)], sem, arrivals.at[j], sibling).start()
        for k in range(n_dp // 2):
            j = lax.rem(sibling + n_dp - 2 * k, n_dp)
            wait_for(ref.at[dp_block(j)], arrivals.at[j])

    x_buf[m] = embedding
    for j in mp_peers:
        to_mp(x_buf.at[m], x_buf.at[m], mp_send.at[1], mp_recv.at[1], j).start()
    items[dp_block(d), :] = embedding
    share(items, dp_send.at[0], item_recv)
    wait_for(x_buf.at[pl.ds(0, n_mp - 1)], mp_recv.at[1])

    states = [x_buf[j].astype(F32) for j in range(n_mp)]
    squares = states[0] * states[0]
    for block in states[1:]:
        squares = squares + block * block
    features = n_mp * LANES
    inverse = lax.rsqrt(jnp.sum(squares, axis=1, keepdims=True) / features + 1e-05)
    normed = jnp.concatenate(
        [(states[j] * inverse * gains[j]).astype(BF16) for j in range(n_mp)], axis=1
    )
    query = jnp.dot(normed, wq_v[...], preferred_element_type=F32) * HEAD_DIM ** (-0.5)
    key = jnp.dot(normed, wk_v[...], preferred_element_type=F32)
    value = jnp.dot(normed, wv_v[...], preferred_element_type=F32)
    item_lane = lax.broadcasted_iota(jnp.int32, (item_dev, LANES), 1)
    first_kv = (item_lane * 0 + lax.rem(m // 4, 2)) == 0
    key_part = jnp.where(first_kv, key, pltpu.roll(key, HEAD_DIM, axis=1))
    value_part = jnp.where(first_kv, pltpu.roll(value, HEAD_DIM, axis=1), value)
    pair = jnp.where(item_lane < HEAD_DIM, key_part, value_part)
    qkv[dp_block(d), :] = jnp.concatenate([query, pair], axis=1).astype(BF16)
    share(qkv, dp_send.at[1], qkv_recv)
    pass_across(items, dp_send.at[0], item_recv)

    placed = jnp.dot(holds, items[...], preferred_element_type=F32)

    def item_block(k):
        return pl.ds(pl.multiple_of(k * chunk_items, chunk_items), chunk_items)

    it_buf[m] = items[item_block(m), :]
    for j in mp_peers:
        to_mp(items.at[item_block(j)], it_buf.at[m], it_sem.at[0], it_sem.at[1], j).start()
    pass_across(qkv, dp_send.at[1], qkv_recv)

    own_rows = jnp.dot(holds, qkv[...], preferred_element_type=F32)
    long_pairs = jnp.dot(holds_long[...], qkv[:, LANES:], preferred_element_type=F32)
    long_here = pl.ds(pl.multiple_of(d * long_rows, long_rows), long_rows)
    cosine = jnp.concatenate([cos_t[0:short, :], cos_t[long_here, :]], axis=0)
    sine = jnp.concatenate([sin_t[0:short, :], sin_t[long_here, :]], axis=0)
    lane = lax.broadcasted_iota(jnp.int32, (mine, LANES), 1)
    left = lane < HEAD_DIM

    def rotate(v, cosine, sine):
        at = lax.rem(lax.broadcasted_iota(jnp.int32, v.shape, 1), HEAD_DIM)
        swapped = jnp.where(
            at < HEAD_DIM // 2,
            pltpu.roll(v, LANES - HEAD_DIM // 2, axis=1),
            pltpu.roll(v, HEAD_DIM // 2, axis=1),
        )
        return v * cosine + swapped * sine

    def rotate_key(v, rows):
        is_key = lax.broadcasted_iota(jnp.int32, v.shape, 1) < HEAD_DIM
        cosine = jnp.where(is_key, cos_t[:rows, :], 1.0)
        sine = jnp.where(is_key, sin_t[:rows, :], 0.0)
        return rotate(v, cosine, sine).astype(BF16)

    query = rotate(own_rows[:, :LANES], cosine, sine)
    short_pairs = rotate_key(own_rows[:short, LANES:], short)
    long_pairs = rotate_key(long_pairs, positions)

    head0 = jnp.where(left, query, 0.0).astype(BF16)
    head1 = jnp.where(left, pltpu.roll(query, HEAD_DIM, axis=1), 0.0).astype(BF16)

    def attend(q_rows, keys, first_position):
        count, n_keys = q_rows.shape[0], keys.shape[0]
        scores = lax.dot_general(q_rows, keys, NT, preferred_element_type=F32)
        at = lax.rem(lax.broadcasted_iota(jnp.int32, (count, n_keys), 0), count // 2)
        of = lax.broadcasted_iota(jnp.int32, (count, n_keys), 1)
        weights = jnp.where(of <= at + first_position, jnp.exp(scores), 0.0)
        weights = (weights / jnp.sum(weights, axis=1, keepdims=True)).astype(BF16)
        mixed = jnp.dot(weights, keys, preferred_element_type=F32)
        top, bottom = mixed[: count // 2], mixed[count // 2 :]
        at_left = lax.broadcasted_iota(jnp.int32, top.shape, 1) < HEAD_DIM
        return jnp.where(at_left, pltpu.roll(top, HEAD_DIM, axis=1), bottom).astype(BF16)

    short_rows = attend(
        jnp.concatenate([head0[:short], head1[:short]], axis=0), short_pairs, 0
    )
    rest = attend(
        jnp.concatenate([head0[short:], head1[short:]], axis=0), long_pairs, d * long_rows
    )
    attended = jnp.concatenate([short_rows, rest], axis=0)
    attn = jnp.dot(attended, wo_v[...], preferred_element_type=F32).astype(BF16)
    for j in range(n_mp):
        s5[j] = attn[:, j * LANES : (j + 1) * LANES]
    r5[m] = s5[m]
    for j in mp_peers:
        to_mp(s5.at[j], r5.at[m], mp_send.at[2], mp_recv.at[2], j).start()

    wait_for(it_buf.at[pl.ds(0, n_mp - 1)], it_sem.at[1])
    wide_items = [it_buf[j].astype(F32) for j in range(n_mp)]
    item_squares = wide_items[0] * wide_items[0]
    for block in wide_items[1:]:
        item_squares = item_squares + block * block
    item_scale = lax.rsqrt(jnp.sum(item_squares, axis=1, keepdims=True) + 1e-06)
    for j in range(n_mp):
        iu[:, j * LANES : (j + 1) * LANES] = (wide_items[j] * item_scale).astype(BF16)

    wait_for(r5.at[pl.ds(0, n_mp - 1)], mp_recv.at[2])
    combined = placed
    for j in range(n_mp):
        combined = combined + r5[j].astype(F32)
    combined = jnp.where(valid > 0.5, combined, 0.0).astype(BF16)
    u_buf[m] = combined
    for j in mp_peers:
        to_mp(u_buf.at[m], u_buf.at[m], mp_send.at[3], mp_recv.at[3], j).start()
    us_long[long_here, :] = combined[short:]
    for j in dp_peers:
        to_dp(
            us_long.at[long_here], us_long.at[long_here], dp_send.at[2], dp_recv.at[2], j
        ).start()

    wait_for(u_buf.at[pl.ds(0, n_mp - 1)], mp_recv.at[3])
    users = [u_buf[j] for j in range(n_mp)]
    user_squares = users[0].astype(F32) * users[0].astype(F32)
    for block in users[1:]:
        user_squares = user_squares + block.astype(F32) * block.astype(F32)
    user_scale = lax.rsqrt(jnp.sum(user_squares, axis=1, keepdims=True) + 1e-06)
    logits = lax.dot_general(
        jnp.concatenate(users, axis=1), iu[...], NT, preferred_element_type=F32
    ) * (SCALE * user_scale)
    stack = jnp.concatenate(
        [jnp.exp(logits), logits * picks, jnp.zeros((LANES - 2 * mine, chunk_items), F32)], axis=0
    )
    sums = lax.dot_general(
        jnp.ones((8, chunk_items), F32), stack, NT,
        precision=lax.Precision.HIGHEST, preferred_element_type=F32,
    )
    tp[m] = sums[0:1]
    for j in mp_peers:
        to_mp(tp.at[m], tp.at[m], mp_send.at[4], mp_recv.at[4], j).start()

    wait_for(us_long.at[pl.ds(0, (n_dp - 1) * long_rows)], dp_recv.at[2])
    short_states = jnp.concatenate(
        [combined[:short].astype(F32), jnp.zeros((positions - short, LANES), F32)], axis=0
    )
    us_out[...] = jnp.where(is_long, us_long[...].astype(F32), short_states).astype(BF16)

    wait_for(tp.at[pl.ds(0, n_mp - 1)], mp_recv.at[4])
    sums = tp[0]
    for j in range(1, n_mp):
        sums = sums + tp[j]
    sums = jnp.broadcast_to(sums, (8, LANES))
    counted = has_target > 0.5
    picked = pltpu.roll(sums, LANES - mine, axis=1)
    loss = jnp.where(counted, jnp.log(jnp.where(counted, sums, 1.0)) - picked, 0.0)
    at_lane = lax.broadcasted_iota(jnp.int32, (LANES, positions), 0)
    at_position = lax.broadcasted_iota(jnp.int32, (LANES, positions), 1)
    chosen = (at_lane >= short) & (at_lane < mine)
    chosen = chosen & (at_position == at_lane - short + d * long_rows)
    spread = jnp.dot(
        loss, jnp.where(chosen, 1.0, 0.0),
        precision=lax.Precision.HIGHEST, preferred_element_type=F32,
    )
    ll[d] = spread[0:1]
    for j in dp_peers:
        to_dp(ll.at[d], ll.at[d], dp_send.at[3], dp_recv.at[3], j).start()
    same = (at_lane < short) & (at_position == at_lane)
    short_loss = jnp.dot(
        loss, jnp.where(same, 1.0, 0.0),
        precision=lax.Precision.HIGHEST, preferred_element_type=F32,
    )[0:1]
    wait_for(ll.at[pl.ds(0, n_dp - 1)], dp_recv.at[3])
    long_loss = ll[0]
    for j in range(1, n_dp):
        long_loss = long_loss + ll[j]
    loss_out[...] = jnp.where(is_long, long_loss, short_loss)

    for c in range(CHUNKS):
        wait_for(g_buf.at[pl.ds(0, n_mp - 1), pl.ds(0, chunk_rows)], g_send.at[c])
    wait_for(w2, w2_send)
    wait_for(pooled_out, p_sem.at[0])
    wait_for(s1.at[pl.ds(0, n_mp - 1)], mp_send.at[0])
    wait_for(x_buf.at[pl.ds(0, n_mp - 1)], mp_send.at[1])
    wait_for(s5.at[pl.ds(0, n_mp - 1)], mp_send.at[2])
    wait_for(u_buf.at[pl.ds(0, n_mp - 1)], mp_send.at[3])
    wait_for(tp.at[pl.ds(0, n_mp - 1)], mp_send.at[4])
    wait_for(it_buf.at[pl.ds(0, n_mp - 1)], it_sem.at[0])
    wait_for(items.at[pl.ds(0, (n_dp - 1) * item_dev)], dp_send.at[0])
    wait_for(qkv.at[pl.ds(0, (n_dp - 1) * item_dev)], dp_send.at[1])
    wait_for(us_long.at[pl.ds(0, (n_dp - 1) * long_rows)], dp_send.at[2])
    wait_for(ll.at[pl.ds(0, n_dp - 1)], dp_send.at[3])


def solution(mesh, short=SHORT):
    n_dp, n_mp = mesh.shape["dp"], mesh.shape["mp"]

    def local(tok, wg, wu, wd, gain, wq, wk, wv, wo, item_slot, lengths, targets):
        rows, features = tok.shape[0], wg.shape[0]
        ff, item_dev, positions = wg.shape[1], item_slot.shape[0], targets.shape[0]
        n_items = n_dp * item_dev
        mine = short + positions // n_dp
        cos_table, sin_table = rope_tables(positions)
        hbm = pl.BlockSpec(memory_space=pltpu.HBM)
        vmem = pl.BlockSpec(memory_space=pltpu.VMEM)
        dma = pltpu.SemaphoreType.DMA
        sizes = (n_dp, n_mp, rows, ff, item_dev, short, positions)
        embeddings, states, losses = pl.pallas_call(
            functools.partial(kernel, sizes),
            out_shape=(
                jax.ShapeDtypeStruct((item_dev, LANES), BF16),
                jax.ShapeDtypeStruct((positions, LANES), BF16),
                jax.ShapeDtypeStruct((1, positions), F32),
            ),
            in_specs=[hbm] * 12,
            out_specs=(vmem, vmem, vmem),
            scratch_shapes=[
                pltpu.VMEM((n_mp, rows // 2, LANES), BF16),
                pltpu.VMEM((rows, LANES), BF16),
                pltpu.VMEM((n_dp, 2, ff, LANES), BF16),
                pltpu.VMEM((ff, features), BF16),
                pltpu.VMEM((ff, features), BF16),
                pltpu.VMEM((ff, features), BF16),
                pltpu.VMEM((features, LANES), BF16),
                pltpu.VMEM((features, LANES), BF16),
                pltpu.VMEM((features, LANES), BF16),
                pltpu.VMEM((LANES, features), BF16),
                pltpu.VMEM((item_dev // 2, ff), F32),
                pltpu.VMEM((item_dev // 2, ff), F32),
                pltpu.VMEM((item_dev // 2, ff), BF16),
                pltpu.VMEM((item_dev // 2, ff), BF16),
                pltpu.VMEM((item_dev, LANES), F32),
                pltpu.VMEM((n_mp, item_dev, LANES), BF16),
                pltpu.VMEM((n_mp, item_dev, LANES), BF16),
                pltpu.VMEM((n_items, LANES), BF16),
                pltpu.VMEM((n_mp, item_dev, LANES), BF16),
                pltpu.VMEM((n_mp, n_items // n_mp, LANES), BF16),
                pltpu.VMEM((n_items // n_mp, features), BF16),
                pltpu.VMEM((n_items, 2 * LANES), BF16),
                pltpu.VMEM((positions, n_items), BF16),
                pltpu.VMEM((n_mp, mine, LANES), BF16),
                pltpu.VMEM((n_mp, mine, LANES), BF16),
                pltpu.VMEM((positions, LANES), BF16),
                pltpu.VMEM((n_mp, mine, LANES), BF16),
                pltpu.VMEM((n_mp, 1, LANES), F32),
                pltpu.VMEM((n_dp, 1, LANES), jnp.int32),
                pltpu.VMEM((n_mp, 1, LANES), F32),
                pltpu.VMEM((n_dp, 1, positions), F32),
                pltpu.VMEM((1, LANES), F32),
                pltpu.VMEM((1, item_dev), jnp.int32),
                pltpu.VMEM((positions, LANES), F32),
                pltpu.VMEM((positions, LANES), F32),
                dma((13,)),
                dma((CHUNKS,)),
                dma((CHUNKS,)),
                dma((CHUNKS, 5)),
                dma,
                dma((2,)),
                dma((n_dp // 4, 2)),
                dma((n_dp // 4, 2)),
                dma,
                dma((2,)),
                dma((5,)),
                dma((5,)),
                dma((2,)),
                dma((2,)),
                dma((4,)),
                dma((4,)),
                dma((n_dp,)),
                dma((n_dp,)),
                dma((4,)),
            ],
            compiler_params=pltpu.CompilerParams(
                collective_id=0, has_side_effects=True, vmem_limit_bytes=(64 * 1024 - 64) * 1024
            ),
        )(
            tok, wg.T, wu.T, wd, wq, wk, wv, wo,
            gain.reshape(1, LANES), item_slot.reshape(1, item_dev),
            jnp.asarray(cos_table), jnp.asarray(sin_table),
        )
        return embeddings, states, losses.reshape(positions)

    return jax.shard_map(
        local,
        mesh=mesh,
        in_specs=(
            P("dp", "mp"), P(None, "mp"), P(None, "mp"), P("mp", None), P("mp"),
            P(None, "mp"), P(), P(), P("mp", None), P("dp"), P("dp"), P("dp"),
        ),
        out_specs=(P("dp", "mp"), P("dp", "mp"), P("dp")),
        check_vma=False,
    )
```

```python
import functools

import jax
import jax.numpy as jnp
import numpy as np
from jax import lax
from jax.experimental import pallas as pl
from jax.experimental.pallas import tpu as pltpu
from jax.sharding import PartitionSpec as P

HEAD_DIM = 64
ITEM_TOK = 32
SCALE = 20.0
SHORT = 32
LANES = 128
RING = 4
SPOT = (0, 2, 3, 1)
CHUNKS = 8
LAG = 2
AHEAD = 2
SPANS = 4
RING_STEPS = (1, 1, 2, 3, 4, 4, 5, 6, 7, 7)
MESH = pl.DeviceIdType.MESH
BF16 = jnp.bfloat16
F32 = jnp.float32
NT = (((1,), (1,)), ((), ()))


def rope_tables(positions):
    half = HEAD_DIM // 2
    exponent = np.arange(half, dtype=np.float32) * np.float32(2.0 / HEAD_DIM)
    frequency = (10000.0 ** (-exponent.astype(np.float64))).astype(np.float32)
    angles = np.arange(positions, dtype=np.float32)[:, None] * frequency[None, :]
    angles = angles.astype(np.float64)
    cosine, sine = np.cos(angles), np.sin(angles)
    cos_table = np.concatenate([cosine, cosine, cosine, cosine], axis=1)
    sin_table = np.concatenate([-sine, sine, -sine, sine], axis=1)
    return cos_table.astype(np.float32), sin_table.astype(np.float32)


def kernel(
    sizes,
    tok, wg, wu, wd, wq, wk, wv, wo, gain, slot, cos_hbm, sin_hbm,
    emb_out, us_out, loss_out,
    g_buf, tok_v, w2, wg_v, wu_v, wd_v, wq_v, wk_v, wv_v, wo_v,
    pooled, pooled2, pooled_out, pooled_in, tok_mean, s1, r1, items, x_buf, it_buf, iu, qkv, holds_long, s5, r5, us_long, u_buf,
    gains, slots, tp, ll, gain_v, slot_v, cos_t, sin_t,
    w_sem, e_recv, g_send, g_recv, w2_send, w2_first, w2_up, w2_down, w2_side, p_sem,
    mp_send, mp_recv, r1_recv, it_sem, dp_send, dp_recv, item_recv, qkv_recv, gs_sem,
):
    n_dp, n_mp, rows, ff, item_dev, short, positions = sizes
    n_items = n_dp * item_dev
    long_rows = positions // n_dp
    mine = short + long_rows
    chunk_items = n_items // n_mp
    half_rows = rows // 2
    chunk_rows = half_rows // CHUNKS
    x_rows = (chunk_rows // 2, chunk_rows // 2 - 16)
    span = half_rows // SPANS
    pool_items = span // ITEM_TOK
    half_items = item_dev // 2
    d = lax.axis_index("dp")
    m = lax.axis_index("mp")
    sibling = d + 1 - 2 * lax.rem(d, 2)

    def to_mp(src, dst, send_sem, recv_sem, j):
        return pltpu.make_async_remote_copy(
            src_ref=src, dst_ref=dst, send_sem=send_sem, recv_sem=recv_sem,
            device_id={"mp": j}, device_id_type=MESH,
        )

    def to_dp(src, dst, send_sem, recv_sem, j):
        return pltpu.make_async_remote_copy(
            src_ref=src, dst_ref=dst, send_sem=send_sem, recv_sem=recv_sem,
            device_id={"dp": j}, device_id_type=MESH,
        )

    def hops(a, size):
        return min(a, size - a)

    apart = [(a, b) for a in range(RING) for b in range(RING) if a or b]
    apart.sort(key=lambda ab: -hops(ab[0], RING) - hops(ab[1], RING))
    mp_peers = [
        lax.rem(m // RING + a, RING) * RING + lax.rem(lax.rem(m, RING) + b, RING) for a, b in apart
    ]
    levels = n_dp // 2
    z_apart = sorted(range(1, levels), key=lambda k: -hops(k, levels))
    z_peers = [lax.rem(d + 2 * k, n_dp) for k in z_apart]
    dp_peers = z_peers + [j + 1 - 2 * lax.rem(j, 2) for j in z_peers] + [sibling]

    def wait_for(ref, sem):
        pltpu.make_async_copy(ref, ref, sem).wait()

    barrier = pltpu.get_barrier_semaphore()
    for j in mp_peers:
        pl.semaphore_signal(barrier, inc=1, device_id={"mp": j}, device_id_type=MESH)
    for j in dp_peers:
        pl.semaphore_signal(barrier, inc=1, device_id={"dp": j}, device_id_type=MESH)

    kv_block = pl.ds(pl.multiple_of((m // 8) * LANES, LANES), LANES)
    at_half = pl.ds(pl.multiple_of((lax.rem(m, RING) // 2) * half_rows, half_rows), half_rows)
    at_spot = m // RING * RING + lax.rem((lax.rem(m, RING) + 1) // 2, 2) * 2 + lax.rem(m, RING) // 2
    loads = [
        (tok.at[at_half], g_buf.at[at_spot]), (tok, tok_v), (wg, wg_v), (wu, wu_v), (wd, wd_v),
        (wq, wq_v), (wk.at[:, kv_block], wk_v), (wv.at[:, kv_block], wv_v), (wo, wo_v),
        (cos_hbm, cos_t), (sin_hbm, sin_t), (gain, gain_v), (slot, slot_v),
    ]
    copies = [pltpu.make_async_copy(a, b, w_sem.at[i]) for i, (a, b) in enumerate(loads)]
    for copy in copies:
        copy.start()
    token_of = lax.broadcasted_iota(jnp.int32, (item_dev, rows), 1) // ITEM_TOK
    token_row = lax.broadcasted_iota(jnp.int32, (item_dev, rows), 0)
    token_pool = (token_of == token_row).astype(F32).astype(BF16)
    pl.semaphore_wait(barrier, n_mp + n_dp - 2)
    copies[-2].wait()
    copies[-1].wait()
    gains[m] = gain_v[...]
    slots[d] = jnp.concatenate(
        [slot_v[...], jnp.full((1, LANES - item_dev), -1, jnp.int32)], axis=1
    )

    x_at, y_at = m // RING, lax.rem(m, RING)
    half = y_at // 2
    pair_at = lax.rem((y_at + 1) // 2, 2)
    base = x_at * RING + pair_at * 2
    partner = x_at * RING + 3 - y_at
    beside = x_at * RING + y_at + 1 - 2 * lax.rem(y_at, 2)
    x_next = lax.rem(x_at + 1, RING)
    x_back = lax.rem(x_at + RING - 1, RING)
    x_far = lax.rem(x_at + 2, RING)
    ahead, behind = x_next * RING + y_at, x_back * RING + y_at
    NEAR, FAR, X_BESIDE, Y_BESIDE, Y_FAR = range(5)

    def chunk(c):
        return pl.ds(pl.multiple_of(c * chunk_rows, chunk_rows), chunk_rows)

    def rows_x(c, odd):
        return pl.ds(pl.multiple_of(c * chunk_rows, 16), x_rows[odd])

    def rows_y(c, odd):
        return pl.ds(pl.multiple_of(c * chunk_rows + x_rows[odd], 16), chunk_rows - x_rows[odd])

    def by_kind(stage, c):
        for odd in range(2):
            @pl.when(lax.rem(c, 2) == odd)
            def _(odd=odd):
                stage(c, odd)

    def send(start, count, here, stage, c, target):
        blocks = g_buf.at[pl.ds(start, count), here]
        to_mp(blocks, blocks, g_send.at[c], g_recv.at[c, stage], target).start()

    def arrived(count, here, stage, c):
        wait_for(g_buf.at[pl.ds(0, count), here], g_recv.at[c, stage])

    def to_neighbours(block, c):
        for target in (beside, ahead, behind):
            send(block, 1, chunk(c), NEAR, c, target)

    def stage_exchange(c, carry):
        theirs = (1 - half) * half_rows + c * chunk_rows
        to_mp(
            tok.at[pl.ds(pl.multiple_of(theirs, chunk_rows), chunk_rows)],
            g_buf.at[base + half, chunk(c)], g_send.at[c], e_recv.at[c], partner,
        ).start()
        to_neighbours(base + half, c)
        return carry

    def stage_partner(c):
        wait_for(g_buf.at[0, chunk(c)], e_recv.at[c])
        to_neighbours(base + 1 - half, c)

    def stage_near(c, odd):
        arrived(6, chunk(c), NEAR, c)
        send(x_back * RING + pair_at * 2, 1, chunk(c), FAR, c, ahead)
        send(x_next * RING + pair_at * 2 + 1, 1, chunk(c), FAR, c, behind)
        beside_pair = x_at * RING + 2 - pair_at * 2
        send(beside_pair, 2, rows_y(c, odd), Y_BESIDE, c, ahead)
        send(beside_pair, 2, rows_y(c, odd), Y_BESIDE, c, behind)
        send(x_back * RING + pair_at * 2, 2, rows_x(c, odd), X_BESIDE, c, beside)
        send(x_next * RING + pair_at * 2, 2, rows_x(c, odd), X_BESIDE, c, beside)

    def stage_far(c, odd):
        arrived(2, chunk(c), FAR, c)
        send(x_far * RING + pair_at * 2, 2, rows_x(c, odd), X_BESIDE, c, beside)
        arrived(4, rows_y(c, odd), Y_BESIDE, c)
        send(x_back * RING + 2 - pair_at * 2, 1, rows_y(c, odd), Y_FAR, c, ahead)
        send(x_next * RING + 3 - pair_at * 2, 1, rows_y(c, odd), Y_FAR, c, behind)

    def stage_last(c, odd):
        arrived(6, rows_x(c, odd), X_BESIDE, c)
        arrived(2, rows_y(c, odd), Y_FAR, c)

    core = lax.rem(d, 2)

    def piece(steps):
        return lax.rem(d + n_dp + 2 * steps, n_dp)

    quarter = n_dp // 4

    def pass_on(steps, part, target, sem):
        ref = w2.at[piece(steps), part]
        to_dp(ref, ref, w2_send, sem, target).start()

    def weights_start():
        lanes = pl.ds(pl.multiple_of(d * LANES, LANES), LANES)
        for part, ref in enumerate((wg, wu)):
            to_mp(ref.at[:, lanes], w2.at[d, part], w2_send, w2_first.at[part], partner).start()

    def weights_step(k, part):
        up, down = piece(1), piece(-1)
        if k == 0:
            wait_for(w2.at[0, 0], w2_first.at[part])
            pass_on(0, part, up, w2_up.at[0, part])
            pass_on(0, part, down, w2_down.at[0, part])
            pass_on(0, part, sibling, w2_side)
            return
        wait_for(w2.at[0, 0], w2_up.at[k - 1, part])
        wait_for(w2.at[0, 0], w2_down.at[k - 1, part])
        if k < quarter - 1 or part == 0:
            pass_on(-k, part, up, w2_up.at[k, part])
        if k < quarter - 1 or part == 1:
            pass_on(k, part, down, w2_down.at[k, part])
        pass_on(-k, part, sibling, w2_side)
        pass_on(k, part, sibling, w2_side)

    def weights_end(part):
        wait_for(w2.at[0, 0], (w2_up, w2_down)[part].at[quarter - 1, part])
        pass_on(quarter, part, sibling, w2_side)

    pool_of = lax.broadcasted_iota(jnp.int32, (pool_items, span), 1) // ITEM_TOK
    pool_row = lax.broadcasted_iota(jnp.int32, (pool_items, span), 0)
    pool = (pool_of == pool_row).astype(F32).astype(BF16)

    def ffn(k, gate_w, up_w, result):
        here = pl.ds(pl.multiple_of(k * span, span), span)
        wide = jnp.concatenate(
            [g_buf[j // RING * RING + SPOT[j % RING], here, :] for j in range(n_mp)], axis=1
        )
        gate = lax.dot_general(gate_w, wide, NT, preferred_element_type=F32)
        up = lax.dot_general(up_w, wide, NT, preferred_element_type=F32)
        hidden = (gate / (1.0 + jnp.exp(-gate)) * up).astype(BF16)
        there = pl.ds(pl.multiple_of(k * pool_items, pool_items), pool_items)
        result[there, :] = lax.dot_general(pool, hidden, NT, preferred_element_type=F32)

    def ffn_own(k):
        ffn(k, wg_v[...], wu_v[...], pooled)

    def ffn_partner(k):
        gate_w = jnp.concatenate([w2[j, 0] for j in range(n_mp)], axis=1)
        up_w = jnp.concatenate([w2[j, 1] for j in range(n_mp)], axis=1)
        ffn(k, gate_w, up_w, pooled2)

    def stage_down(h, source, order):
        here = pl.ds(pl.multiple_of(h * half_items, half_items), half_items)
        part = jnp.dot(source, wd_v[...], preferred_element_type=F32).astype(BF16)
        for j in range(n_mp):
            s1[j, here, :] = part[:, j * LANES : (j + 1) * LANES]
        r1[m, here, :] = s1[m, here, :]
        for j in mp_peers:
            to_mp(s1.at[j, here], r1.at[m, here], mp_send.at[0], r1_recv.at[order], j).start()

    def step(i, carry):
        @pl.when(i < CHUNKS - AHEAD)
        def _():
            stage_partner(i + AHEAD)

        @pl.when(i < CHUNKS)
        def _():
            by_kind(stage_near, i)

        @pl.when((i >= LAG) & (i < CHUNKS + LAG))
        def _():
            by_kind(stage_far, i - LAG)

        for k in range(quarter + 1):
            for part in range(2):
                @pl.when(i == RING_STEPS[2 * k + part])
                def _(k=k, part=part):
                    weights_step(k, part) if k < quarter else weights_end(part)

        @pl.when(i >= 2 * LAG)
        def _():
            by_kind(stage_last, i - 2 * LAG)

        @pl.when(i == 2)
        def _():
            for copy in copies[1:-2]:
                copy.wait()
            token_sum = jnp.dot(token_pool, tok_v[...], preferred_element_type=F32)
            tok_mean[...] = token_sum * (1.0 / ITEM_TOK)

        behind_by = CHUNKS + 2 * LAG - 1 - i

        @pl.when(behind_by == SPANS - 1)
        def _():
            wait_for(w2.at[pl.ds(0, n_dp // 2)], w2_side)

        @pl.when(behind_by < SPANS)
        def _():
            ffn_partner(SPANS - 1 - behind_by)

        @pl.when(behind_by == 0)
        def _():
            pooled_out[...] = (pooled2[...] * (1.0 / ITEM_TOK)).astype(BF16)
            to_mp(pooled_out, pooled_in, p_sem.at[0], p_sem.at[1], partner).start()

        @pl.when((i >= 2 * LAG) & (lax.rem(behind_by, CHUNKS // SPANS) == 0))
        def _():
            ffn_own(SPANS - 1 - behind_by // (CHUNKS // SPANS))

        return carry

    for j in mp_peers:
        to_mp(gains.at[m], gains.at[m], gs_sem.at[0], gs_sem.at[1], j).start()
    for j in dp_peers:
        to_dp(slots.at[d], slots.at[d], gs_sem.at[2], gs_sem.at[3], j).start()

    copies[0].wait()
    lax.fori_loop(0, CHUNKS // 2, stage_exchange, 0)
    weights_start()
    lax.fori_loop(CHUNKS // 2, CHUNKS, stage_exchange, 0)
    for c in range(AHEAD):
        stage_partner(c)
    lax.fori_loop(0, CHUNKS + 2 * LAG, step, 0)
    stage_down(half, (pooled[...] * (1.0 / ITEM_TOK)).astype(BF16), 0)
    wait_for(pooled_in, p_sem.at[1])
    stage_down(1 - half, pooled_in[...], 1)

    for i, (ref, count) in enumerate(((gains, n_mp), (gains, n_mp), (slots, n_dp), (slots, n_dp))):
        wait_for(ref.at[pl.ds(0, count - 1)], gs_sem.at[i])

    slot_row = jnp.concatenate([slots[k][:, :item_dev] for k in range(n_dp)], axis=1)
    last = (slot_row >= 0) & (jnp.bitwise_and(slot_row, positions - 1) == positions - 1)
    long_base = jnp.max(
        jnp.where(last, slot_row, positions - 1), axis=1, keepdims=True
    ) - (positions - 1)
    is_long = long_base == d * positions
    row = lax.broadcasted_iota(jnp.int32, (LANES, 1), 0)
    position = jnp.where(row < short, row, row - short + d * long_rows)
    row_slot = jnp.where(row < short, d * positions, long_base) + position
    row_slot = jnp.where(row < mine, row_slot, -2)
    holds = jnp.where(slot_row == row_slot[:mine], 1.0, 0.0).astype(BF16)
    long_row = lax.broadcasted_iota(jnp.int32, (positions, 1), 0)
    holds_long[...] = jnp.where(slot_row == long_base + long_row, 1.0, 0.0).astype(BF16)
    next_slot = jnp.where((position + 1 < positions) & (row < mine), row_slot + 1, -2)
    follows = jnp.where(slot_row == next_slot, 1.0, 0.0).astype(BF16)
    valid = jnp.sum(holds.astype(F32), axis=1, keepdims=True)
    has_target = lax.dot_general(
        jnp.ones((8, n_items), BF16), follows, NT, preferred_element_type=F32
    )
    item_id = lax.broadcasted_iota(jnp.int32, (n_items, chunk_items), 0)
    chunk_id = lax.broadcasted_iota(jnp.int32, (n_items, chunk_items), 1) + m * chunk_items
    to_chunk = jnp.where(item_id == chunk_id, 1.0, 0.0).astype(BF16)
    picks = jnp.dot(follows[:mine], to_chunk, preferred_element_type=F32)

    for h in range(2):
        wait_for(r1.at[pl.ds(0, n_mp - 1), pl.ds(0, half_items)], r1_recv.at[h])
    total = tok_mean[...]
    for j in range(n_mp):
        total = total + r1[j].astype(F32)
    embedding = total.astype(BF16)
    emb_out[...] = embedding

    def dp_block(k):
        return pl.ds(pl.multiple_of(k * item_dev, item_dev), item_dev)

    def share(ref, sem, arrivals):
        here = dp_block(d)
        for j in z_peers + [sibling]:
            to_dp(ref.at[here], ref.at[here], sem, arrivals.at[d], j).start()

    def pass_across(ref, sem, arrivals):
        for k in sorted(range(1, n_dp // 2), key=lambda k: min(k, n_dp // 2 - k)):
            j = lax.rem(d + n_dp - 2 * k, n_dp)
            wait_for(ref.at[dp_block(j)], arrivals.at[j])
            to_dp(ref.at[dp_block(j)], ref.at[dp_block(j)], sem, arrivals.at[j], sibling).start()
        for k in range(n_dp // 2):
            j = lax.rem(sibling + n_dp - 2 * k, n_dp)
            wait_for(ref.at[dp_block(j)], arrivals.at[j])

    x_buf[m] = embedding
    for j in mp_peers:
        to_mp(x_buf.at[m], x_buf.at[m], mp_send.at[1], mp_recv.at[1], j).start()
    items[dp_block(d), :] = embedding
    share(items, dp_send.at[0], item_recv)
    wait_for(x_buf.at[pl.ds(0, n_mp - 1)], mp_recv.at[1])

    states = [x_buf[j].astype(F32) for j in range(n_mp)]
    squares = states[0] * states[0]
    for block in states[1:]:
        squares = squares + block * block
    features = n_mp * LANES
    inverse = lax.rsqrt(jnp.sum(squares, axis=1, keepdims=True) / features + 1e-05)
    normed = jnp.concatenate(
        [(states[j] * inverse * gains[j]).astype(BF16) for j in range(n_mp)], axis=1
    )
    query = jnp.dot(normed, wq_v[...], preferred_element_type=F32) * HEAD_DIM ** (-0.5)
    key = jnp.dot(normed, wk_v[...], preferred_element_type=F32)
    value = jnp.dot(normed, wv_v[...], preferred_element_type=F32)
    item_lane = lax.broadcasted_iota(jnp.int32, (item_dev, LANES), 1)
    first_kv = (item_lane * 0 + lax.rem(m // 4, 2)) == 0
    key_part = jnp.where(first_kv, key, pltpu.roll(key, HEAD_DIM, axis=1))
    value_part = jnp.where(first_kv, pltpu.roll(value, HEAD_DIM, axis=1), value)
    pair = jnp.where(item_lane < HEAD_DIM, key_part, value_part)
    qkv[dp_block(d), :] = jnp.concatenate([query, pair], axis=1).astype(BF16)
    share(qkv, dp_send.at[1], qkv_recv)
    pass_across(items, dp_send.at[0], item_recv)

    placed = jnp.dot(holds, items[...], preferred_element_type=F32)

    def item_block(k):
        return pl.ds(pl.multiple_of(k * chunk_items, chunk_items), chunk_items)

    it_buf[m] = items[item_block(m), :]
    for j in mp_peers:
        to_mp(items.at[item_block(j)], it_buf.at[m], it_sem.at[0], it_sem.at[1], j).start()
    pass_across(qkv, dp_send.at[1], qkv_recv)

    own_rows = jnp.dot(holds, qkv[...], preferred_element_type=F32)
    long_pairs = jnp.dot(holds_long[...], qkv[:, LANES:], preferred_element_type=F32)
    long_here = pl.ds(pl.multiple_of(d * long_rows, long_rows), long_rows)
    cosine = jnp.concatenate([cos_t[0:short, :], cos_t[long_here, :]], axis=0)
    sine = jnp.concatenate([sin_t[0:short, :], sin_t[long_here, :]], axis=0)
    lane = lax.broadcasted_iota(jnp.int32, (mine, LANES), 1)
    left = lane < HEAD_DIM

    def rotate(v, cosine, sine):
        at = lax.rem(lax.broadcasted_iota(jnp.int32, v.shape, 1), HEAD_DIM)
        swapped = jnp.where(
            at < HEAD_DIM // 2,
            pltpu.roll(v, LANES - HEAD_DIM // 2, axis=1),
            pltpu.roll(v, HEAD_DIM // 2, axis=1),
        )
        return v * cosine + swapped * sine

    def rotate_key(v, rows):
        is_key = lax.broadcasted_iota(jnp.int32, v.shape, 1) < HEAD_DIM
        cosine = jnp.where(is_key, cos_t[:rows, :], 1.0)
        sine = jnp.where(is_key, sin_t[:rows, :], 0.0)
        return rotate(v, cosine, sine).astype(BF16)

    query = rotate(own_rows[:, :LANES], cosine, sine)
    short_pairs = rotate_key(own_rows[:short, LANES:], short)
    long_pairs = rotate_key(long_pairs, positions)

    head0 = jnp.where(left, query, 0.0).astype(BF16)
    head1 = jnp.where(left, pltpu.roll(query, HEAD_DIM, axis=1), 0.0).astype(BF16)

    def attend(q_rows, keys, first_position):
        count, n_keys = q_rows.shape[0], keys.shape[0]
        scores = lax.dot_general(q_rows, keys, NT, preferred_element_type=F32)
        at = lax.rem(lax.broadcasted_iota(jnp.int32, (count, n_keys), 0), count // 2)
        of = lax.broadcasted_iota(jnp.int32, (count, n_keys), 1)
        weights = jnp.where(of <= at + first_position, jnp.exp(scores), 0.0)
        weights = (weights / jnp.sum(weights, axis=1, keepdims=True)).astype(BF16)
        mixed = jnp.dot(weights, keys, preferred_element_type=F32)
        top, bottom = mixed[: count // 2], mixed[count // 2 :]
        at_left = lax.broadcasted_iota(jnp.int32, top.shape, 1) < HEAD_DIM
        return jnp.where(at_left, pltpu.roll(top, HEAD_DIM, axis=1), bottom).astype(BF16)

    short_rows = attend(
        jnp.concatenate([head0[:short], head1[:short]], axis=0), short_pairs, 0
    )
    rest = attend(
        jnp.concatenate([head0[short:], head1[short:]], axis=0), long_pairs, d * long_rows
    )
    attended = jnp.concatenate([short_rows, rest], axis=0)
    attn = jnp.dot(attended, wo_v[...], preferred_element_type=F32).astype(BF16)
    for j in range(n_mp):
        s5[j] = attn[:, j * LANES : (j + 1) * LANES]
    r5[m] = s5[m]
    for j in mp_peers:
        to_mp(s5.at[j], r5.at[m], mp_send.at[2], mp_recv.at[2], j).start()

    wait_for(it_buf.at[pl.ds(0, n_mp - 1)], it_sem.at[1])
    wide_items = [it_buf[j].astype(F32) for j in range(n_mp)]
    item_squares = wide_items[0] * wide_items[0]
    for block in wide_items[1:]:
        item_squares = item_squares + block * block
    item_scale = lax.rsqrt(jnp.sum(item_squares, axis=1, keepdims=True) + 1e-06)
    for j in range(n_mp):
        iu[:, j * LANES : (j + 1) * LANES] = (wide_items[j] * item_scale).astype(BF16)

    wait_for(r5.at[pl.ds(0, n_mp - 1)], mp_recv.at[2])
    combined = placed
    for j in range(n_mp):
        combined = combined + r5[j].astype(F32)
    combined = jnp.where(valid > 0.5, combined, 0.0).astype(BF16)
    u_buf[m] = combined
    for j in mp_peers:
        to_mp(u_buf.at[m], u_buf.at[m], mp_send.at[3], mp_recv.at[3], j).start()
    us_long[long_here, :] = combined[short:]
    for j in dp_peers:
        to_dp(
            us_long.at[long_here], us_long.at[long_here], dp_send.at[2], dp_recv.at[2], j
        ).start()

    wait_for(u_buf.at[pl.ds(0, n_mp - 1)], mp_recv.at[3])
    users = [u_buf[j] for j in range(n_mp)]
    user_squares = users[0].astype(F32) * users[0].astype(F32)
    for block in users[1:]:
        user_squares = user_squares + block.astype(F32) * block.astype(F32)
    user_scale = lax.rsqrt(jnp.sum(user_squares, axis=1, keepdims=True) + 1e-06)
    logits = lax.dot_general(
        jnp.concatenate(users, axis=1), iu[...], NT, preferred_element_type=F32
    ) * (SCALE * user_scale)
    stack = jnp.concatenate(
        [jnp.exp(logits), logits * picks, jnp.zeros((LANES - 2 * mine, chunk_items), F32)], axis=0
    )
    sums = lax.dot_general(
        jnp.ones((8, chunk_items), F32), stack, NT,
        precision=lax.Precision.HIGHEST, preferred_element_type=F32,
    )
    tp[m] = sums[0:1]
    for j in mp_peers:
        to_mp(tp.at[m], tp.at[m], mp_send.at[4], mp_recv.at[4], j).start()

    wait_for(us_long.at[pl.ds(0, (n_dp - 1) * long_rows)], dp_recv.at[2])
    short_states = jnp.concatenate(
        [combined[:short].astype(F32), jnp.zeros((positions - short, LANES), F32)], axis=0
    )
    us_out[...] = jnp.where(is_long, us_long[...].astype(F32), short_states).astype(BF16)

    wait_for(tp.at[pl.ds(0, n_mp - 1)], mp_recv.at[4])
    sums = tp[0]
    for j in range(1, n_mp):
        sums = sums + tp[j]
    sums = jnp.broadcast_to(sums, (8, LANES))
    counted = has_target > 0.5
    picked = pltpu.roll(sums, LANES - mine, axis=1)
    loss = jnp.where(counted, jnp.log(jnp.where(counted, sums, 1.0)) - picked, 0.0)
    at_lane = lax.broadcasted_iota(jnp.int32, (LANES, positions), 0)
    at_position = lax.broadcasted_iota(jnp.int32, (LANES, positions), 1)
    chosen = (at_lane >= short) & (at_lane < mine)
    chosen = chosen & (at_position == at_lane - short + d * long_rows)
    spread = jnp.dot(
        loss, jnp.where(chosen, 1.0, 0.0),
        precision=lax.Precision.HIGHEST, preferred_element_type=F32,
    )
    ll[d] = spread[0:1]
    for j in dp_peers:
        to_dp(ll.at[d], ll.at[d], dp_send.at[3], dp_recv.at[3], j).start()
    same = (at_lane < short) & (at_position == at_lane)
    short_loss = jnp.dot(
        loss, jnp.where(same, 1.0, 0.0),
        precision=lax.Precision.HIGHEST, preferred_element_type=F32,
    )[0:1]
    wait_for(ll.at[pl.ds(0, n_dp - 1)], dp_recv.at[3])
    long_loss = ll[0]
    for j in range(1, n_dp):
        long_loss = long_loss + ll[j]
    loss_out[...] = jnp.where(is_long, long_loss, short_loss)

    for c in range(CHUNKS):
        wait_for(g_buf.at[pl.ds(0, n_mp - 1), pl.ds(0, chunk_rows)], g_send.at[c])
    wait_for(w2, w2_send)
    wait_for(pooled_out, p_sem.at[0])
    wait_for(s1.at[pl.ds(0, n_mp - 1)], mp_send.at[0])
    wait_for(x_buf.at[pl.ds(0, n_mp - 1)], mp_send.at[1])
    wait_for(s5.at[pl.ds(0, n_mp - 1)], mp_send.at[2])
    wait_for(u_buf.at[pl.ds(0, n_mp - 1)], mp_send.at[3])
    wait_for(tp.at[pl.ds(0, n_mp - 1)], mp_send.at[4])
    wait_for(it_buf.at[pl.ds(0, n_mp - 1)], it_sem.at[0])
    wait_for(items.at[pl.ds(0, (n_dp - 1) * item_dev)], dp_send.at[0])
    wait_for(qkv.at[pl.ds(0, (n_dp - 1) * item_dev)], dp_send.at[1])
    wait_for(us_long.at[pl.ds(0, (n_dp - 1) * long_rows)], dp_send.at[2])
    wait_for(ll.at[pl.ds(0, n_dp - 1)], dp_send.at[3])


def solution(mesh, short=SHORT):
    n_dp, n_mp = mesh.shape["dp"], mesh.shape["mp"]

    def local(tok, wg, wu, wd, gain, wq, wk, wv, wo, item_slot, lengths, targets):
        rows, features = tok.shape[0], wg.shape[0]
        ff, item_dev, positions = wg.shape[1], item_slot.shape[0], targets.shape[0]
        n_items = n_dp * item_dev
        mine = short + positions // n_dp
        cos_table, sin_table = rope_tables(positions)
        hbm = pl.BlockSpec(memory_space=pltpu.HBM)
        vmem = pl.BlockSpec(memory_space=pltpu.VMEM)
        dma = pltpu.SemaphoreType.DMA
        sizes = (n_dp, n_mp, rows, ff, item_dev, short, positions)
        embeddings, states, losses = pl.pallas_call(
            functools.partial(kernel, sizes),
            out_shape=(
                pltpu.VMEM((item_dev, LANES), BF16),
                pltpu.VMEM((positions, LANES), BF16),
                pltpu.VMEM((1, positions), F32),
            ),
            in_specs=[hbm] * 12,
            out_specs=(vmem, vmem, vmem),
            scratch_shapes=[
                pltpu.VMEM((n_mp, rows // 2, LANES), BF16),
                pltpu.VMEM((rows, LANES), BF16),
                pltpu.VMEM((n_dp, 2, ff, LANES), BF16),
                pltpu.VMEM((ff, features), BF16),
                pltpu.VMEM((ff, features), BF16),
                pltpu.VMEM((ff, features), BF16),
                pltpu.VMEM((features, LANES), BF16),
                pltpu.VMEM((features, LANES), BF16),
                pltpu.VMEM((features, LANES), BF16),
                pltpu.VMEM((LANES, features), BF16),
                pltpu.VMEM((item_dev // 2, ff), F32),
                pltpu.VMEM((item_dev // 2, ff), F32),
                pltpu.VMEM((item_dev // 2, ff), BF16),
                pltpu.VMEM((item_dev // 2, ff), BF16),
                pltpu.VMEM((item_dev, LANES), F32),
                pltpu.VMEM((n_mp, item_dev, LANES), BF16),
                pltpu.VMEM((n_mp, item_dev, LANES), BF16),
                pltpu.VMEM((n_items, LANES), BF16),
                pltpu.VMEM((n_mp, item_dev, LANES), BF16),
                pltpu.VMEM((n_mp, n_items // n_mp, LANES), BF16),
                pltpu.VMEM((n_items // n_mp, features), BF16),
                pltpu.VMEM((n_items, 2 * LANES), BF16),
                pltpu.VMEM((positions, n_items), BF16),
                pltpu.VMEM((n_mp, mine, LANES), BF16),
                pltpu.VMEM((n_mp, mine, LANES), BF16),
                pltpu.VMEM((positions, LANES), BF16),
                pltpu.VMEM((n_mp, mine, LANES), BF16),
                pltpu.VMEM((n_mp, 1, LANES), F32),
                pltpu.VMEM((n_dp, 1, LANES), jnp.int32),
                pltpu.VMEM((n_mp, 1, LANES), F32),
                pltpu.VMEM((n_dp, 1, positions), F32),
                pltpu.VMEM((1, LANES), F32),
                pltpu.VMEM((1, item_dev), jnp.int32),
                pltpu.VMEM((positions, LANES), F32),
                pltpu.VMEM((positions, LANES), F32),
                dma((13,)),
                dma((CHUNKS,)),
                dma((CHUNKS,)),
                dma((CHUNKS, 5)),
                dma,
                dma((2,)),
                dma((n_dp // 4, 2)),
                dma((n_dp // 4, 2)),
                dma,
                dma((2,)),
                dma((5,)),
                dma((5,)),
                dma((2,)),
                dma((2,)),
                dma((4,)),
                dma((4,)),
                dma((n_dp,)),
                dma((n_dp,)),
                dma((4,)),
            ],
            compiler_params=pltpu.CompilerParams(
                collective_id=0, has_side_effects=True, vmem_limit_bytes=48 * 1024 * 1024
            ),
        )(
            *[
                pltpu.with_memory_space_constraint(a, pltpu.HBM)
                for a in (
                    tok, wg.T, wu.T, wd, wq, wk, wv, wo,
                    gain.reshape(1, LANES), item_slot.reshape(1, item_dev),
                    jnp.asarray(cos_table), jnp.asarray(sin_table),
                )
            ]
        )
        return embeddings, states, losses.reshape(positions)

    return jax.shard_map(
        local,
        mesh=mesh,
        in_specs=(
            P("dp", "mp"), P(None, "mp"), P(None, "mp"), P("mp", None), P("mp"),
            P(None, "mp"), P(), P(), P("mp", None), P("dp"), P("dp"), P("dp"),
        ),
        out_specs=(P("dp", "mp"), P("dp", "mp"), P("dp")),
        check_vma=False,
    )
```

```python
import functools

import jax
import jax.numpy as jnp
import numpy as np
from jax import lax
from jax.experimental import pallas as pl
from jax.experimental.pallas import tpu as pltpu
from jax.sharding import PartitionSpec as P

HEAD_DIM = 64
ITEM_TOK = 32
SCALE = 20.0
SHORT = 32
LANES = 128
RING = 4
SPOT = (0, 2, 3, 1)
CHUNKS = 8
LAG = 2
AHEAD = 2
SPANS = 4
W2_NEAR, W2_FAR, W2_END = (1, 2, 2, 3), (3, 3, 4, 5), (5, 5, 6, 6)
MESH = pl.DeviceIdType.MESH
BF16 = jnp.bfloat16
F32 = jnp.float32
NT = (((1,), (1,)), ((), ()))


def rope_tables(positions):
    half = HEAD_DIM // 2
    exponent = np.arange(half, dtype=np.float32) * np.float32(2.0 / HEAD_DIM)
    frequency = (10000.0 ** (-exponent.astype(np.float64))).astype(np.float32)
    angles = np.arange(positions, dtype=np.float32)[:, None] * frequency[None, :]
    angles = angles.astype(np.float64)
    cosine, sine = np.cos(angles), np.sin(angles)
    cos_table = np.concatenate([cosine, cosine, cosine, cosine], axis=1)
    sin_table = np.concatenate([-sine, sine, -sine, sine], axis=1)
    return cos_table.astype(np.float32), sin_table.astype(np.float32)


def kernel(
    sizes,
    tok, wg, wu, wd, wq, wk, wv, wo, gain, slot, cos_hbm, sin_hbm,
    emb_out, us_out, loss_out,
    g_buf, tok_v, w2, wg_v, wu_v, wd_v, wq_v, wk_v, wv_v, wo_v,
    pooled, pooled2, pooled_out, pooled_in, tok_mean, s1, r1, items, x_buf, it_buf, iu, qkv, holds_long, s5, r5, us_long, u_buf,
    gains, slots, tp, ll, gain_v, slot_v, cos_t, sin_t,
    w_sem, e_recv, g_send, g_recv, w2_send, w2_first, w2_up, w2_down, w2_far, w2_side, p_sem,
    mp_send, mp_recv, r1_recv, it_sem, dp_send, dp_recv, item_recv, qkv_recv, gs_sem,
):
    n_dp, n_mp, rows, ff, item_dev, short, positions = sizes
    n_items = n_dp * item_dev
    long_rows = positions // n_dp
    mine = short + long_rows
    chunk_items = n_items // n_mp
    half_rows = rows // 2
    chunk_rows = half_rows // CHUNKS
    x_rows = (chunk_rows // 2, chunk_rows // 2 - 16)
    span = half_rows // SPANS
    pool_items = span // ITEM_TOK
    half_items = item_dev // 2
    d = lax.axis_index("dp")
    m = lax.axis_index("mp")
    sibling = d + 1 - 2 * lax.rem(d, 2)

    def to_mp(src, dst, send_sem, recv_sem, j):
        return pltpu.make_async_remote_copy(
            src_ref=src, dst_ref=dst, send_sem=send_sem, recv_sem=recv_sem,
            device_id={"mp": j}, device_id_type=MESH,
        )

    def to_dp(src, dst, send_sem, recv_sem, j):
        return pltpu.make_async_remote_copy(
            src_ref=src, dst_ref=dst, send_sem=send_sem, recv_sem=recv_sem,
            device_id={"dp": j}, device_id_type=MESH,
        )

    def hops(a, size):
        return min(a, size - a)

    apart = [(a, b) for a in range(RING) for b in range(RING) if a or b]
    apart.sort(key=lambda ab: -hops(ab[0], RING) - hops(ab[1], RING))
    mp_peers = [
        lax.rem(m // RING + a, RING) * RING + lax.rem(lax.rem(m, RING) + b, RING) for a, b in apart
    ]
    levels = n_dp // 2
    z_apart = sorted(range(1, levels), key=lambda k: -hops(k, levels))
    z_peers = [lax.rem(d + 2 * k, n_dp) for k in z_apart]
    dp_peers = z_peers + [j + 1 - 2 * lax.rem(j, 2) for j in z_peers] + [sibling]

    def wait_for(ref, sem):
        pltpu.make_async_copy(ref, ref, sem).wait()

    barrier = pltpu.get_barrier_semaphore()
    for j in mp_peers:
        pl.semaphore_signal(barrier, inc=1, device_id={"mp": j}, device_id_type=MESH)
    for j in dp_peers:
        pl.semaphore_signal(barrier, inc=1, device_id={"dp": j}, device_id_type=MESH)

    kv_block = pl.ds(pl.multiple_of((m // 8) * LANES, LANES), LANES)
    at_half = pl.ds(pl.multiple_of((lax.rem(m, RING) // 2) * half_rows, half_rows), half_rows)
    at_spot = m // RING * RING + lax.rem((lax.rem(m, RING) + 1) // 2, 2) * 2 + lax.rem(m, RING) // 2
    loads = [
        (tok.at[at_half], g_buf.at[at_spot]), (tok, tok_v), (wg, wg_v), (wu, wu_v), (wd, wd_v),
        (wq, wq_v), (wk.at[:, kv_block], wk_v), (wv.at[:, kv_block], wv_v), (wo, wo_v),
        (cos_hbm, cos_t), (sin_hbm, sin_t), (gain, gain_v), (slot, slot_v),
    ]
    copies = [pltpu.make_async_copy(a, b, w_sem.at[i]) for i, (a, b) in enumerate(loads)]
    for copy in copies:
        copy.start()
    token_of = lax.broadcasted_iota(jnp.int32, (item_dev, rows), 1) // ITEM_TOK
    token_row = lax.broadcasted_iota(jnp.int32, (item_dev, rows), 0)
    token_pool = (token_of == token_row).astype(F32).astype(BF16)
    pl.semaphore_wait(barrier, n_mp + n_dp - 2)
    copies[-2].wait()
    copies[-1].wait()
    gains[m] = gain_v[...]
    slots[d] = jnp.concatenate(
        [slot_v[...], jnp.full((1, LANES - item_dev), -1, jnp.int32)], axis=1
    )

    x_at, y_at = m // RING, lax.rem(m, RING)
    half = y_at // 2
    pair_at = lax.rem((y_at + 1) // 2, 2)
    base = x_at * RING + pair_at * 2
    partner = x_at * RING + 3 - y_at
    beside = x_at * RING + y_at + 1 - 2 * lax.rem(y_at, 2)
    x_next = lax.rem(x_at + 1, RING)
    x_back = lax.rem(x_at + RING - 1, RING)
    x_far = lax.rem(x_at + 2, RING)
    ahead, behind = x_next * RING + y_at, x_back * RING + y_at
    NEAR, FAR, X_BESIDE, Y_BESIDE, Y_FAR = range(5)

    def chunk(c):
        return pl.ds(pl.multiple_of(c * chunk_rows, chunk_rows), chunk_rows)

    def rows_x(c, odd):
        return pl.ds(pl.multiple_of(c * chunk_rows, 16), x_rows[odd])

    def rows_y(c, odd):
        return pl.ds(pl.multiple_of(c * chunk_rows + x_rows[odd], 16), chunk_rows - x_rows[odd])

    def by_kind(stage, c):
        for odd in range(2):
            @pl.when(lax.rem(c, 2) == odd)
            def _(odd=odd):
                stage(c, odd)

    def send(start, count, here, stage, c, target):
        blocks = g_buf.at[pl.ds(start, count), here]
        to_mp(blocks, blocks, g_send.at[c], g_recv.at[c, stage], target).start()

    def arrived(count, here, stage, c):
        wait_for(g_buf.at[pl.ds(0, count), here], g_recv.at[c, stage])

    def to_neighbours(block, c):
        for target in (beside, ahead, behind):
            send(block, 1, chunk(c), NEAR, c, target)

    def stage_exchange(c, carry):
        theirs = (1 - half) * half_rows + c * chunk_rows
        to_mp(
            tok.at[pl.ds(pl.multiple_of(theirs, chunk_rows), chunk_rows)],
            g_buf.at[base + half, chunk(c)], g_send.at[c], e_recv.at[c], partner,
        ).start()
        to_neighbours(base + half, c)
        return carry

    def stage_partner(c):
        wait_for(g_buf.at[0, chunk(c)], e_recv.at[c])
        to_neighbours(base + 1 - half, c)

    def stage_near(c, odd):
        arrived(6, chunk(c), NEAR, c)
        send(x_back * RING + pair_at * 2, 1, chunk(c), FAR, c, ahead)
        send(x_next * RING + pair_at * 2 + 1, 1, chunk(c), FAR, c, behind)
        beside_pair = x_at * RING + 2 - pair_at * 2
        send(beside_pair, 2, rows_y(c, odd), Y_BESIDE, c, ahead)
        send(beside_pair, 2, rows_y(c, odd), Y_BESIDE, c, behind)
        send(x_back * RING + pair_at * 2, 2, rows_x(c, odd), X_BESIDE, c, beside)
        send(x_next * RING + pair_at * 2, 2, rows_x(c, odd), X_BESIDE, c, beside)

    def stage_far(c, odd):
        arrived(2, chunk(c), FAR, c)
        send(x_far * RING + pair_at * 2, 2, rows_x(c, odd), X_BESIDE, c, beside)
        arrived(4, rows_y(c, odd), Y_BESIDE, c)
        send(x_back * RING + 2 - pair_at * 2, 1, rows_y(c, odd), Y_FAR, c, ahead)
        send(x_next * RING + 3 - pair_at * 2, 1, rows_y(c, odd), Y_FAR, c, behind)

    def stage_last(c, odd):
        arrived(6, rows_x(c, odd), X_BESIDE, c)
        arrived(2, rows_y(c, odd), Y_FAR, c)

    up, down = lax.rem(d + 2, n_dp), lax.rem(d + n_dp - 2, n_dp)

    def block_of(steps, s):
        return lax.rem(d + n_dp + 2 * steps, n_dp // 2) * 2 + s // 2

    def pass_on(steps, s, target, sem):
        ref = w2.at[block_of(steps, s), s % 2]
        to_dp(ref, ref, w2_send, sem, target).start()

    def weights_start(s):
        k = block_of(0, s)
        lanes = pl.ds(pl.multiple_of(k * LANES, LANES), LANES)
        ref = (wg, wu)[s % 2]
        to_mp(ref.at[:, lanes], w2.at[k, s % 2], w2_send, w2_first.at[s], partner).start()

    def weights_near(s):
        wait_for(w2.at[0, 0], w2_first.at[s])
        pass_on(0, s, up, w2_up.at[s])
        pass_on(0, s, down, w2_down.at[s])
        pass_on(0, s, sibling, w2_side)

    def weights_far(s):
        wait_for(w2.at[0, 0], w2_up.at[s])
        wait_for(w2.at[0, 0], w2_down.at[s])
        if s < 2:
            pass_on(-1, s, up, w2_far.at[s])
        else:
            pass_on(1, s, down, w2_far.at[s])
        pass_on(-1, s, sibling, w2_side)
        pass_on(1, s, sibling, w2_side)

    def weights_end(s):
        wait_for(w2.at[0, 0], w2_far.at[s])
        pass_on(2, s, sibling, w2_side)

    pool_of = lax.broadcasted_iota(jnp.int32, (pool_items, span), 1) // ITEM_TOK
    pool_row = lax.broadcasted_iota(jnp.int32, (pool_items, span), 0)
    pool = (pool_of == pool_row).astype(F32).astype(BF16)

    def ffn(k, gate_w, up_w, result):
        here = pl.ds(pl.multiple_of(k * span, span), span)
        wide = jnp.concatenate(
            [g_buf[j // RING * RING + SPOT[j % RING], here, :] for j in range(n_mp)], axis=1
        )
        gate = lax.dot_general(gate_w, wide, NT, preferred_element_type=F32)
        up = lax.dot_general(up_w, wide, NT, preferred_element_type=F32)
        hidden = (gate / (1.0 + jnp.exp(-gate)) * up).astype(BF16)
        there = pl.ds(pl.multiple_of(k * pool_items, pool_items), pool_items)
        result[there, :] = lax.dot_general(pool, hidden, NT, preferred_element_type=F32)

    def ffn_own(k):
        ffn(k, wg_v[...], wu_v[...], pooled)

    def ffn_partner(k):
        gate_w = jnp.concatenate([w2[j, 0] for j in range(n_mp)], axis=1)
        up_w = jnp.concatenate([w2[j, 1] for j in range(n_mp)], axis=1)
        ffn(k, gate_w, up_w, pooled2)

    def stage_down(h, source, order):
        here = pl.ds(pl.multiple_of(h * half_items, half_items), half_items)
        part = jnp.dot(source, wd_v[...], preferred_element_type=F32).astype(BF16)
        for j in range(n_mp):
            s1[j, here, :] = part[:, j * LANES : (j + 1) * LANES]
        r1[m, here, :] = s1[m, here, :]
        for j in mp_peers:
            to_mp(s1.at[j, here], r1.at[m, here], mp_send.at[0], r1_recv.at[order], j).start()

    def step(i, carry):
        @pl.when(i < CHUNKS - AHEAD)
        def _():
            stage_partner(i + AHEAD)

        @pl.when(i < CHUNKS)
        def _():
            by_kind(stage_near, i)

        @pl.when((i >= LAG) & (i < CHUNKS + LAG))
        def _():
            by_kind(stage_far, i - LAG)

        for move, steps in ((weights_near, W2_NEAR), (weights_far, W2_FAR), (weights_end, W2_END)):
            for part, at in enumerate(steps):
                @pl.when(i == at)
                def _(move=move, part=part):
                    move(part)

        @pl.when(i >= 2 * LAG)
        def _():
            by_kind(stage_last, i - 2 * LAG)

        @pl.when(i == 2)
        def _():
            for copy in copies[1:-2]:
                copy.wait()
            token_sum = jnp.dot(token_pool, tok_v[...], preferred_element_type=F32)
            tok_mean[...] = token_sum * (1.0 / ITEM_TOK)

        behind_by = CHUNKS + 2 * LAG - 1 - i

        @pl.when(behind_by == SPANS)
        def _():
            wait_for(w2.at[pl.ds(0, n_dp // 2)], w2_side)

        @pl.when((behind_by <= SPANS) & (behind_by != 2))
        def _():
            ffn_partner(SPANS - behind_by - jnp.where(behind_by < 2, 1, 0))

        @pl.when(behind_by == 0)
        def _():
            pooled_out[...] = (pooled2[...] * (1.0 / ITEM_TOK)).astype(BF16)
            to_mp(pooled_out, pooled_in, p_sem.at[0], p_sem.at[1], partner).start()

        @pl.when((i >= 2 * LAG) & (lax.rem(behind_by, CHUNKS // SPANS) == 0))
        def _():
            ffn_own(SPANS - 1 - behind_by // (CHUNKS // SPANS))

        return carry

    for j in mp_peers:
        to_mp(gains.at[m], gains.at[m], gs_sem.at[0], gs_sem.at[1], j).start()
    for j in dp_peers:
        to_dp(slots.at[d], slots.at[d], gs_sem.at[2], gs_sem.at[3], j).start()

    copies[0].wait()
    lax.fori_loop(0, CHUNKS // 2, stage_exchange, 0)
    for part in range(4):
        weights_start(part)
        stage_exchange(CHUNKS // 2 + part, 0)
    for c in range(AHEAD):
        stage_partner(c)
    lax.fori_loop(0, CHUNKS + 2 * LAG, step, 0)
    stage_down(half, (pooled[...] * (1.0 / ITEM_TOK)).astype(BF16), 0)
    wait_for(pooled_in, p_sem.at[1])
    stage_down(1 - half, pooled_in[...], 1)

    for i, (ref, count) in enumerate(((gains, n_mp), (gains, n_mp), (slots, n_dp), (slots, n_dp))):
        wait_for(ref.at[pl.ds(0, count - 1)], gs_sem.at[i])

    slot_row = jnp.concatenate([slots[k][:, :item_dev] for k in range(n_dp)], axis=1)
    last = (slot_row >= 0) & (jnp.bitwise_and(slot_row, positions - 1) == positions - 1)
    long_base = jnp.max(
        jnp.where(last, slot_row, positions - 1), axis=1, keepdims=True
    ) - (positions - 1)
    is_long = long_base == d * positions
    row = lax.broadcasted_iota(jnp.int32, (LANES, 1), 0)
    position = jnp.where(row < short, row, row - short + d * long_rows)
    row_slot = jnp.where(row < short, d * positions, long_base) + position
    row_slot = jnp.where(row < mine, row_slot, -2)
    holds = jnp.where(slot_row == row_slot[:mine], 1.0, 0.0).astype(BF16)
    long_row = lax.broadcasted_iota(jnp.int32, (positions, 1), 0)
    holds_long[...] = jnp.where(slot_row == long_base + long_row, 1.0, 0.0).astype(BF16)
    next_slot = jnp.where((position + 1 < positions) & (row < mine), row_slot + 1, -2)
    follows = jnp.where(slot_row == next_slot, 1.0, 0.0).astype(BF16)
    valid = jnp.sum(holds.astype(F32), axis=1, keepdims=True)
    has_target = lax.dot_general(
        jnp.ones((8, n_items), BF16), follows, NT, preferred_element_type=F32
    )
    item_id = lax.broadcasted_iota(jnp.int32, (n_items, chunk_items), 0)
    chunk_id = lax.broadcasted_iota(jnp.int32, (n_items, chunk_items), 1) + m * chunk_items
    to_chunk = jnp.where(item_id == chunk_id, 1.0, 0.0).astype(BF16)
    picks = jnp.dot(follows[:mine], to_chunk, preferred_element_type=F32)

    for h in range(2):
        wait_for(r1.at[pl.ds(0, n_mp - 1), pl.ds(0, half_items)], r1_recv.at[h])
    total = tok_mean[...]
    for j in range(n_mp):
        total = total + r1[j].astype(F32)
    embedding = total.astype(BF16)
    emb_out[...] = embedding

    def dp_block(k):
        return pl.ds(pl.multiple_of(k * item_dev, item_dev), item_dev)

    def share(ref, sem, arrivals):
        here = dp_block(d)
        for j in z_peers + [sibling]:
            to_dp(ref.at[here], ref.at[here], sem, arrivals.at[d], j).start()

    def pass_across(ref, sem, arrivals):
        for k in sorted(range(1, n_dp // 2), key=lambda k: min(k, n_dp // 2 - k)):
            j = lax.rem(d + n_dp - 2 * k, n_dp)
            wait_for(ref.at[dp_block(j)], arrivals.at[j])
            to_dp(ref.at[dp_block(j)], ref.at[dp_block(j)], sem, arrivals.at[j], sibling).start()
        for k in range(n_dp // 2):
            j = lax.rem(sibling + n_dp - 2 * k, n_dp)
            wait_for(ref.at[dp_block(j)], arrivals.at[j])

    x_buf[m] = embedding
    for j in mp_peers:
        to_mp(x_buf.at[m], x_buf.at[m], mp_send.at[1], mp_recv.at[1], j).start()
    items[dp_block(d), :] = embedding
    share(items, dp_send.at[0], item_recv)
    wait_for(x_buf.at[pl.ds(0, n_mp - 1)], mp_recv.at[1])

    states = [x_buf[j].astype(F32) for j in range(n_mp)]
    squares = states[0] * states[0]
    for block in states[1:]:
        squares = squares + block * block
    features = n_mp * LANES
    inverse = lax.rsqrt(jnp.sum(squares, axis=1, keepdims=True) / features + 1e-05)
    normed = jnp.concatenate(
        [(states[j] * inverse * gains[j]).astype(BF16) for j in range(n_mp)], axis=1
    )
    query = jnp.dot(normed, wq_v[...], preferred_element_type=F32) * HEAD_DIM ** (-0.5)
    key = jnp.dot(normed, wk_v[...], preferred_element_type=F32)
    value = jnp.dot(normed, wv_v[...], preferred_element_type=F32)
    item_lane = lax.broadcasted_iota(jnp.int32, (item_dev, LANES), 1)
    first_kv = (item_lane * 0 + lax.rem(m // 4, 2)) == 0
    key_part = jnp.where(first_kv, key, pltpu.roll(key, HEAD_DIM, axis=1))
    value_part = jnp.where(first_kv, pltpu.roll(value, HEAD_DIM, axis=1), value)
    pair = jnp.where(item_lane < HEAD_DIM, key_part, value_part)
    qkv[dp_block(d), :] = jnp.concatenate([query, pair], axis=1).astype(BF16)
    share(qkv, dp_send.at[1], qkv_recv)
    pass_across(items, dp_send.at[0], item_recv)

    placed = jnp.dot(holds, items[...], preferred_element_type=F32)

    def item_block(k):
        return pl.ds(pl.multiple_of(k * chunk_items, chunk_items), chunk_items)

    it_buf[m] = items[item_block(m), :]
    for j in mp_peers:
        to_mp(items.at[item_block(j)], it_buf.at[m], it_sem.at[0], it_sem.at[1], j).start()
    pass_across(qkv, dp_send.at[1], qkv_recv)

    own_rows = jnp.dot(holds, qkv[...], preferred_element_type=F32)
    long_pairs = jnp.dot(holds_long[...], qkv[:, LANES:], preferred_element_type=F32)
    long_here = pl.ds(pl.multiple_of(d * long_rows, long_rows), long_rows)
    cosine = jnp.concatenate([cos_t[0:short, :], cos_t[long_here, :]], axis=0)
    sine = jnp.concatenate([sin_t[0:short, :], sin_t[long_here, :]], axis=0)
    lane = lax.broadcasted_iota(jnp.int32, (mine, LANES), 1)
    left = lane < HEAD_DIM

    def rotate(v, cosine, sine):
        at = lax.rem(lax.broadcasted_iota(jnp.int32, v.shape, 1), HEAD_DIM)
        swapped = jnp.where(
            at < HEAD_DIM // 2,
            pltpu.roll(v, LANES - HEAD_DIM // 2, axis=1),
            pltpu.roll(v, HEAD_DIM // 2, axis=1),
        )
        return v * cosine + swapped * sine

    def rotate_key(v, rows):
        is_key = lax.broadcasted_iota(jnp.int32, v.shape, 1) < HEAD_DIM
        cosine = jnp.where(is_key, cos_t[:rows, :], 1.0)
        sine = jnp.where(is_key, sin_t[:rows, :], 0.0)
        return rotate(v, cosine, sine).astype(BF16)

    query = rotate(own_rows[:, :LANES], cosine, sine)
    short_pairs = rotate_key(own_rows[:short, LANES:], short)
    long_pairs = rotate_key(long_pairs, positions)

    head0 = jnp.where(left, query, 0.0).astype(BF16)
    head1 = jnp.where(left, pltpu.roll(query, HEAD_DIM, axis=1), 0.0).astype(BF16)

    def attend(q_rows, keys, first_position):
        count, n_keys = q_rows.shape[0], keys.shape[0]
        scores = lax.dot_general(q_rows, keys, NT, preferred_element_type=F32)
        at = lax.rem(lax.broadcasted_iota(jnp.int32, (count, n_keys), 0), count // 2)
        of = lax.broadcasted_iota(jnp.int32, (count, n_keys), 1)
        weights = jnp.where(of <= at + first_position, jnp.exp(scores), 0.0)
        weights = (weights / jnp.sum(weights, axis=1, keepdims=True)).astype(BF16)
        mixed = jnp.dot(weights, keys, preferred_element_type=F32)
        top, bottom = mixed[: count // 2], mixed[count // 2 :]
        at_left = lax.broadcasted_iota(jnp.int32, top.shape, 1) < HEAD_DIM
        return jnp.where(at_left, pltpu.roll(top, HEAD_DIM, axis=1), bottom).astype(BF16)

    short_rows = attend(
        jnp.concatenate([head0[:short], head1[:short]], axis=0), short_pairs, 0
    )
    rest = attend(
        jnp.concatenate([head0[short:], head1[short:]], axis=0), long_pairs, d * long_rows
    )
    attended = jnp.concatenate([short_rows, rest], axis=0)
    attn = jnp.dot(attended, wo_v[...], preferred_element_type=F32).astype(BF16)
    for j in range(n_mp):
        s5[j] = attn[:, j * LANES : (j + 1) * LANES]
    r5[m] = s5[m]
    for j in mp_peers:
        to_mp(s5.at[j], r5.at[m], mp_send.at[2], mp_recv.at[2], j).start()

    wait_for(it_buf.at[pl.ds(0, n_mp - 1)], it_sem.at[1])
    wide_items = [it_buf[j].astype(F32) for j in range(n_mp)]
    item_squares = wide_items[0] * wide_items[0]
    for block in wide_items[1:]:
        item_squares = item_squares + block * block
    item_scale = lax.rsqrt(jnp.sum(item_squares, axis=1, keepdims=True) + 1e-06)
    for j in range(n_mp):
        iu[:, j * LANES : (j + 1) * LANES] = (wide_items[j] * item_scale).astype(BF16)

    wait_for(r5.at[pl.ds(0, n_mp - 1)], mp_recv.at[2])
    combined = placed
    for j in range(n_mp):
        combined = combined + r5[j].astype(F32)
    combined = jnp.where(valid > 0.5, combined, 0.0).astype(BF16)
    u_buf[m] = combined
    for j in mp_peers:
        to_mp(u_buf.at[m], u_buf.at[m], mp_send.at[3], mp_recv.at[3], j).start()
    us_long[long_here, :] = combined[short:]
    for j in dp_peers:
        to_dp(
            us_long.at[long_here], us_long.at[long_here], dp_send.at[2], dp_recv.at[2], j
        ).start()

    wait_for(u_buf.at[pl.ds(0, n_mp - 1)], mp_recv.at[3])
    users = [u_buf[j] for j in range(n_mp)]
    user_squares = users[0].astype(F32) * users[0].astype(F32)
    for block in users[1:]:
        user_squares = user_squares + block.astype(F32) * block.astype(F32)
    user_scale = lax.rsqrt(jnp.sum(user_squares, axis=1, keepdims=True) + 1e-06)
    logits = lax.dot_general(
        jnp.concatenate(users, axis=1), iu[...], NT, preferred_element_type=F32
    ) * (SCALE * user_scale)
    stack = jnp.concatenate(
        [jnp.exp(logits), logits * picks, jnp.zeros((LANES - 2 * mine, chunk_items), F32)], axis=0
    )
    sums = lax.dot_general(
        jnp.ones((8, chunk_items), F32), stack, NT,
        precision=lax.Precision.HIGHEST, preferred_element_type=F32,
    )
    tp[m] = sums[0:1]
    for j in mp_peers:
        to_mp(tp.at[m], tp.at[m], mp_send.at[4], mp_recv.at[4], j).start()

    wait_for(us_long.at[pl.ds(0, (n_dp - 1) * long_rows)], dp_recv.at[2])
    short_states = jnp.concatenate(
        [combined[:short].astype(F32), jnp.zeros((positions - short, LANES), F32)], axis=0
    )
    us_out[...] = jnp.where(is_long, us_long[...].astype(F32), short_states).astype(BF16)

    wait_for(tp.at[pl.ds(0, n_mp - 1)], mp_recv.at[4])
    sums = tp[0]
    for j in range(1, n_mp):
        sums = sums + tp[j]
    sums = jnp.broadcast_to(sums, (8, LANES))
    counted = has_target > 0.5
    picked = pltpu.roll(sums, LANES - mine, axis=1)
    loss = jnp.where(counted, jnp.log(jnp.where(counted, sums, 1.0)) - picked, 0.0)
    at_lane = lax.broadcasted_iota(jnp.int32, (LANES, positions), 0)
    at_position = lax.broadcasted_iota(jnp.int32, (LANES, positions), 1)
    chosen = (at_lane >= short) & (at_lane < mine)
    chosen = chosen & (at_position == at_lane - short + d * long_rows)
    spread = jnp.dot(
        loss, jnp.where(chosen, 1.0, 0.0),
        precision=lax.Precision.HIGHEST, preferred_element_type=F32,
    )
    ll[d] = spread[0:1]
    for j in dp_peers:
        to_dp(ll.at[d], ll.at[d], dp_send.at[3], dp_recv.at[3], j).start()
    same = (at_lane < short) & (at_position == at_lane)
    short_loss = jnp.dot(
        loss, jnp.where(same, 1.0, 0.0),
        precision=lax.Precision.HIGHEST, preferred_element_type=F32,
    )[0:1]
    wait_for(ll.at[pl.ds(0, n_dp - 1)], dp_recv.at[3])
    long_loss = ll[0]
    for j in range(1, n_dp):
        long_loss = long_loss + ll[j]
    loss_out[...] = jnp.where(is_long, long_loss, short_loss)

    for c in range(CHUNKS):
        wait_for(g_buf.at[pl.ds(0, n_mp - 1), pl.ds(0, chunk_rows)], g_send.at[c])
    wait_for(w2, w2_send)
    wait_for(pooled_out, p_sem.at[0])
    wait_for(s1.at[pl.ds(0, n_mp - 1)], mp_send.at[0])
    wait_for(x_buf.at[pl.ds(0, n_mp - 1)], mp_send.at[1])
    wait_for(s5.at[pl.ds(0, n_mp - 1)], mp_send.at[2])
    wait_for(u_buf.at[pl.ds(0, n_mp - 1)], mp_send.at[3])
    wait_for(tp.at[pl.ds(0, n_mp - 1)], mp_send.at[4])
    wait_for(it_buf.at[pl.ds(0, n_mp - 1)], it_sem.at[0])
    wait_for(items.at[pl.ds(0, (n_dp - 1) * item_dev)], dp_send.at[0])
    wait_for(qkv.at[pl.ds(0, (n_dp - 1) * item_dev)], dp_send.at[1])
    wait_for(us_long.at[pl.ds(0, (n_dp - 1) * long_rows)], dp_send.at[2])
    wait_for(ll.at[pl.ds(0, n_dp - 1)], dp_send.at[3])


def solution(mesh, short=SHORT):
    n_dp, n_mp = mesh.shape["dp"], mesh.shape["mp"]

    def local(tok, wg, wu, wd, gain, wq, wk, wv, wo, item_slot, lengths, targets):
        rows, features = tok.shape[0], wg.shape[0]
        ff, item_dev, positions = wg.shape[1], item_slot.shape[0], targets.shape[0]
        n_items = n_dp * item_dev
        mine = short + positions // n_dp
        cos_table, sin_table = rope_tables(positions)
        hbm = pl.BlockSpec(memory_space=pltpu.HBM)
        vmem = pl.BlockSpec(memory_space=pltpu.VMEM)
        dma = pltpu.SemaphoreType.DMA
        sizes = (n_dp, n_mp, rows, ff, item_dev, short, positions)
        embeddings, states, losses = pl.pallas_call(
            functools.partial(kernel, sizes),
            out_shape=(
                pltpu.VMEM((item_dev, LANES), BF16),
                pltpu.VMEM((positions, LANES), BF16),
                pltpu.VMEM((1, positions), F32),
            ),
            in_specs=[hbm] * 12,
            out_specs=(vmem, vmem, vmem),
            scratch_shapes=[
                pltpu.VMEM((n_mp, rows // 2, LANES), BF16),
                pltpu.VMEM((rows, LANES), BF16),
                pltpu.VMEM((n_dp, 2, ff, LANES), BF16),
                pltpu.VMEM((ff, features), BF16),
                pltpu.VMEM((ff, features), BF16),
                pltpu.VMEM((ff, features), BF16),
                pltpu.VMEM((features, LANES), BF16),
                pltpu.VMEM((features, LANES), BF16),
                pltpu.VMEM((features, LANES), BF16),
                pltpu.VMEM((LANES, features), BF16),
                pltpu.VMEM((item_dev // 2, ff), F32),
                pltpu.VMEM((item_dev // 2, ff), F32),
                pltpu.VMEM((item_dev // 2, ff), BF16),
                pltpu.VMEM((item_dev // 2, ff), BF16),
                pltpu.VMEM((item_dev, LANES), F32),
                pltpu.VMEM((n_mp, item_dev, LANES), BF16),
                pltpu.VMEM((n_mp, item_dev, LANES), BF16),
                pltpu.VMEM((n_items, LANES), BF16),
                pltpu.VMEM((n_mp, item_dev, LANES), BF16),
                pltpu.VMEM((n_mp, n_items // n_mp, LANES), BF16),
                pltpu.VMEM((n_items // n_mp, features), BF16),
                pltpu.VMEM((n_items, 2 * LANES), BF16),
                pltpu.VMEM((positions, n_items), BF16),
                pltpu.VMEM((n_mp, mine, LANES), BF16),
                pltpu.VMEM((n_mp, mine, LANES), BF16),
                pltpu.VMEM((positions, LANES), BF16),
                pltpu.VMEM((n_mp, mine, LANES), BF16),
                pltpu.VMEM((n_mp, 1, LANES), F32),
                pltpu.VMEM((n_dp, 1, LANES), jnp.int32),
                pltpu.VMEM((n_mp, 1, LANES), F32),
                pltpu.VMEM((n_dp, 1, positions), F32),
                pltpu.VMEM((1, LANES), F32),
                pltpu.VMEM((1, item_dev), jnp.int32),
                pltpu.VMEM((positions, LANES), F32),
                pltpu.VMEM((positions, LANES), F32),
                dma((13,)),
                dma((CHUNKS,)),
                dma((CHUNKS,)),
                dma((CHUNKS, 5)),
                dma,
                dma((4,)),
                dma((4,)),
                dma((4,)),
                dma((4,)),
                dma,
                dma((2,)),
                dma((5,)),
                dma((5,)),
                dma((2,)),
                dma((2,)),
                dma((4,)),
                dma((4,)),
                dma((n_dp,)),
                dma((n_dp,)),
                dma((4,)),
            ],
            compiler_params=pltpu.CompilerParams(
                collective_id=0, has_side_effects=True, vmem_limit_bytes=48 * 1024 * 1024
            ),
        )(
            *[
                pltpu.with_memory_space_constraint(a, pltpu.HBM)
                for a in (
                    tok, wg.T, wu.T, wd, wq, wk, wv, wo,
                    gain.reshape(1, LANES), item_slot.reshape(1, item_dev),
                    jnp.asarray(cos_table), jnp.asarray(sin_table),
                )
            ]
        )
        return embeddings, states, losses.reshape(positions)

    return jax.shard_map(
        local,
        mesh=mesh,
        in_specs=(
            P("dp", "mp"), P(None, "mp"), P(None, "mp"), P("mp", None), P("mp"),
            P(None, "mp"), P(), P(), P("mp", None), P("dp"), P("dp"), P("dp"),
        ),
        out_specs=(P("dp", "mp"), P("dp", "mp"), P("dp")),
        check_vma=False,
    )
```
